32 devices in a mesh: img: 8 (over z, x), row: 4 (over y, core).
Axes of the slice: x: 2, y: 2, z: 4, core: 2. Of those that a mesh axis runs over, the one named last changes fastest.
Arguments:
- features: bfloat16 [32, 32, 32, 2048], P('img', 'row'), may hold values from -6 to 6
- w_reduce: bfloat16 [2048, 512], P(('img', 'row')), may hold values from -0.125 to 0.125
- w_dilated: bfloat16 [9, 512, 512], P(None, ('img', 'row')), may hold values from -0.09375 to 0.09375
- w_expand: bfloat16 [512, 2048], P(('img', 'row')), may hold values from -0.25 to 0.25
- gain_reduce: float32 [512], replicated, may hold values from 0.1 to 1.9
- bias_reduce: float32 [512], replicated, may hold values from -3 to 3
- gain_dilated: float32 [512], replicated, may hold values from 0.1 to 1.9
- bias_dilated: float32 [512], replicated, may hold values from -3 to 3
- gain_expand: float32 [2048], replicated, may hold values from 0.1 to 1.9
- bias_expand: float32 [2048], replicated, may hold values from -3 to 3
- w_heads: bfloat16 [9, 2048, 1024], P(None, ('img', 'row')), may hold values from -0.046875 to 0.046875
- gain_heads: float32 [1024], replicated, may hold values from 0.1 to 1.9
- bias_heads: float32 [1024], replicated, may hold values from -3 to 3
- w_message: bfloat16 [2, 9, 512, 512], P(None, None, ('img', 'row')), may hold values from -0.09375 to 0.09375
- w_gate: bfloat16 [2, 9, 512, 512], P(None, None, ('img', 'row')), may hold values from -0.09375 to 0.09375
- w_seg: bfloat16 [512, 40], P(('img', 'row')), may hold values from -0.59765625 to 0.59765625
- w_depth: bfloat16 [512], P(('img', 'row')), may hold values from -0.29882812 to 0.29882812
- labels: int32 [32, 32, 32], P('img', 'row'), may hold values from 0 to 39
- depth_target: float32 [32, 32, 32], P('img', 'row'), may hold values from -6 to 6
- depth_mask: int32 [32, 32, 32], P('img', 'row'), may hold values from 0 to 1, as said below
Outputs:
- depth_pred: float32 [32, 32, 32], P('img', 'row')
- seg_logits: float32 [32, 32, 32, 40], P('img', 'row')
- features_grad: float32 [32, 32, 32, 2048], P('img', 'row')
- w_reduce_grad: float32 [2048, 512], P(('img', 'row'))
- w_dilated_grad: float32 [9, 512, 512], P(None, ('img', 'row'))
- w_expand_grad: float32 [512, 2048], P(('img', 'row'))
- gain_reduce_grad: float32 [512], replicated
- bias_reduce_grad: float32 [512], replicated
- gain_dilated_grad: float32 [512], replicated
- bias_dilated_grad: float32 [512], replicated
- gain_expand_grad: float32 [2048], replicated
- bias_expand_grad: float32 [2048], replicated
- w_heads_grad: float32 [9, 2048, 1024], P(None, ('img', 'row'))
- gain_heads_grad: float32 [1024], replicated
- bias_heads_grad: float32 [1024], replicated
- w_message_grad: float32 [2, 9, 512, 512], P(None, None, ('img', 'row'))
- w_gate_grad: float32 [2, 9, 512, 512], P(None, None, ('img', 'row'))
- w_seg_grad: float32 [512, 40], P(('img', 'row'))
- w_depth_grad: float32 [512], P(('img', 'row'))
The draws below stay inside these ranges and needn't reach their ends.
Inputs may be any that keep to these rules, and one draw needn't show every extreme that they name: `depth_mask`: each crop has its own share of pixels without valid depth, from none to most of them, differing widely between crops; every crop keeps some valid pixels.
All inputs are finite; a program needn't handle non-finite values.
Results may differ from the reference program's by a relative error of at most 0.018.
Values may be sent and summed in bfloat16 or wider, within the bound.
A program may use at most 384 MiB of HBM per device.

```python
import jax
import jax.numpy as jnp
from jax import lax

D = 2048
M = 512
CLS = 40
H = 32
W = 32
IMAGES = 32


def draw_depth_mask(key, part):
    key = jax.random.fold_in(key, 7)
    image_key, pixel_key = jax.random.split(key)
    levels = jax.random.randint(image_key, (IMAGES, 1, 1), 0, 240)
    threshold = levels * levels // 256
    pixels = jax.random.randint(pixel_key, (IMAGES, H, W), 0, 256)
    return (pixels >= threshold).astype(jnp.int32)


def set_ends(result, own_key, low, top_value):
    spot = [jax.random.randint(jax.random.fold_in(own_key, axis), (), 0, length) for axis, length in enumerate(result.shape)]
    main_axis = result.shape.index(max(result.shape))
    neighbour = spot[:main_axis] + [(spot[main_axis] + 1) % result.shape[main_axis]] + spot[main_axis + 1:]
    return result.at[tuple(spot)].set(low).at[tuple(neighbour)].set(top_value)


def level_of(own_key, extent, cuts, smallest, high):
    loudness, own = 1.0, jax.random.fold_in(own_key, 6)
    for dim, parts in cuts:
        steps = jnp.exp(jax.random.uniform(jax.random.fold_in(own, dim), (parts,), jnp.float32, smallest / len(cuts), high / len(cuts)))
        loudness = loudness * jnp.repeat(steps, extent[dim] // parts).reshape([-1 if axis == dim else 1 for axis in range(len(extent))])
    return loudness


def noise(rng, shape, scale, reach, cuts=(), held_as=jnp.bfloat16):
    level = level_of(rng, shape, cuts, -0.22, 0.18) if cuts else 1.0
    entries = jax.random.normal(rng, shape, jnp.float32) * scale * level
    return jnp.minimum(jnp.maximum(entries, -reach), reach).astype(held_as)


def setup_inputs(seed: int = 0) -> dict:
    keys = jax.random.split(jax.random.key(seed), 21)
    return {
        "features": noise(keys[0], (IMAGES, H, W, D), 1.0, 6.0, ((0, 8), (1, 4))),
        "w_reduce": noise(keys[1], (D, M), D ** -0.5, 0.125, ((0, 32),)),
        "w_dilated": noise(keys[2], (9, M, M), (9 * M) ** -0.5, 0.09375, ((1, 32),)),
        "w_expand": noise(keys[3], (M, D), M ** -0.5, 0.25, ((0, 32),)),
        "gain_reduce": jnp.clip(1.0 + 0.18 * jax.random.normal(keys[4], (M,), jnp.float32), 0.1, 1.9),
        "bias_reduce": noise(keys[5], (M,), 0.5, 3.0, (), jnp.float32),
        "gain_dilated": jnp.clip(1.0 + 0.18 * jax.random.normal(keys[6], (M,), jnp.float32), 0.1, 1.9),
        "bias_dilated": noise(keys[7], (M,), 0.5, 3.0, (), jnp.float32),
        "gain_expand": jnp.clip(1.0 + 0.18 * jax.random.normal(keys[8], (D,), jnp.float32), 0.1, 1.9),
        "bias_expand": noise(keys[9], (D,), 0.5, 3.0, (), jnp.float32),
        "w_heads": noise(keys[10], (9, D, 2 * M), (9 * D) ** -0.5, 0.046875, ((1, 32),)),
        "gain_heads": jnp.clip(1.0 + 0.18 * jax.random.normal(keys[11], (2 * M,), jnp.float32), 0.1, 1.9),
        "bias_heads": noise(keys[12], (2 * M,), 0.5, 3.0, (), jnp.float32),
        "w_message": noise(keys[13], (2, 9, M, M), (9 * M) ** -0.5, 0.09375, ((2, 32),)),
        "w_gate": noise(keys[14], (2, 9, M, M), (9 * M) ** -0.5, 0.09375, ((2, 32),)),
        "w_seg": noise(keys[15], (M, CLS), 0.1, 0.59765625, ((0, 32),)),
        "w_depth": noise(keys[16], (M,), 0.05, 0.29882812, ((0, 32),)),
        "labels": set_ends(jax.random.randint(keys[17], (IMAGES, H, W), 0, CLS), jax.random.fold_in(keys[17], 1), 0, CLS - 1).astype(jnp.int32),
        "depth_target": noise(keys[18], (IMAGES, H, W), 1.0, 6.0, ((0, 8), (1, 4)), jnp.float32),
        "depth_mask": draw_depth_mask(jax.random.fold_in(keys[20], 71), 0),
    }


@jax.custom_vjp
def low(v):
    return lax.optimization_barrier(v.astype(jnp.bfloat16)).astype(jnp.float32)

@jax.custom_vjp
def low_back(v):
    return v

def low_keep(v):
    return (low(v), None)

def low_pass(kept, grad):
    return (grad,)

def back_keep(v):
    return (v, None)

def back_low(kept, grad):
    return (low(grad),)
low.defvjp(low_keep, low_pass)
low_back.defvjp(back_keep, back_low)
EPS = 1e-05

def conv_full(values_in, weight, spread):
    height = values_in.shape[1]
    breadth = values_in.shape[2]
    padded = jnp.pad(values_in, ((0, 0), (spread, spread), (spread, spread), (0, 0)))
    running = jnp.zeros(values_in.shape[:3] + (weight.shape[2],), jnp.float32)
    for tap_index in range(9):
        tap_row = tap_index // 3
        tap_col = tap_index % 3
        shifted_piece = padded[:, tap_row * spread:tap_row * spread + height, tap_col * spread:tap_col * spread + breadth, :]
        running = running + jnp.einsum('bhwc,co->bhwo', shifted_piece, weight[tap_index], precision=lax.Precision.HIGHEST)
    return running

def batch_norm(values_in, gain, bias):
    center = lax.optimization_barrier(jnp.mean(values_in, axis=(0, 1, 2)))
    spread = lax.optimization_barrier(jnp.mean(jnp.square(values_in - center), axis=(0, 1, 2)))
    return (values_in - center) * lax.rsqrt(spread + EPS) * gain + bias

def network(params, labels, depth_target, depth_mask):
    features, w_reduce, w_dilated, w_expand, gain_reduce, bias_reduce, gain_dilated, bias_dilated, gain_expand, bias_expand, w_heads, gain_heads, bias_heads, w_message, w_gate, w_seg, w_depth = params
    highest = lax.Precision.HIGHEST
    first_raw = low_back(jnp.einsum('bhwc,co->bhwo', features, w_reduce, precision=highest))
    hidden_one = low(jax.nn.gelu(batch_norm(first_raw, gain_reduce, bias_reduce)))
    second_raw = low_back(conv_full(hidden_one, w_dilated, 2))
    hidden_two = low(jax.nn.gelu(batch_norm(second_raw, gain_dilated, bias_dilated)))
    third_raw = low_back(jnp.einsum('bhwc,co->bhwo', hidden_two, w_expand, precision=highest))
    output = low(jax.nn.gelu(batch_norm(third_raw, gain_expand, bias_expand) + features))
    heads_raw = low_back(conv_full(output, w_heads, 1))
    feature = low(jax.nn.gelu(batch_norm(heads_raw, gain_heads, bias_heads)))
    width_mid = w_message.shape[2]
    depth_feat = feature[..., :width_mid]
    seg_feat = feature[..., width_mid:]
    to_depth = low_back(conv_full(seg_feat, w_message[0], 1))
    to_seg = low_back(conv_full(depth_feat, w_message[1], 1))
    gate_depth = low_back(conv_full(depth_feat, w_gate[0], 1))
    gate_seg = low_back(conv_full(seg_feat, w_gate[1], 1))
    depth_stream = low(depth_feat + jax.nn.sigmoid(gate_depth) * to_depth)
    seg_stream = low(seg_feat + jax.nn.sigmoid(gate_seg) * to_seg)
    depth_pred = low_back(jnp.einsum('bhwc,c->bhw', depth_stream, w_depth, precision=highest))
    seg_logits = low_back(jnp.einsum('bhwc,ck->bhwk', seg_stream, w_seg, precision=highest))
    log_total = jax.nn.logsumexp(seg_logits, axis=-1)
    classes = jnp.arange(seg_logits.shape[-1], dtype=jnp.int32)
    picked = lax.optimization_barrier(jnp.sum(jnp.where(labels[..., None] == classes, seg_logits, 0.0), axis=-1))
    seg_loss = jnp.sum(log_total - picked)
    differ = depth_pred - depth_target
    depth_loss = jnp.sum(depth_mask.astype(jnp.float32) * (jnp.sqrt(differ * differ + 1.0) - 1.0))
    return (seg_loss + depth_loss, (depth_pred, seg_logits))

def reference(features, w_reduce, w_dilated, w_expand, gain_reduce, bias_reduce, gain_dilated, bias_dilated, gain_expand, bias_expand, w_heads, gain_heads, bias_heads, w_message, w_gate, w_seg, w_depth, labels, depth_target, depth_mask):
    params = tuple((element.astype(jnp.float32) for element in (features, w_reduce, w_dilated, w_expand, gain_reduce, bias_reduce, gain_dilated, bias_dilated, gain_expand, bias_expand, w_heads, gain_heads, bias_heads, w_message, w_gate, w_seg, w_depth)))
    target_wide = depth_target.astype(jnp.float32)

    def loss_of(*inputs):
        return network(inputs, labels, target_wide, depth_mask)
    loss_total, pullback, outputs = jax.vjp(loss_of, *params, has_aux=True)
    gradients = pullback(jnp.ones_like(loss_total))
    return (outputs[0], outputs[1], gradients[0], gradients[1], gradients[2], gradients[3], gradients[4], gradients[5], gradients[6], gradients[7], gradients[8], gradients[9], gradients[10], gradients[11], gradients[12], gradients[13], gradients[14], gradients[15], gradients[16])
```

```python
import functools

import jax
import jax.numpy as jnp
from jax import lax
from jax.experimental import pallas as pl
from jax.experimental.pallas import tpu as pltpu
from jax.sharding import Mesh
from jax.sharding import PartitionSpec as P

EPS = 1e-05
ALL = ("z", "x", "y", "c")
CHIPS = ("z", "x", "y")
ROWS = ("y", "c")
BF, F32 = jnp.bfloat16, jnp.float32
MESH = pl.DeviceIdType.MESH
VMEM_BYTES = 60 * 1024 * 1024


def at(axis, index):
    return {axis: index}


def small_sum_kernel(axes, sizes, kind, count, v_ref, o_ref, *scratch):
    slots, send_sem, recv_sem = scratch[: len(axes)], scratch[-2], scratch[-1]
    barrier = pltpu.get_barrier_semaphore()
    peers = 0
    for axis, n in zip(axes, sizes):
        me = lax.axis_index(axis)
        for s in range(1, n):
            pl.semaphore_signal(
                barrier, inc=1, device_id=at(axis, lax.rem(me + s, n)), device_id_type=MESH
            )
            peers += 1
    pl.semaphore_wait(barrier, peers)
    current = v_ref[...]
    which = 0
    for stage, (axis, n) in enumerate(zip(axes, sizes)):
        me = lax.axis_index(axis)
        slot = slots[stage]
        slot[me] = current
        copies = []
        for s in range(1, n):
            copy = pltpu.make_async_remote_copy(
                src_ref=slot.at[me],
                dst_ref=slot.at[me],
                send_sem=send_sem.at[which],
                recv_sem=recv_sem.at[which],
                device_id=at(axis, lax.rem(me + s, n)),
                device_id_type=MESH,
            )
            copy.start()
            copies.append(copy)
            which += 1
        for copy in copies:
            copy.wait()
        first, second = slot[0, 0], slot[0, 1]
        for s in range(1, n):
            first = first + slot[s, 0]
            second = second + slot[s, 1]
        if kind == "moments":
            mean = first / n
            for s in range(n):
                second = second + count * jnp.square(slot[s, 0] - mean)
            first = mean
            count = count * n
        current = jnp.stack([first, second])
    o_ref[...] = current


def small_sum(pair, axes, kind, count, collective):
    channels = pair[0].shape[0]
    sizes = tuple(lax.axis_size(a) for a in axes)
    shape = (2, channels // 128, 128)
    n_copies = sum(n - 1 for n in sizes)
    out = pl.pallas_call(
        functools.partial(small_sum_kernel, axes, sizes, kind, float(count)),
        out_shape=jax.ShapeDtypeStruct(shape, F32),
        in_specs=[pl.BlockSpec(memory_space=pltpu.VMEM)],
        out_specs=pl.BlockSpec(memory_space=pltpu.VMEM),
        scratch_shapes=[pltpu.VMEM((n,) + shape, F32) for n in sizes]
        + [pltpu.SemaphoreType.DMA((n_copies,)), pltpu.SemaphoreType.DMA((n_copies,))],
        compiler_params=pltpu.CompilerParams(collective_id=collective, has_side_effects=True),
    )(jnp.stack(pair).reshape(shape))
    return out[0].reshape(channels), out[1].reshape(channels)


def combine_cols(before, same, after, col):
    n = same.shape[0]
    before = jnp.where(col == 0, 0.0, pltpu.roll(before, 1, 0))
    after = jnp.where(col == n - 1, 0.0, pltpu.roll(after, n - 1, 0))
    return before + same + after


def conv_fwd(xpad, w, kc, nc):
    batch, height_pad, width, depth = xpad.shape
    height, wide = height_pad - 2, w.shape[2]
    px = batch * height * width
    steps = depth // kc

    def body(x_ref, w_ref, o_ref, s_ref, acc):
        k = pl.program_id(1)

        def dots(first):
            for b in range(3):
                for a in range(3):
                    xa = x_ref[:, a : a + height].reshape(px, kc)
                    d = jnp.dot(xa, w_ref[3 * a + b], preferred_element_type=F32)
                    if first and a == 0:
                        acc[b] = d
                    else:
                        acc[b] += d

        @pl.when(k == 0)
        def _():
            dots(True)

        @pl.when(k > 0)
        def _():
            dots(False)

        @pl.when(k == steps - 1)
        def _():
            col = lax.broadcasted_iota(jnp.int32, (width, nc), 0)

            def store(i, total):
                r = pl.ds(pl.multiple_of(i * width, width), width)
                v = combine_cols(acc[0, r], acc[1, r], acc[2, r], col)
                o_ref[r] = v
                return total + jnp.sum(v.reshape(width // 8, 8, nc), axis=0)

            total = lax.fori_loop(0, batch * height, store, jnp.zeros((8, nc), F32))
            mean = jnp.sum(total, axis=0, keepdims=True) / px

            def spread(i, total):
                r = pl.ds(pl.multiple_of(i * width, width), width)
                v = jnp.square(o_ref[r] - mean)
                return total + jnp.sum(v.reshape(width // 8, 8, nc), axis=0)

            m2 = lax.fori_loop(0, batch * height, spread, jnp.zeros((8, nc), F32))
            row = lax.broadcasted_iota(jnp.int32, (8, nc), 0)
            s_ref[...] = jnp.where(row == 0, mean, jnp.sum(m2, axis=0, keepdims=True))

    return pl.pallas_call(
        body,
        grid=(wide // nc, steps),
        in_specs=[
            pl.BlockSpec((batch, height_pad, width, kc), lambda n, k: (0, 0, 0, k)),
            pl.BlockSpec((9, kc, nc), lambda n, k: (0, k, n)),
        ],
        out_specs=[
            pl.BlockSpec((px, nc), lambda n, k: (0, n)),
            pl.BlockSpec((8, nc), lambda n, k: (0, n)),
        ],
        out_shape=[jax.ShapeDtypeStruct((px, wide), F32), jax.ShapeDtypeStruct((8, wide), F32)],
        scratch_shapes=[pltpu.VMEM((3, px, nc), F32)],
        compiler_params=pltpu.CompilerParams(vmem_limit_bytes=VMEM_BYTES),
        cost_estimate=pl.CostEstimate(
            flops=18 * px * depth * wide,
            bytes_accessed=18 * depth * wide + 2 * px * depth + 4 * px * wide,
            transcendentals=0,
        ),
    )(xpad, w)


def conv_dgrad(gpads, weights, cc, out_dtype):
    batch, height_pad, width, wide = gpads[0].shape
    many = len(gpads)
    height, depth = height_pad - 2, weights[0].shape[1]
    px = batch * height * width
    dims = (((1,), (1,)), ((), ()))

    def body(*refs):
        gs, ws, o_ref, acc = refs[:many], refs[many : 2 * many], refs[2 * many], refs[2 * many + 1]
        for q in range(many):
            for b in range(3):
                for a in range(3):
                    ga = gs[q][:, 2 - a : 2 - a + height].reshape(px, wide)
                    d = lax.dot_general(ga, ws[q][3 * a + b], dims, preferred_element_type=F32)
                    if q == 0 and a == 0:
                        acc[2 - b] = d
                    else:
                        acc[2 - b] += d
        col = lax.broadcasted_iota(jnp.int32, (width, cc), 0)

        def store(i, carry):
            r = pl.ds(pl.multiple_of(i * width, width), width)
            o_ref[r] = combine_cols(acc[0, r], acc[1, r], acc[2, r], col).astype(out_dtype)
            return carry

        lax.fori_loop(0, batch * height, store, 0)

    return pl.pallas_call(
        body,
        grid=(depth // cc,),
        in_specs=[pl.BlockSpec((batch, height_pad, width, wide), lambda c: (0, 0, 0, 0))] * many
        + [pl.BlockSpec((9, cc, wide), lambda c: (0, c, 0))] * many,
        out_specs=pl.BlockSpec((px, cc), lambda c: (0, c)),
        out_shape=jax.ShapeDtypeStruct((px, depth), out_dtype),
        scratch_shapes=[pltpu.VMEM((3, px, cc), F32)],
        compiler_params=pltpu.CompilerParams(vmem_limit_bytes=VMEM_BYTES),
        cost_estimate=pl.CostEstimate(
            flops=18 * many * px * depth * wide,
            bytes_accessed=18 * many * depth * wide + 4 * px * depth,
            transcendentals=0,
        ),
    )(*gpads, *weights)


def conv_wgrad(xpad, gt, cc, nc, piece):
    batch, height_pad, width, depth = xpad.shape
    height, wide = height_pad - 2, gt.shape[1]
    px = batch * height * width
    each = cc // piece

    def body(x_ref, g_ref, o_ref):
        for a in range(3):
            xa = x_ref[:, a : a + height].reshape(px, cc)
            for b in range(3):
                d = jnp.dot(g_ref[b], xa, preferred_element_type=F32).T.astype(BF)
                for j in range(each):
                    o_ref[j, 3 * a + b] = d[j * piece : (j + 1) * piece]

    return pl.pallas_call(
        body,
        grid=(wide // nc, depth // cc),
        in_specs=[
            pl.BlockSpec((batch, height_pad, width, cc), lambda n, c: (0, 0, 0, c)),
            pl.BlockSpec((3, nc, px), lambda n, c: (0, n, 0)),
        ],
        out_specs=pl.BlockSpec((each, 9, piece, nc), lambda n, c: (c, 0, 0, n)),
        out_shape=jax.ShapeDtypeStruct((depth // piece, 9, piece, wide), BF),
        compiler_params=pltpu.CompilerParams(vmem_limit_bytes=VMEM_BYTES),
        cost_estimate=pl.CostEstimate(
            flops=18 * px * depth * wide,
            bytes_accessed=18 * depth * wide + 2 * px * depth,
            transcendentals=0,
        ),
    )(xpad, gt)


def swap(value):
    return lax.ppermute(value, "c", [(0, 1), (1, 0)])


def in_order(mine, other, dim):
    first = lax.axis_index("c") == 0
    return jnp.concatenate(
        [jnp.where(first, mine, other), jnp.where(first, other, mine)], axis=dim
    )


def rims(block, axes, width):
    count = 1
    for a in axes:
        count *= lax.axis_size(a)
    forward = [(i, i + 1) for i in range(count - 1)]
    backward = [(t, s) for s, t in forward]
    low = lax.ppermute(block[:, block.shape[1] - width :], axes, forward)
    high = lax.ppermute(block[:, :width], axes, backward)
    return low, high


def with_rims(block, axes, width):
    low, high = rims(block, axes, width)
    return jnp.concatenate([low, block, high], axis=1)


def column_shifts(grad):
    width, wide = grad.shape[2], grad.shape[3]
    padded = jnp.pad(grad, ((0, 0), (0, 0), (1, 1), (0, 0)))
    return jnp.stack([padded[:, :, 2 - b : 2 - b + width].reshape(-1, wide).T for b in range(3)])


def taps_of(padded, spread, height):
    width = padded.shape[2]
    cols = jnp.pad(padded, ((0, 0), (0, 0), (spread, spread), (0, 0)))
    return [
        cols[:, a * spread : a * spread + height, b * spread : b * spread + width]
        for a in range(3)
        for b in range(3)
    ]


def local_moments(value):
    mean = jnp.mean(value, axis=(0, 1, 2))
    return mean, jnp.sum(jnp.square(value - mean), axis=(0, 1, 2))


def gelu_back(inner, upstream):
    return jax.vjp(jax.nn.gelu, inner)[1](upstream)[0]


def gather(value, axes, dim):
    return lax.all_gather(value, axes, axis=dim, tiled=True)


def scatter_sum(value, axes, dim):
    return lax.psum_scatter(value, axes, scatter_dimension=dim, tiled=True)


def per_device(
    features,
    w_reduce,
    w_dilated,
    w_expand,
    gain_reduce,
    bias_reduce,
    gain_dilated,
    bias_dilated,
    gain_expand,
    bias_expand,
    w_heads,
    gain_heads,
    bias_heads,
    w_message,
    w_gate,
    w_seg,
    w_depth,
    labels,
    depth_target,
    depth_mask,
):
    core = lax.axis_index("c")
    chips = lax.axis_size("z") * lax.axis_size("x") * lax.axis_size("y")
    devices = chips * 2
    crops, height, width, deep = features.shape
    mid = w_reduce.shape[1]
    classes = w_seg.shape[1]
    local_px = crops * height * width
    pixels = local_px * devices
    chip_px = local_px * 2

    r_rows, d_rows, e_rows = w_reduce.shape[0], w_dilated.shape[1], w_expand.shape[0]
    small = jnp.concatenate([w_seg, w_depth[:, None]], axis=1)
    small = jnp.pad(small, ((0, 0), (0, mid - classes - 1)))
    packed = jnp.concatenate(
        [
            w_reduce,
            w_dilated.reshape(9 * d_rows, mid),
            w_expand.reshape(e_rows * (deep // mid), mid),
            small,
        ]
    )
    packed = gather(packed[None], ALL, 0)
    cut = (r_rows, r_rows + 9 * d_rows, r_rows + 9 * d_rows + e_rows * (deep // mid))
    reduce_full = packed[:, : cut[0]].reshape(deep, mid)
    dilated_full = (
        packed[:, cut[0] : cut[1]].reshape(devices, 9, d_rows, mid).transpose(1, 0, 2, 3)
    ).reshape(9, mid, mid)
    expand_full = packed[:, cut[1] : cut[2]].reshape(mid, deep)
    class_full = packed[:, cut[2] :, :128].reshape(mid, 128)

    def half(value, which):
        return lax.dynamic_slice_in_dim(value, which * mid, mid, axis=value.ndim - 1)

    heads_full = gather(
        in_order(half(w_heads, core), swap(half(w_heads, 1 - core)), 1), CHIPS, 1
    )
    sides_own = jnp.stack([w_message[1 - core], w_gate[core]])
    sides_other = jnp.stack([w_message[core], w_gate[1 - core]])
    sides_full = gather(in_order(sides_own, swap(sides_other), 2), CHIPS, 2)

    first_raw = jnp.einsum("bhwc,co->bhwo", features, reduce_full, preferred_element_type=F32)

    def norm(raw_moments, axes, count, collective):
        mean, m2 = small_sum(raw_moments, axes, "moments", count, collective)
        return mean, lax.rsqrt(m2 / pixels + EPS)

    stats_one = norm(local_moments(first_raw), ALL, local_px, 0)
    scaled_one = (first_raw - stats_one[0]) * stats_one[1]
    inner_one = scaled_one * gain_reduce + bias_reduce
    hidden_one = jax.nn.gelu(inner_one).astype(BF)
    padded_one = with_rims(hidden_one, ROWS, 2)

    def dilated(padded, weights, back):
        total = None
        pieces = taps_of(padded, 2, height)
        for t in range(9):
            term = jnp.einsum(
                "bhwo,co->bhwc" if back else "bhwc,co->bhwo",
                pieces[8 - t if back else t],
                weights[t],
                preferred_element_type=F32,
            )
            total = term if total is None else total + term
        return total

    second_raw = dilated(padded_one, dilated_full, False)
    stats_two = norm(local_moments(second_raw), ALL, local_px, 1)
    scaled_two = (second_raw - stats_two[0]) * stats_two[1]
    inner_two = scaled_two * gain_dilated + bias_dilated
    hidden_two = jax.nn.gelu(inner_two).astype(BF)
    third_raw = jnp.einsum("bhwc,co->bhwo", hidden_two, expand_full, preferred_element_type=F32)
    stats_three = norm(local_moments(third_raw), ALL, local_px, 2)
    scaled_three = (third_raw - stats_three[0]) * stats_three[1]
    inner_three = scaled_three * gain_expand + bias_expand + features.astype(F32)
    output = jax.nn.gelu(inner_three).astype(BF)

    low, high = rims(output, ROWS, 1)
    outer = jnp.where(core == 0, low, high)
    outer_other = swap(outer)
    output_other = swap(output)
    output_pad = jnp.concatenate(
        [
            jnp.where(core == 0, low, outer_other),
            in_order(output, output_other, 1),
            jnp.where(core == 0, outer_other, high),
        ],
        axis=1,
    )
    tall = 2 * height
    heads_raw, heads_moments = conv_fwd(output_pad, heads_full, 512, mid)
    stats_heads = norm((heads_moments[0], heads_moments[1]), CHIPS, chip_px, 3)
    gain_own = lax.dynamic_slice_in_dim(gain_heads, core * mid, mid)
    bias_own = lax.dynamic_slice_in_dim(bias_heads, core * mid, mid)
    scaled_heads = (heads_raw - stats_heads[0]) * stats_heads[1]
    inner_heads = scaled_heads * gain_own + bias_own
    feature = jax.nn.gelu(inner_heads).astype(BF)
    feature_pad = with_rims(feature.reshape(crops, tall, width, mid), ("y",), 1)

    give, _ = conv_fwd(feature_pad, sides_full[0], 512, mid)
    gate, _ = conv_fwd(feature_pad, sides_full[1], 512, mid)
    message = swap(give.astype(BF)).astype(F32)
    sigma = jax.nn.sigmoid(gate)
    stream = (feature.astype(F32) + sigma * message).astype(BF)
    scores = jnp.dot(stream, class_full, preferred_element_type=F32)
    own_side = jnp.stack(
        [labels.astype(F32), depth_target, depth_mask.astype(F32)]
    )
    labels_chip, target_chip, mask_chip = in_order(own_side, swap(own_side), 2).reshape(3, chip_px)
    seg_scores = scores[:, :classes]
    log_total = jax.nn.logsumexp(seg_scores, axis=-1, keepdims=True)
    class_ids = jnp.arange(classes, dtype=jnp.int32)
    seg_back = jnp.exp(seg_scores - log_total) - (
        labels_chip.astype(jnp.int32)[:, None] == class_ids
    ).astype(F32)
    depth_scores = scores[:, classes]
    differ = depth_scores - target_chip
    depth_back = mask_chip * differ * lax.rsqrt(differ * differ + 1.0)
    score_back = jnp.concatenate(
        [
            jnp.where(core == 1, seg_back, 0.0),
            jnp.where(core == 0, depth_back, 0.0)[:, None],
            jnp.zeros((chip_px, 128 - classes - 1), F32),
        ],
        axis=1,
    ).astype(BF)
    class_grad = lax.dot_general(
        stream, score_back, (((0,), (0,)), ((), ())), preferred_element_type=F32
    )
    stream_grad = lax.dot_general(
        score_back, class_full, (((1,), (1,)), ((), ())), preferred_element_type=F32
    )

    scores_map = scores[:, : classes + 1].reshape(crops, tall, width, classes + 1)
    for_own = lax.dynamic_slice_in_dim(scores_map, core * height, height, axis=1)
    for_other = lax.dynamic_slice_in_dim(scores_map, (1 - core) * height, height, axis=1)
    from_other = swap(for_other)
    depth_pred = jnp.where(core == 0, for_own[..., classes], from_other[..., classes])
    seg_logits = jnp.where(core == 0, from_other[..., :classes], for_own[..., :classes])

    give_grad_other = (stream_grad * sigma).astype(BF)
    gate_grad_low = (stream_grad * message * sigma * (1.0 - sigma)).astype(BF)
    give_grad_low = swap(give_grad_other)
    side_grads = jnp.concatenate([give_grad_low, gate_grad_low], axis=1).reshape(
        crops, tall, width, 2 * mid
    )
    piece_side = mid // chips
    sides_grad = conv_wgrad(
        feature_pad, column_shifts(side_grads), mid, mid, piece_side
    )
    sides_grad = scatter_sum(sides_grad.reshape(-1, 2 * mid), CHIPS, 0)
    side_pad = with_rims(side_grads, ("y",), 1)
    feature_back = conv_dgrad(
        [side_pad[..., :mid], side_pad[..., mid:]], [sides_full[0], sides_full[1]], 256, F32
    )
    feature_grad = stream_grad + feature_back

    def norm_back(upstream, scaled, inverse, gain, axes, collective):
        dims = tuple(range(upstream.ndim - 1))
        bias_grad, gain_grad = small_sum(
            (jnp.sum(upstream, axis=dims), jnp.sum(upstream * scaled, axis=dims)),
            axes,
            "sums",
            1,
            collective,
        )
        grad = gain * inverse * (upstream - bias_grad / pixels - scaled * (gain_grad / pixels))
        return grad, gain_grad, bias_grad

    heads_raw_grad, gain_heads_own, bias_heads_own = norm_back(
        gelu_back(inner_heads, feature_grad), scaled_heads, stats_heads[1], gain_own, CHIPS, 4
    )
    heads_pair = jnp.stack([gain_heads_own, bias_heads_own])
    gain_heads_grad, bias_heads_grad = in_order(heads_pair, swap(heads_pair), 1)
    heads_low = heads_raw_grad.astype(BF).reshape(crops, tall, width, mid)
    heads_grad = conv_wgrad(output_pad, column_shifts(heads_low), 512, mid, deep // chips)
    heads_grad = scatter_sum(heads_grad.reshape(-1, mid), CHIPS, 0)
    output_both = conv_dgrad([with_rims(heads_low, ("y",), 1)], [heads_full], 512, BF).reshape(
        crops, tall, width, deep
    )
    output_grad = lax.dynamic_slice_in_dim(output_both, core * height, height, axis=1).astype(
        F32
    ) + swap(
        lax.dynamic_slice_in_dim(output_both, (1 - core) * height, height, axis=1)
    ).astype(F32)

    inner_three_grad = gelu_back(inner_three, output_grad)
    third_grad, gain_expand_grad, bias_expand_grad = norm_back(
        inner_three_grad, scaled_three, stats_three[1], gain_expand, ALL, 5
    )
    third_low = third_grad.astype(BF)
    expand_grad = jnp.einsum("bhwc,bhwo->co", hidden_two, third_low, preferred_element_type=F32)
    hidden_two_grad = jnp.einsum(
        "bhwo,co->bhwc", third_low, expand_full, preferred_element_type=F32
    )
    second_grad, gain_dilated_grad, bias_dilated_grad = norm_back(
        gelu_back(inner_two, hidden_two_grad), scaled_two, stats_two[1], gain_dilated, ALL, 6
    )
    second_low = second_grad.astype(BF)
    dilated_grad = jnp.stack(
        [
            jnp.einsum("bhwc,bhwo->co", tap, second_low, preferred_element_type=F32)
            for tap in taps_of(padded_one, 2, height)
        ],
        axis=1,
    )
    hidden_one_grad = dilated(with_rims(second_low, ROWS, 2), dilated_full, True)
    first_grad, gain_reduce_grad, bias_reduce_grad = norm_back(
        gelu_back(inner_one, hidden_one_grad), scaled_one, stats_one[1], gain_reduce, ALL, 7
    )
    first_low = first_grad.astype(BF)
    reduce_grad = jnp.einsum("bhwc,bhwo->co", features, first_low, preferred_element_type=F32)
    features_grad = inner_three_grad + jnp.einsum(
        "bhwo,co->bhwc", first_low, reduce_full, preferred_element_type=F32
    )

    heads_grad = heads_grad.astype(F32).reshape(9, 2 * w_heads.shape[1], mid)
    own_rows = w_heads.shape[1]
    heads_grad = in_order(
        lax.dynamic_slice_in_dim(heads_grad, core * own_rows, own_rows, axis=1),
        swap(lax.dynamic_slice_in_dim(heads_grad, (1 - core) * own_rows, own_rows, axis=1)),
        2,
    )
    sides_grad = sides_grad.astype(F32).reshape(9, piece_side, 2, mid)
    own_rows = piece_side // 2
    sides_mine = lax.dynamic_slice_in_dim(sides_grad, core * own_rows, own_rows, axis=1)
    sides_from = swap(
        lax.dynamic_slice_in_dim(sides_grad, (1 - core) * own_rows, own_rows, axis=1)
    )
    message_grad = jnp.stack(
        [
            jnp.where(core == 0, sides_from[:, :, 0], sides_mine[:, :, 0]),
            jnp.where(core == 0, sides_mine[:, :, 0], sides_from[:, :, 0]),
        ]
    )
    gate_grad = jnp.stack(
        [
            jnp.where(core == 0, sides_mine[:, :, 1], sides_from[:, :, 1]),
            jnp.where(core == 0, sides_from[:, :, 1], sides_mine[:, :, 1]),
        ]
    )
    packed_grad = jnp.concatenate(
        [
            reduce_grad.reshape(devices, r_rows, mid),
            dilated_grad.reshape(devices, d_rows * 9, mid),
            expand_grad.reshape(devices, -1, mid),
            jnp.pad(class_grad, ((0, 0), (0, mid - 128))).reshape(devices, -1, mid),
        ],
        axis=1,
    ).astype(BF)
    packed_grad = scatter_sum(packed_grad, ALL, 0)[0].astype(F32)
    class_own = packed_grad[cut[2] :]
    return (
        depth_pred,
        seg_logits,
        features_grad,
        packed_grad[: cut[0]],
        packed_grad[cut[0] : cut[1]].reshape(d_rows, 9, mid).transpose(1, 0, 2),
        packed_grad[cut[1] : cut[2]].reshape(e_rows, deep),
        gain_reduce_grad,
        bias_reduce_grad,
        gain_dilated_grad,
        bias_dilated_grad,
        gain_expand_grad,
        bias_expand_grad,
        heads_grad,
        gain_heads_grad,
        bias_heads_grad,
        message_grad,
        gate_grad,
        class_own[:, :classes],
        class_own[:, classes],
    )


def solution(mesh):
    img, row = mesh.shape["img"], mesh.shape["row"]
    side = row // 2
    fine = Mesh(mesh.devices.reshape(img // side, side, side, 2), ALL)
    crops, rows = ("z", "x"), ("y", "c")
    every = ALL
    placed = (
        P(crops, rows, None, None),
        P(every, None),
        P(None, every, None),
        P(every, None),
        P(),
        P(),
        P(),
        P(),
        P(),
        P(),
        P(None, every, None),
        P(),
        P(),
        P(None, None, every, None),
        P(None, None, every, None),
        P(every, None),
        P(every),
        P(crops, rows, None),
        P(crops, rows, None),
        P(crops, rows, None),
    )
    return jax.shard_map(
        per_device,
        mesh=fine,
        in_specs=placed,
        out_specs=(
            P(crops, rows, None),
            P(crops, rows, None, None),
            P(crops, rows, None, None),
            P(every, None),
            P(None, every, None),
            P(every, None),
            P(),
            P(),
            P(),
            P(),
            P(),
            P(),
            P(None, every, None),
            P(),
            P(),
            P(None, None, every, None),
            P(None, None, every, None),
            P(every, None),
            P(every),
        ),
        check_vma=False,
    )
```

```python
import functools

import jax
import jax.numpy as jnp
from jax import lax
from jax.experimental import pallas as pl
from jax.experimental.pallas import tpu as pltpu
from jax.sharding import Mesh
from jax.sharding import PartitionSpec as P

EPS = 1e-05
ALL = ("z", "x", "y", "c")
CHIPS = ("z", "x", "y")
ROWS = ("y", "c")
BF, F32 = jnp.bfloat16, jnp.float32
MESH = pl.DeviceIdType.MESH
VMEM_BYTES = 60 * 1024 * 1024


def flat_index(axes, sizes):
    index = 0
    for a, n in zip(axes, sizes):
        index = index * n + lax.axis_index(a)
    return index


def coordinates(axes, sizes, index):
    place = {}
    for a, n in reversed(list(zip(axes, sizes))):
        place[a] = lax.rem(index, n)
        index = index // n
    return place


def small_sum_kernel(stages, kind, count, v_ref, o_ref, *scratch):
    slots, send_sem, recv_sem = scratch[: len(stages)], scratch[-2], scratch[-1]
    barrier = pltpu.get_barrier_semaphore()
    peers = 0
    for axes, sizes in stages:
        me, n = flat_index(axes, sizes), total(sizes)
        for s in range(1, n):
            pl.semaphore_signal(
                barrier,
                inc=1,
                device_id=coordinates(axes, sizes, lax.rem(me + s, n)),
                device_id_type=MESH,
            )
            peers += 1
    pl.semaphore_wait(barrier, peers)
    current = v_ref[...]
    which = 0
    for slot, (axes, sizes) in zip(slots, stages):
        me, n = flat_index(axes, sizes), total(sizes)
        slot[me] = current
        copies = []
        for s in range(1, n):
            copy = pltpu.make_async_remote_copy(
                src_ref=slot.at[me],
                dst_ref=slot.at[me],
                send_sem=send_sem.at[which],
                recv_sem=recv_sem.at[which],
                device_id=coordinates(axes, sizes, lax.rem(me + s, n)),
                device_id_type=MESH,
            )
            copy.start()
            copies.append(copy)
            which += 1
        for copy in copies:
            copy.wait()
        first, second = slot[0, 0], slot[0, 1]
        for s in range(1, n):
            first = first + slot[s, 0]
            second = second + slot[s, 1]
        if kind == "moments":
            mean = first / n
            for s in range(n):
                second = second + count * jnp.square(slot[s, 0] - mean)
            first = mean
            count = count * n
        current = jnp.stack([first, second])
    o_ref[...] = current


def total(sizes):
    n = 1
    for size in sizes:
        n *= size
    return n


def small_sum(pair, axes, kind, count, collective):
    channels = pair[0].shape[0]
    stages = tuple(
        (group, tuple(lax.axis_size(a) for a in group)) for group in (axes[1:], axes[:1])
    )
    shape = (2, channels // 128, 128)
    n_copies = sum(total(sizes) - 1 for _, sizes in stages)
    out = pl.pallas_call(
        functools.partial(small_sum_kernel, stages, kind, float(count)),
        out_shape=jax.ShapeDtypeStruct(shape, F32),
        in_specs=[pl.BlockSpec(memory_space=pltpu.VMEM)],
        out_specs=pl.BlockSpec(memory_space=pltpu.VMEM),
        scratch_shapes=[pltpu.VMEM((total(sizes),) + shape, F32) for _, sizes in stages]
        + [pltpu.SemaphoreType.DMA((n_copies,)), pltpu.SemaphoreType.DMA((n_copies,))],
        compiler_params=pltpu.CompilerParams(collective_id=collective, has_side_effects=True),
        cost_estimate=pl.CostEstimate(flops=0, bytes_accessed=30_000_000, transcendentals=0),
    )(jnp.stack(pair).reshape(shape))
    return out[0].reshape(channels), out[1].reshape(channels)


def gather_kernel(geometry, both_cores, parts, *refs):
    n_z, n_x, n_y = geometry
    many = len(parts)
    arrays = (len(refs) - 3) // 2
    ins, outs = refs[:arrays], refs[arrays : 2 * arrays]
    own_sem, send_sem, recv_sem = refs[2 * arrays :]
    z, x, y, core = (lax.axis_index(a) for a in ALL)
    sizes = {"z": n_z, "x": n_x, "y": n_y, "c": 2}
    here = {"z": z, "x": x, "y": y, "c": core}
    used = ("z", "x", "y", "c") if both_cores else ("z", "x", "y")

    def peer(axis, s):
        return {axis: lax.rem(here[axis] + s, sizes[axis])}

    barrier = pltpu.get_barrier_semaphore()
    peers = 0
    for axis in used:
        for s in range(1, sizes[axis]):
            pl.semaphore_signal(barrier, inc=1, device_id=peer(axis, s), device_id_type=MESH)
            peers += 1
    pl.semaphore_wait(barrier, peers)

    def back(axis, s):
        return lax.rem(here[axis] + sizes[axis] - s, sizes[axis])

    def view(p, place):
        array, lead, dim, rows, _ = parts[p]
        index = (back("z", place[0]) * n_x + back("x", place[1])) * n_y + back("y", place[2])
        if both_cores:
            index = index * 2 + core
        span = pl.ds(pl.multiple_of(index * rows, rows), rows)
        if dim == 0:
            return outs[array].at[span]
        return outs[array].at[pl.ds(*lead), span] if lead else outs[array].at[:, span]

    def given(p):
        array, lead = parts[p][:2]
        return ins[array].at[pl.ds(*lead)] if lead else ins[array]

    started = []

    def send(p, place, axis, s):
        source = given(p) if place == (0, 0, 0) else view(p, place)
        which = len(started)
        copy = pltpu.make_async_remote_copy(
            src_ref=source,
            dst_ref=view(p, place),
            send_sem=send_sem.at[which],
            recv_sem=recv_sem.at[which],
            device_id=peer(axis, s),
            device_id_type=MESH,
        )
        copy.start()
        started.append(copy)
        return copy

    last = []

    def to_core(p, place):
        if both_cores:
            last.append(send(p, place, "c", 1))

    own = []
    along_z = {}
    for s in range(1, n_z):
        for p in range(many):
            along_z[s, p] = send(p, (0, 0, 0), "z", s)
    second, third = {}, {}

    def spread(p, zs):
        first_axis, second_axis = ("x", "y") if parts[p][4] == 1 else ("y", "x")
        for s in range(1, sizes[first_axis]):
            second[p, zs, s] = send(p, (zs, 0, 0), first_axis, s)
        for s in range(1, sizes[second_axis]):
            third[p, zs, 0, s] = send(p, (zs, 0, 0), second_axis, s)
        to_core(p, (zs, 0, 0))

    def place_of(p, zs, a, b):
        return (zs, a, b) if parts[p][4] == 1 else (zs, b, a)

    for p in range(many):
        spread(p, 0)
    for p in range(many):
        copy = pltpu.make_async_copy(given(p), view(p, (0, 0, 0)), own_sem.at[p])
        copy.start()
        own.append(copy)
    for zs in range(1, n_z):
        for p in range(many):
            along_z[zs, p].wait_recv()
            spread(p, zs)
    for zs in range(n_z):
        for p in range(many):
            first_axis, second_axis = ("x", "y") if parts[p][4] == 1 else ("y", "x")
            for a in range(1, sizes[first_axis]):
                second[p, zs, a].wait_recv()
                for s in range(1, sizes[second_axis]):
                    third[p, zs, a, s] = send(p, place_of(p, zs, a, 0), second_axis, s)
                to_core(p, place_of(p, zs, a, 0))
    for zs in range(n_z):
        for p in range(many):
            first_axis, second_axis = ("x", "y") if parts[p][4] == 1 else ("y", "x")
            for b in range(1, sizes[second_axis]):
                for a in range(sizes[first_axis]):
                    third[p, zs, a, b].wait_recv()
                    to_core(p, place_of(p, zs, a, b))
    for copy in last:
        copy.wait_recv()
    for copy in own:
        copy.wait()
    for copy in started:
        copy.wait_send()


def gather_pieces(arrays, parts, both_cores, collective, microseconds):
    geometry = tuple(lax.axis_size(a) for a in CHIPS)
    chips = total(geometry)
    many = len(parts)
    cut_at = {part[0]: part[2] for part in parts}
    shapes = []
    for i, array in enumerate(arrays):
        shape = list(array.shape)
        shape[cut_at[i]] *= chips * (2 if both_cores else 1)
        shapes.append(jax.ShapeDtypeStruct(tuple(shape), array.dtype))
    n_copies = many * (chips - 1 + (chips if both_cores else 0))
    return pl.pallas_call(
        functools.partial(gather_kernel, geometry, both_cores, parts),
        out_shape=shapes,
        in_specs=[pl.BlockSpec(memory_space=pl.ANY)] * len(arrays),
        out_specs=[pl.BlockSpec(memory_space=pl.ANY)] * len(arrays),
        scratch_shapes=[
            pltpu.SemaphoreType.DMA((many,)),
            pltpu.SemaphoreType.DMA((n_copies,)),
            pltpu.SemaphoreType.DMA((n_copies,)),
        ],
        compiler_params=pltpu.CompilerParams(collective_id=collective, has_side_effects=True),
        cost_estimate=pl.CostEstimate(
            flops=0, bytes_accessed=int(3.5e6 * microseconds), transcendentals=0
        ),
    )(*arrays)


def send_blocks(value, axis, dim):
    n, me = lax.axis_size(axis), lax.axis_index(axis)
    own = lax.dynamic_index_in_dim(value, me, dim, keepdims=False)
    arrived = []
    for s in range(1, n):
        block = lax.dynamic_index_in_dim(value, lax.rem(me + s, n), dim, keepdims=False)
        arrived.append(lax.ppermute(block, axis, [(i, (i + s) % n) for i in range(n)]))
    return own, arrived


def add_blocks(own, arrived):
    result = own.astype(F32)
    for block in arrived:
        result = result + block.astype(F32)
    return result.astype(BF)


def scatter_kernel(geometry, orders, window, *refs):
    many = len(orders)
    ins, outs = refs[:many], refs[many : 2 * many]
    own, from_first, from_second, from_third = (
        refs[(2 + i) * many : (3 + i) * many] for i in range(4)
    )
    own_sem, send_sem, recv_sem = refs[6 * many :]
    sizes = dict(zip(CHIPS, geometry))
    sizes[None] = 1
    here = {a: lax.axis_index(a) for a in CHIPS}

    def forth(axis, s):
        return lax.rem(here[axis] + s, sizes[axis])

    barrier = pltpu.get_barrier_semaphore()
    peers = 0
    for axis in CHIPS:
        for s in range(1, sizes[axis]):
            pl.semaphore_signal(
                barrier, inc=1, device_id={axis: forth(axis, s)}, device_id_type=MESH
            )
            peers += 1
    pl.semaphore_wait(barrier, peers)

    started = []

    def send(source, target, axis, s):
        which = len(started)
        copy = pltpu.make_async_remote_copy(
            src_ref=source,
            dst_ref=target,
            send_sem=send_sem.at[which],
            recv_sem=recv_sem.at[which],
            device_id={axis: forth(axis, s)},
            device_id_type=MESH,
        )
        copy.start()
        started.append(copy)
        return copy

    plans = []
    for order in orders:
        first, second, third = (tuple(order) + (None, None))[:3]
        places = [
            (s3, s2)
            for s2 in reversed(range(sizes[second]))
            for s3 in list(range(1, sizes[third])) + [0]
        ]
        plans.append((first, second, third, places))

    def block(p, s3, s2, s1):
        index = 0
        steps = dict(zip(plans[p][:3], (s1, s2, s3)))
        for axis in CHIPS:
            if axis in steps:
                index = index * sizes[axis] + forth(axis, steps[axis])
        return index

    loads, one, two, three = {}, {}, {}, {}
    for p in range(many):
        for k, (s3, s2) in enumerate(plans[p][3]):
            copy = pltpu.make_async_copy(
                ins[p].at[block(p, s3, s2, 0)], own[p].at[k], own_sem.at[len(loads)]
            )
            copy.start()
            loads[p, k] = copy

    def send_first(k):
        for p in range(many):
            first, places = plans[p][0], plans[p][3]
            if k < len(places):
                s3, s2 = places[k]
                for s1 in range(1, sizes[first]):
                    one[p, k, s1] = send(
                        ins[p].at[block(p, s3, s2, s1)], from_first[p].at[s1 - 1, k], first, s1
                    )

    waited = set()
    longest = max(len(plan[3]) for plan in plans)
    for k in range(min(window, longest)):
        send_first(k)
    for k in range(longest):
        for p in range(many):
            first, second, third, places = plans[p]
            if k < longest - len(places):
                continue
            own_k = k - (longest - len(places))
            s3, s2 = places[own_k]
            loads[p, own_k].wait()
            terms = []
            for s in range(1, sizes[first]):
                one[p, own_k, s].wait_recv()
                terms.append((from_first[p], (s - 1, own_k)))
            if s2 == 0:
                for s in range(1, sizes[second]):
                    two[p, s3, s].wait_recv()
                    terms.append((from_second[p], (s - 1, s3)))
                if s3 == 0:
                    for s in range(1, sizes[third]):
                        three[p, s].wait_recv()
                        terms.append((from_third[p], (s - 1,)))
            final = s2 == 0 and s3 == 0

            def add(t, carry, p=p, k=own_k, terms=terms, final=final):
                value = own[p][k, t].astype(F32)
                for ref, index in terms:
                    value = value + ref[(*index, t)].astype(F32)
                if final:
                    outs[p][t] = value
                else:
                    own[p][k, t] = value.astype(BF)
                return carry

            lax.fori_loop(0, own[p].shape[1], add, 0)
            if s2 > 0:
                two[p, s3, s2] = send(own[p].at[own_k], from_second[p].at[s2 - 1, s3], second, s2)
            elif s3 > 0:
                three[p, s3] = send(own[p].at[own_k], from_third[p].at[s3 - 1], third, s3)
        if k + window < longest:
            for key, copy in one.items():
                if key[1] == k:
                    copy.wait_send()
                    waited.add(id(copy))
            send_first(k + window)
    for copy in started:
        if id(copy) not in waited:
            copy.wait_send()


def scatter_blocks(arrays, orders, window, collective):
    geometry = tuple(lax.axis_size(a) for a in CHIPS)
    own, first, second, third = [], [], [], []
    copies = 0
    for array, order in zip(arrays, orders):
        shape = array.shape[1:]
        n1, n2, n3 = (tuple(lax.axis_size(a) for a in order) + (1, 1))[:3]
        own.append(pltpu.VMEM((n3 * n2,) + shape, BF))
        first.append(pltpu.VMEM((n1 - 1, n3 * n2) + shape, BF))
        nothing = (1, 1, 16, 128)
        second.append(pltpu.VMEM((n2 - 1, n3) + shape if n2 > 1 else nothing, BF))
        third.append(pltpu.VMEM((n3 - 1,) + shape if n3 > 1 else nothing, BF))
        copies += n3 * n2 * (n1 - 1) + n3 * (n2 - 1) + n3 - 1
    loads = sum(s.shape[0] for s in own)
    return pl.pallas_call(
        functools.partial(scatter_kernel, geometry, orders, window),
        out_shape=[jax.ShapeDtypeStruct(a.shape[1:], F32) for a in arrays],
        in_specs=[pl.BlockSpec(memory_space=pl.ANY)] * len(arrays),
        out_specs=[pl.BlockSpec(memory_space=pltpu.VMEM)] * len(arrays),
        scratch_shapes=own
        + first
        + second
        + third
        + [
            pltpu.SemaphoreType.DMA((loads,)),
            pltpu.SemaphoreType.DMA((copies,)),
            pltpu.SemaphoreType.DMA((copies,)),
        ],
        compiler_params=pltpu.CompilerParams(
            collective_id=collective, has_side_effects=True, vmem_limit_bytes=VMEM_BYTES
        ),
        cost_estimate=pl.CostEstimate(flops=0, bytes_accessed=150_000_000, transcendentals=0),
    )(*arrays)


def combine_cols(before, same, after, col, spread):
    n = same.shape[0]
    before = jnp.where(col < spread, 0.0, pltpu.roll(before, spread, 0))
    after = jnp.where(col >= n - spread, 0.0, pltpu.roll(after, n - spread, 0))
    return before + same + after


def conv_fwd(xpad, w, spread, kc, nc, n_blocks, n_first, moments, out_dtype):
    batch, height_pad, width, depth = xpad.shape
    height, wide = height_pad - 2 * spread, n_blocks * nc
    px = batch * height * width
    steps = depth // kc

    def body(first_ref, x_ref, w_ref, *rest):
        o_ref, acc = rest[0], rest[-1]
        k = pl.program_id(1)

        def dots(first):
            for b in range(3):
                for a in range(3):
                    xa = x_ref[:, a * spread : a * spread + height].reshape(px, kc)
                    d = jnp.dot(xa, w_ref[3 * a + b], preferred_element_type=F32)
                    if first and a == 0:
                        acc[b] = d
                    else:
                        acc[b] += d

        @pl.when(k == 0)
        def _():
            dots(True)

        @pl.when(k > 0)
        def _():
            dots(False)

        @pl.when(k == steps - 1)
        def _():
            col = lax.broadcasted_iota(jnp.int32, (width, nc), 0)

            def store(i, running):
                r = pl.ds(pl.multiple_of(i * width, width), width)
                v = combine_cols(acc[0, r], acc[1, r], acc[2, r], col, spread)
                o_ref[r] = v.astype(out_dtype)
                return running + jnp.sum(v.reshape(width // 8, 8, nc), axis=0) if moments else 0

            start = jnp.zeros((8, nc), F32)
            running = lax.fori_loop(0, batch * height, store, start if moments else 0)
            if moments:
                mean = jnp.sum(running, axis=0, keepdims=True) / px

                def deviation(i, so_far):
                    r = pl.ds(pl.multiple_of(i * width, width), width)
                    v = jnp.square(o_ref[r] - mean)
                    return so_far + jnp.sum(v.reshape(width // 8, 8, nc), axis=0)

                m2 = lax.fori_loop(0, batch * height, deviation, start)
                row = lax.broadcasted_iota(jnp.int32, (8, nc), 0)
                rest[1][...] = jnp.where(row == 0, mean, jnp.sum(m2, axis=0, keepdims=True))

    out_specs = [pl.BlockSpec((px, nc), lambda n, k, f: (0, n))]
    out_shape = [jax.ShapeDtypeStruct((px, wide), out_dtype)]
    if moments:
        out_specs.append(pl.BlockSpec((8, nc), lambda n, k, f: (0, n)))
        out_shape.append(jax.ShapeDtypeStruct((8, wide), F32))
    return pl.pallas_call(
        body,
        grid_spec=pltpu.PrefetchScalarGridSpec(
            num_scalar_prefetch=1,
            grid=(n_blocks, steps),
            in_specs=[
                pl.BlockSpec((batch, height_pad, width, kc), lambda n, k, f: (0, 0, 0, k)),
                pl.BlockSpec((9, kc, nc), lambda n, k, f: (0, k, n + f[0])),
            ],
            out_specs=out_specs,
            scratch_shapes=[pltpu.VMEM((3, px, nc), F32)],
        ),
        out_shape=out_shape,
        compiler_params=pltpu.CompilerParams(vmem_limit_bytes=VMEM_BYTES),
        cost_estimate=pl.CostEstimate(
            flops=18 * px * depth * wide,
            bytes_accessed=18 * depth * wide + 2 * px * depth + 4 * px * wide,
            transcendentals=0,
        ),
    )(n_first, xpad, w)


def conv_dgrad(gpads, weights, spread, cc, c_range, n_first, out_dtype, by_core=False):
    batch, height_pad, width, wide = gpads[0].shape
    many = len(gpads)
    height, depth = height_pad - 2 * spread, len(c_range) * cc
    c_first = c_range[0]
    px = batch * height * width
    dims = (((1,), (1,)), ((), ()))
    results = 2 if by_core else 1
    lines = height // results

    def body(first_ref, *refs):
        gs, ws, outs, acc = refs[:many], refs[many : 2 * many], refs[2 * many : -1], refs[-1]
        for q in range(many):
            for b in range(3):
                for a in range(3):
                    top = (2 - a) * spread
                    ga = gs[q][:, top : top + height].reshape(px, wide)
                    d = lax.dot_general(ga, ws[q][3 * a + b], dims, preferred_element_type=F32)
                    if q == 0 and a == 0:
                        acc[2 - b] = d
                    else:
                        acc[2 - b] += d
        col = lax.broadcasted_iota(jnp.int32, (width, cc), 0)

        for which, o_ref in enumerate(outs):

            def store(i, carry, which=which, o_ref=o_ref):
                line = i
                if by_core:
                    part = first_ref[0] if which == 0 else 1 - first_ref[0]
                    line = i // lines * height + part * lines + lax.rem(i, lines)
                r = pl.ds(pl.multiple_of(line * width, width), width)
                value = combine_cols(acc[0, r], acc[1, r], acc[2, r], col, spread)
                o_ref[pl.ds(pl.multiple_of(i * width, width), width)] = value.astype(out_dtype)
                return carry

            lax.fori_loop(0, batch * lines, store, 0)

    return pl.pallas_call(
        body,
        grid_spec=pltpu.PrefetchScalarGridSpec(
            num_scalar_prefetch=1,
            grid=(depth // cc,),
            in_specs=[pl.BlockSpec((batch, height_pad, width, wide), lambda c, f: (0, 0, 0, 0))]
            * many
            + [pl.BlockSpec((9, cc, wide), lambda c, f: (0, c + c_first, f[0]))] * many,
            out_specs=[pl.BlockSpec((px // results, cc), lambda c, f: (0, c))] * results,
            scratch_shapes=[pltpu.VMEM((3, px, cc), F32)],
        ),
        out_shape=[jax.ShapeDtypeStruct((px // results, depth), out_dtype)] * results,
        compiler_params=pltpu.CompilerParams(vmem_limit_bytes=VMEM_BYTES),
        cost_estimate=pl.CostEstimate(
            flops=18 * many * px * depth * wide,
            bytes_accessed=18 * many * depth * wide + 4 * px * depth,
            transcendentals=0,
        ),
    )(n_first, *gpads, *weights)


def conv_wgrad(xpad, grad, spread, cc, nc, piece, shares):
    batch, height_pad, width, depth = xpad.shape
    height, wide = height_pad - 2 * spread, grad.shape[1]
    px = batch * height * width
    each, blocks = cc // piece, wide // nc
    lines = 128 // width

    def body(x_ref, g_ref, *rest):
        outs, shifted = rest[:-1], rest[-1]

        @pl.when(pl.program_id(1) == 0)
        def _():
            col = lax.broadcasted_iota(jnp.int32, (width, nc), 0)

            def turn(i, carry):
                r = pl.ds(pl.multiple_of(i * 128, 128), 128)
                block = g_ref[r].astype(F32)
                for b in range(3):
                    moved = []
                    for j in range(lines):
                        v = block[j * width : (j + 1) * width]
                        if b == 0:
                            v = jnp.where(
                                col >= width - spread, 0.0, pltpu.roll(v, width - spread, 0)
                            )
                        elif b == 2:
                            v = jnp.where(col < spread, 0.0, pltpu.roll(v, spread, 0))
                        moved.append(v)
                    shifted[b, :, r] = jnp.concatenate(moved, axis=0).T.astype(BF)
                return carry

            lax.fori_loop(0, px // 128, turn, 0)

        for a in range(3):
            xa = x_ref[:, a * spread : a * spread + height].reshape(px, cc)
            for b in range(3):
                d = jnp.dot(shifted[b], xa, preferred_element_type=F32).T.astype(BF)
                for out, (taps, low, high) in zip(outs, shares):
                    if 3 * a + b in taps:
                        for j in range(each):
                            out[j, taps.index(3 * a + b)] = d[j * piece : (j + 1) * piece, low:high]

    return pl.pallas_call(
        body,
        grid=(blocks, depth // cc),
        in_specs=[
            pl.BlockSpec((batch, height_pad, width, cc), lambda n, c: (0, 0, 0, c)),
            pl.BlockSpec((px, nc), lambda n, c: (0, n)),
        ],
        out_specs=[
            pl.BlockSpec((each, len(taps), piece, high - low), lambda n, c: (c, 0, 0, n))
            for taps, low, high in shares
        ],
        out_shape=[
            jax.ShapeDtypeStruct((depth // piece, len(taps), piece, blocks * (high - low)), BF)
            for taps, low, high in shares
        ],
        scratch_shapes=[pltpu.VMEM((3, nc, px), BF)],
        compiler_params=pltpu.CompilerParams(vmem_limit_bytes=VMEM_BYTES),
        cost_estimate=pl.CostEstimate(
            flops=18 * px * depth * wide,
            bytes_accessed=18 * depth * wide + 2 * px * depth,
            transcendentals=0,
        ),
    )(xpad, grad)


def swap(value):
    return lax.ppermute(value, "c", [(0, 1), (1, 0)])


def in_order(mine, other, dim):
    first = lax.axis_index("c") == 0
    return jnp.concatenate(
        [jnp.where(first, mine, other), jnp.where(first, other, mine)], axis=dim
    )


def core_sum(blocks):
    core = lax.axis_index("c")
    mine = lax.dynamic_index_in_dim(blocks, core, 1, keepdims=False)
    other = lax.dynamic_index_in_dim(blocks, 1 - core, 1, keepdims=False).astype(BF)
    return (mine.astype(F32) + swap(other).astype(F32)).astype(BF)


def rims(block, axes, width):
    count = 1
    for a in axes:
        count *= lax.axis_size(a)
    forward = [(i, i + 1) for i in range(count - 1)]
    backward = [(t, s) for s, t in forward]
    low = lax.ppermute(block[:, block.shape[1] - width :], axes, forward)
    high = lax.ppermute(block[:, :width], axes, backward)
    return low, high


def with_rims(block, axes, width):
    low, high = rims(block, axes, width)
    return jnp.concatenate([low, block, high], axis=1)


def local_moments(value):
    mean = jnp.mean(value, axis=(0, 1, 2))
    return mean, jnp.sum(jnp.square(value - mean), axis=(0, 1, 2))


def gelu_back(inner, upstream):
    return jax.vjp(jax.nn.gelu, inner)[1](upstream)[0]


def gather(value, axes, dim):
    return lax.all_gather(value, axes, axis=dim, tiled=True)


def scatter_sum(value, axes, dim):
    return lax.psum_scatter(value, axes, scatter_dimension=dim, tiled=True)


def per_device(
    features,
    w_reduce,
    w_dilated,
    w_expand,
    gain_reduce,
    bias_reduce,
    gain_dilated,
    bias_dilated,
    gain_expand,
    bias_expand,
    w_heads,
    gain_heads,
    bias_heads,
    w_message,
    w_gate,
    w_seg,
    w_depth,
    labels,
    depth_target,
    depth_mask,
):
    core = lax.axis_index("c")
    chips = lax.axis_size("z") * lax.axis_size("x") * lax.axis_size("y")
    devices = chips * 2
    crops, height, width, deep = features.shape
    mid = w_reduce.shape[1]
    classes = w_seg.shape[1]
    local_px = crops * height * width
    pixels = local_px * devices
    chip_px = local_px * 2

    tied = lax.optimization_barrier
    r_rows, d_rows = w_reduce.shape[0], w_dilated.shape[1]
    heads_full = gather(w_heads, ALL, 1)
    message_chip = in_order(w_message[1 - core], swap(w_message[core]), 1)
    message_full = gather(message_chip, CHIPS, 1)
    gate_chip = in_order(w_gate[core], swap(w_gate[1 - core]), 1)
    side_rows = gate_chip.shape[1]
    quarters = deep // mid
    small = jnp.concatenate([w_seg, w_depth[:, None]], axis=1)
    small = jnp.pad(small, ((0, 0), (0, mid - classes - 1)))
    side_blocks = jnp.stack(
        [w_expand[:, q * mid : (q + 1) * mid] for q in range(quarters)] + [small]
    )
    reduce_full, dilated_full, blocks_full = gather_pieces(
        (w_reduce, w_dilated, side_blocks),
        ((0, None, 0, r_rows, 2), (1, None, 1, d_rows, 1), (2, None, 1, d_rows, 2)),
        True,
        8,
        40,
    )
    expand_full = blocks_full[:quarters]
    class_full = blocks_full[quarters, :, :128]
    none = jnp.zeros((1,), jnp.int32)
    own_half = core.astype(jnp.int32).reshape(1)

    first_raw = jnp.einsum("bhwc,co->bhwo", features, reduce_full, preferred_element_type=F32)

    def norm(raw_moments, axes, count, collective):
        mean, m2 = small_sum(raw_moments, axes, "moments", count, collective)
        return mean, lax.rsqrt(m2 / pixels + EPS)

    stats_one = norm(local_moments(first_raw), ALL, local_px, 0)
    scaled_one = (first_raw - stats_one[0]) * stats_one[1]
    inner_one = scaled_one * gain_reduce + bias_reduce
    hidden_one = jax.nn.gelu(inner_one).astype(BF)
    padded_one = with_rims(hidden_one, ROWS, 2)

    second_raw, second_moments = conv_fwd(
        padded_one, dilated_full, 2, 256, mid, 1, none, True, F32
    )
    second_raw = second_raw.reshape(crops, height, width, mid)
    stats_two = norm((second_moments[0], second_moments[1]), ALL, local_px, 1)
    scaled_two = (second_raw - stats_two[0]) * stats_two[1]
    inner_two = scaled_two * gain_dilated + bias_dilated
    hidden_two = jax.nn.gelu(inner_two).astype(BF)
    third_raw = jnp.einsum(
        "bhwc,qco->bhwqo", hidden_two, expand_full, preferred_element_type=F32
    ).reshape(crops, height, width, deep)
    stats_three = norm(local_moments(third_raw), ALL, local_px, 2)
    scaled_three = (third_raw - stats_three[0]) * stats_three[1]
    inner_three = scaled_three * gain_expand + bias_expand + features.astype(F32)
    output = jax.nn.gelu(inner_three).astype(BF)

    low, high = rims(output, ROWS, 1)
    outer = jnp.where(core == 0, low, high)
    outer_other = swap(outer)
    output_other = swap(output)
    output_pad = jnp.concatenate(
        [
            jnp.where(core == 0, low, outer_other),
            in_order(output, output_other, 1),
            jnp.where(core == 0, outer_other, high),
        ],
        axis=1,
    )
    tall = 2 * height
    gate_chip, output_pad = tied((gate_chip, output_pad))
    (gate_full,) = gather_pieces(
        (gate_chip,), ((0, (0, 5), 1, side_rows, 1), (0, (5, 4), 1, side_rows, 2)), False, 9, 50
    )
    gate_full, output_pad = tied((gate_full, output_pad))
    heads_raw, heads_moments = conv_fwd(
        output_pad, heads_full, 1, 512, mid, 1, own_half, True, F32
    )
    stats_heads = norm((heads_moments[0], heads_moments[1]), CHIPS, chip_px, 3)
    gain_own = lax.dynamic_slice_in_dim(gain_heads, core * mid, mid)
    bias_own = lax.dynamic_slice_in_dim(bias_heads, core * mid, mid)
    scaled_heads = (heads_raw - stats_heads[0]) * stats_heads[1]
    inner_heads = scaled_heads * gain_own + bias_own
    feature = jax.nn.gelu(inner_heads).astype(BF)
    feature_pad = with_rims(feature.reshape(crops, tall, width, mid), ("y",), 1)

    (give,) = conv_fwd(feature_pad, message_full, 1, 256, mid, 1, none, False, BF)
    (gate,) = conv_fwd(feature_pad, gate_full, 1, 256, mid, 1, none, False, F32)
    message = swap(give).astype(F32)
    sigma = jax.nn.sigmoid(gate)
    stream = (feature.astype(F32) + sigma * message).astype(BF)
    scores = jnp.dot(stream, class_full, preferred_element_type=F32)
    own_side = jnp.stack(
        [labels.astype(F32), depth_target, depth_mask.astype(F32)]
    )
    labels_chip, target_chip, mask_chip = in_order(own_side, swap(own_side), 2).reshape(3, chip_px)
    seg_scores = scores[:, :classes]
    log_total = jax.nn.logsumexp(seg_scores, axis=-1, keepdims=True)
    class_ids = jnp.arange(classes, dtype=jnp.int32)
    seg_back = jnp.exp(seg_scores - log_total) - (
        labels_chip.astype(jnp.int32)[:, None] == class_ids
    ).astype(F32)
    depth_scores = scores[:, classes]
    differ = depth_scores - target_chip
    depth_back = mask_chip * differ * lax.rsqrt(differ * differ + 1.0)
    score_back = jnp.concatenate(
        [
            jnp.where(core == 1, seg_back, 0.0),
            jnp.where(core == 0, depth_back, 0.0)[:, None],
            jnp.zeros((chip_px, 128 - classes - 1), F32),
        ],
        axis=1,
    ).astype(BF)
    class_grad = lax.dot_general(
        stream, score_back, (((0,), (0,)), ((), ())), preferred_element_type=F32
    )
    stream_grad = lax.dot_general(
        score_back, class_full, (((1,), (1,)), ((), ())), preferred_element_type=F32
    )

    scores_map = scores[:, : classes + 1].reshape(crops, tall, width, classes + 1)
    for_own = lax.dynamic_slice_in_dim(scores_map, core * height, height, axis=1)
    for_other = lax.dynamic_slice_in_dim(scores_map, (1 - core) * height, height, axis=1)
    from_other = swap(for_other)
    depth_pred = jnp.where(core == 0, for_own[..., classes], from_other[..., classes])
    seg_logits = jnp.where(core == 0, from_other[..., :classes], for_own[..., :classes])

    give_grad_other = (stream_grad * sigma).astype(BF)
    gate_grad_low = (stream_grad * message * sigma * (1.0 - sigma)).astype(BF)
    give_grad_low = swap(give_grad_other)
    piece_side = mid // chips
    tall_shape = (crops, tall, width, mid)
    give_pad, gate_pad = (
        with_rims(g.reshape(tall_shape), ("y",), 1) for g in (give_grad_low, gate_grad_low)
    )
    every_tap = tuple(range(9))
    (sides_grad,) = conv_wgrad(
        feature_pad,
        jnp.concatenate([give_grad_low, gate_grad_low], axis=1),
        1,
        mid,
        mid,
        piece_side,
        ((every_tap, 0, mid),),
    )
    sides_grad, give_pad, gate_pad = tied((sides_grad, give_pad, gate_pad))
    sides_grad = scatter_sum(sides_grad.reshape(-1, 2 * mid), CHIPS, 0)
    (feature_back,) = conv_dgrad(
        [give_pad, gate_pad], [message_full, gate_full], 1, 256, range(mid // 256), none, F32
    )
    feature_grad = stream_grad + feature_back

    def norm_back(upstream, scaled, inverse, gain, axes, collective):
        dims = tuple(range(upstream.ndim - 1))
        bias_grad, gain_grad = small_sum(
            (jnp.sum(upstream, axis=dims), jnp.sum(upstream * scaled, axis=dims)),
            axes,
            "sums",
            1,
            collective,
        )
        grad = gain * inverse * (upstream - bias_grad / pixels - scaled * (gain_grad / pixels))
        return grad, gain_grad, bias_grad

    heads_raw_grad, gain_heads_own, bias_heads_own = norm_back(
        gelu_back(inner_heads, feature_grad), scaled_heads, stats_heads[1], gain_own, CHIPS, 4
    )
    heads_pair = jnp.stack([gain_heads_own, bias_heads_own])
    gain_heads_grad, bias_heads_grad = in_order(heads_pair, swap(heads_pair), 1)
    heads_low = heads_raw_grad.astype(BF)
    heads_pad = with_rims(heads_low.reshape(tall_shape), ("y",), 1)
    quarter = mid // 4
    heads_first, heads_yx, heads_xy = conv_wgrad(
        output_pad,
        heads_low,
        1,
        512,
        mid,
        deep // chips,
        (
            (every_tap, 0, 2 * quarter),
            (every_tap, 2 * quarter, 3 * quarter),
            (every_tap, 3 * quarter, mid),
        ),
    )
    heads_first, heads_yx, heads_xy, heads_pad = tied((heads_first, heads_yx, heads_xy, heads_pad))
    heads_first = scatter_sum(heads_first.reshape(-1, 2 * quarter), CHIPS, 0)
    geometry = tuple(lax.axis_size(a) for a in CHIPS)
    heads_yx, heads_xy = (v.reshape(geometry + v.shape[1:]) for v in (heads_yx, heads_xy))
    heads_yx, heads_xy = send_blocks(heads_yx, "y", 2), send_blocks(heads_xy, "x", 1)
    grad_own, grad_other = conv_dgrad(
        [heads_pad], [heads_full], 1, 512, range(deep // 512), own_half, BF, True
    )
    grad_own, grad_other, heads_yx, heads_xy = tied((grad_own, grad_other, heads_yx, heads_xy))
    output_grad = (grad_own.astype(F32) + swap(grad_other).astype(F32)).reshape(
        crops, height, width, deep
    )

    inner_three_grad = gelu_back(inner_three, output_grad)
    third_grad, gain_expand_grad, bias_expand_grad = norm_back(
        inner_three_grad, scaled_three, stats_three[1], gain_expand, ALL, 5
    )
    third_low, sides_grad = tied((third_grad.astype(BF), sides_grad))
    expand_grad = jnp.einsum("bhwc,bhwo->co", hidden_two, third_low, preferred_element_type=F32)
    expand_grad = core_sum(
        jnp.concatenate([expand_grad, class_grad], axis=1).reshape(chips, 2, 1, d_rows, deep + 128)
    )
    hidden_two_grad = jnp.einsum(
        "bhwqo,qco->bhwc",
        third_low.reshape(crops, height, width, quarters, mid),
        expand_full,
        preferred_element_type=F32,
    )
    second_grad, gain_dilated_grad, bias_dilated_grad = norm_back(
        gelu_back(inner_two, hidden_two_grad), scaled_two, stats_two[1], gain_dilated, ALL, 6
    )
    second_low = second_grad.astype(BF)
    second_pad, second_low, heads_yx, heads_xy = tied(
        (with_rims(second_low, ROWS, 2), second_low, heads_yx, heads_xy)
    )
    heads_yx = send_blocks(add_blocks(*heads_yx), "x", 1)
    heads_xy = send_blocks(add_blocks(*heads_xy), "y", 1)
    (dilated_grad,) = conv_wgrad(
        padded_one, second_low.reshape(-1, mid), 2, mid, mid, d_rows, ((every_tap, 0, mid),)
    )
    dilated_grad = core_sum(dilated_grad.reshape(chips, 2, 9, d_rows, mid))
    (hidden_one_grad,) = conv_dgrad(
        [second_pad], [dilated_full], 2, 256, range(mid // 256), none, F32
    )
    hidden_one_grad, heads_yx, heads_xy = tied((hidden_one_grad, heads_yx, heads_xy))
    hidden_one_grad = hidden_one_grad.reshape(crops, height, width, mid)
    first_grad, gain_reduce_grad, bias_reduce_grad = norm_back(
        gelu_back(inner_one, hidden_one_grad), scaled_one, stats_one[1], gain_reduce, ALL, 7
    )
    first_low = first_grad.astype(BF)
    reduce_grad = jnp.einsum("bhwc,bhwo->co", features, first_low, preferred_element_type=F32)
    reduce_grad = core_sum(reduce_grad.reshape(chips, 2, 1, r_rows, mid))
    features_grad = inner_three_grad + jnp.einsum(
        "bhwo,co->bhwc", first_low, reduce_full, preferred_element_type=F32
    )

    heads_yx, heads_xy = add_blocks(*heads_yx), add_blocks(*heads_xy)
    features_grad, heads_first, heads_yx, heads_xy, reduce_grad = tied(
        (features_grad, heads_first, heads_yx, heads_xy, reduce_grad)
    )
    heads_yx, heads_xy, dilated_grad, expand_grad, reduce_grad = scatter_blocks(
        (heads_yx, heads_xy, dilated_grad, expand_grad, reduce_grad),
        (("z",), ("z",), ("y", "x", "z"), ("x", "y", "z"), ("x", "y", "z")),
        4,
        10,
    )
    reduce_grad = reduce_grad[0]
    expand_grad, class_grad = expand_grad[0, :, :deep], expand_grad[0, :, deep:]

    heads_first = heads_first.astype(F32).reshape(9, deep // chips, 2 * quarter)
    heads_grad = jnp.concatenate([heads_first, heads_yx, heads_xy], axis=2)
    own_rows = w_heads.shape[1]
    heads_grad = in_order(
        lax.dynamic_slice_in_dim(heads_grad, core * own_rows, own_rows, axis=1),
        swap(lax.dynamic_slice_in_dim(heads_grad, (1 - core) * own_rows, own_rows, axis=1)),
        2,
    ).astype(F32)
    sides_grad = sides_grad.astype(F32).reshape(9, piece_side, 2, mid)
    own_rows = piece_side // 2
    sides_mine = lax.dynamic_slice_in_dim(sides_grad, core * own_rows, own_rows, axis=1)
    sides_from = swap(
        lax.dynamic_slice_in_dim(sides_grad, (1 - core) * own_rows, own_rows, axis=1)
    )
    message_grad = jnp.stack(
        [
            jnp.where(core == 0, sides_from[:, :, 0], sides_mine[:, :, 0]),
            jnp.where(core == 0, sides_mine[:, :, 0], sides_from[:, :, 0]),
        ]
    )
    gate_grad = jnp.stack(
        [
            jnp.where(core == 0, sides_mine[:, :, 1], sides_from[:, :, 1]),
            jnp.where(core == 0, sides_from[:, :, 1], sides_mine[:, :, 1]),
        ]
    )
    return (
        depth_pred,
        seg_logits,
        features_grad,
        reduce_grad,
        dilated_grad,
        expand_grad,
        gain_reduce_grad,
        bias_reduce_grad,
        gain_dilated_grad,
        bias_dilated_grad,
        gain_expand_grad,
        bias_expand_grad,
        heads_grad,
        gain_heads_grad,
        bias_heads_grad,
        message_grad.astype(F32),
        gate_grad.astype(F32),
        class_grad[:, :classes],
        class_grad[:, classes],
    )


def solution(mesh):
    img, row = mesh.shape["img"], mesh.shape["row"]
    side = row // 2
    fine = Mesh(mesh.devices.reshape(img // side, side, side, 2), ALL)
    crops, rows = ("z", "x"), ("y", "c")
    every = ALL
    placed = (
        P(crops, rows, None, None),
        P(every, None),
        P(None, every, None),
        P(every, None),
        P(),
        P(),
        P(),
        P(),
        P(),
        P(),
        P(None, every, None),
        P(),
        P(),
        P(None, None, every, None),
        P(None, None, every, None),
        P(every, None),
        P(every),
        P(crops, rows, None),
        P(crops, rows, None),
        P(crops, rows, None),
    )
    return jax.shard_map(
        per_device,
        mesh=fine,
        in_specs=placed,
        out_specs=(
            P(crops, rows, None),
            P(crops, rows, None, None),
            P(crops, rows, None, None),
            P(every, None),
            P(None, every, None),
            P(every, None),
            P(),
            P(),
            P(),
            P(),
            P(),
            P(),
            P(None, every, None),
            P(),
            P(),
            P(None, None, every, None),
            P(None, None, every, None),
            P(every, None),
            P(every),
        ),
        check_vma=False,
    )
```

```python
import functools
import itertools

import jax
import jax.numpy as jnp
from jax import lax
from jax.experimental import pallas as pl
from jax.experimental.pallas import tpu as pltpu
from jax.sharding import Mesh
from jax.sharding import PartitionSpec as P

EPS = 1e-05
ALL = ("z", "x", "y", "c")
CHIPS = ("z", "x", "y")
PLANE = ("x", "y")
ROWS = ("y", "c")
BF, F32 = jnp.bfloat16, jnp.float32
MESH = pl.DeviceIdType.MESH
VMEM_BYTES = 60 * 1024 * 1024


def flat_index(axes, sizes):
    index = 0
    for a, n in zip(axes, sizes):
        index = index * n + lax.axis_index(a)
    return index


def coordinates(axes, sizes, index):
    place = {}
    for a, n in reversed(list(zip(axes, sizes))):
        place[a] = lax.rem(index, n)
        index = index // n
    return place


def small_sum_kernel(stages, kind, count, v_ref, o_ref, *scratch):
    slots, send_sem, recv_sem = scratch[: len(stages)], scratch[-2], scratch[-1]
    barrier = pltpu.get_barrier_semaphore()
    peers = 0
    for axes, sizes in stages:
        me, n = flat_index(axes, sizes), total(sizes)
        for s in range(1, n):
            pl.semaphore_signal(
                barrier,
                inc=1,
                device_id=coordinates(axes, sizes, lax.rem(me + s, n)),
                device_id_type=MESH,
            )
            peers += 1
    pl.semaphore_wait(barrier, peers)
    current = v_ref[...]
    which = 0
    for slot, (axes, sizes) in zip(slots, stages):
        me, n = flat_index(axes, sizes), total(sizes)
        slot[me] = current
        copies = []
        for s in range(1, n):
            copy = pltpu.make_async_remote_copy(
                src_ref=slot.at[me],
                dst_ref=slot.at[me],
                send_sem=send_sem.at[which],
                recv_sem=recv_sem.at[which],
                device_id=coordinates(axes, sizes, lax.rem(me + s, n)),
                device_id_type=MESH,
            )
            copy.start()
            copies.append(copy)
            which += 1
        for copy in copies:
            copy.wait()
        first, second = slot[0, 0], slot[0, 1]
        for s in range(1, n):
            first = first + slot[s, 0]
            second = second + slot[s, 1]
        if kind == "moments":
            mean = first / n
            for s in range(n):
                second = second + count * jnp.square(slot[s, 0] - mean)
            first = mean
            count = count * n
        current = jnp.stack([first, second])
    o_ref[...] = current


def total(sizes):
    n = 1
    for size in sizes:
        n *= size
    return n


def small_sum(pair, axes, kind, count, collective):
    channels = pair[0].shape[0]
    stages = tuple(
        (group, tuple(lax.axis_size(a) for a in group)) for group in (axes[1:], axes[:1])
    )
    shape = (2, channels // 128, 128)
    n_copies = sum(total(sizes) - 1 for _, sizes in stages)
    out = pl.pallas_call(
        functools.partial(small_sum_kernel, stages, kind, float(count)),
        out_shape=jax.ShapeDtypeStruct(shape, F32),
        in_specs=[pl.BlockSpec(memory_space=pltpu.VMEM)],
        out_specs=pl.BlockSpec(memory_space=pltpu.VMEM),
        scratch_shapes=[pltpu.VMEM((total(sizes),) + shape, F32) for _, sizes in stages]
        + [pltpu.SemaphoreType.DMA((n_copies,)), pltpu.SemaphoreType.DMA((n_copies,))],
        compiler_params=pltpu.CompilerParams(collective_id=collective, has_side_effects=True),
        cost_estimate=pl.CostEstimate(flops=0, bytes_accessed=30_000_000, transcendentals=0),
    )(jnp.stack(pair).reshape(shape))
    return out[0].reshape(channels), out[1].reshape(channels)


def gather_kernel(geometry, both_cores, parts, *refs):
    n_z, n_x, n_y = geometry
    many = len(parts)
    arrays = (len(refs) - 3) // 2
    ins, outs = refs[:arrays], refs[arrays : 2 * arrays]
    own_sem, send_sem, recv_sem = refs[2 * arrays :]
    z, x, y, core = (lax.axis_index(a) for a in ALL)
    sizes = {"z": n_z, "x": n_x, "y": n_y, "c": 2}
    here = {"z": z, "x": x, "y": y, "c": core}
    used = ("z", "x", "y", "c") if both_cores else ("z", "x", "y")

    def peer(axis, s):
        return {axis: lax.rem(here[axis] + s, sizes[axis])}

    barrier = pltpu.get_barrier_semaphore()
    peers = 0
    for axis in used:
        for s in range(1, sizes[axis]):
            pl.semaphore_signal(barrier, inc=1, device_id=peer(axis, s), device_id_type=MESH)
            peers += 1
    pl.semaphore_wait(barrier, peers)

    def back(axis, s):
        return lax.rem(here[axis] + sizes[axis] - s, sizes[axis])

    def view(p, place):
        array, lead, dim, rows, _ = parts[p]
        index = (back("z", place[0]) * n_x + back("x", place[1])) * n_y + back("y", place[2])
        if both_cores:
            index = index * 2 + core
        span = pl.ds(pl.multiple_of(index * rows, rows), rows)
        if dim == 0:
            return outs[array].at[span]
        return outs[array].at[pl.ds(*lead), span] if lead else outs[array].at[:, span]

    def given(p):
        array, lead = parts[p][:2]
        return ins[array].at[pl.ds(*lead)] if lead else ins[array]

    started = []

    def send(p, place, axis, s):
        source = given(p) if place == (0, 0, 0) else view(p, place)
        which = len(started)
        copy = pltpu.make_async_remote_copy(
            src_ref=source,
            dst_ref=view(p, place),
            send_sem=send_sem.at[which],
            recv_sem=recv_sem.at[which],
            device_id=peer(axis, s),
            device_id_type=MESH,
        )
        copy.start()
        started.append(copy)
        return copy

    last = []

    def to_core(p, place):
        if both_cores:
            last.append(send(p, place, "c", 1))

    own = []
    along_z = {}
    for s in range(1, n_z):
        for p in range(many):
            along_z[s, p] = send(p, (0, 0, 0), "z", s)
    second, third = {}, {}

    def spread(p, zs):
        first_axis, second_axis = ("x", "y") if parts[p][4] == 1 else ("y", "x")
        for s in range(1, sizes[first_axis]):
            second[p, zs, s] = send(p, (zs, 0, 0), first_axis, s)
        for s in range(1, sizes[second_axis]):
            third[p, zs, 0, s] = send(p, (zs, 0, 0), second_axis, s)
        to_core(p, (zs, 0, 0))

    def place_of(p, zs, a, b):
        return (zs, a, b) if parts[p][4] == 1 else (zs, b, a)

    for p in range(many):
        spread(p, 0)
    for p in range(many):
        copy = pltpu.make_async_copy(given(p), view(p, (0, 0, 0)), own_sem.at[p])
        copy.start()
        own.append(copy)
    for zs in range(1, n_z):
        for p in range(many):
            along_z[zs, p].wait_recv()
            spread(p, zs)
    for zs in range(n_z):
        for p in range(many):
            first_axis, second_axis = ("x", "y") if parts[p][4] == 1 else ("y", "x")
            for a in range(1, sizes[first_axis]):
                second[p, zs, a].wait_recv()
                for s in range(1, sizes[second_axis]):
                    third[p, zs, a, s] = send(p, place_of(p, zs, a, 0), second_axis, s)
                to_core(p, place_of(p, zs, a, 0))
    for zs in range(n_z):
        for p in range(many):
            first_axis, second_axis = ("x", "y") if parts[p][4] == 1 else ("y", "x")
            for b in range(1, sizes[second_axis]):
                for a in range(sizes[first_axis]):
                    third[p, zs, a, b].wait_recv()
                    to_core(p, place_of(p, zs, a, b))
    for copy in last:
        copy.wait_recv()
    for copy in own:
        copy.wait()
    for copy in started:
        copy.wait_send()


def gather_pieces(arrays, parts, both_cores, collective, microseconds):
    geometry = tuple(lax.axis_size(a) for a in CHIPS)
    chips = total(geometry)
    many = len(parts)
    cut_at = {part[0]: part[2] for part in parts}
    shapes = []
    for i, array in enumerate(arrays):
        shape = list(array.shape)
        shape[cut_at[i]] *= chips * (2 if both_cores else 1)
        shapes.append(jax.ShapeDtypeStruct(tuple(shape), array.dtype))
    n_copies = many * (chips - 1 + (chips if both_cores else 0))
    return pl.pallas_call(
        functools.partial(gather_kernel, geometry, both_cores, parts),
        out_shape=shapes,
        in_specs=[pl.BlockSpec(memory_space=pl.ANY)] * len(arrays),
        out_specs=[pl.BlockSpec(memory_space=pl.ANY)] * len(arrays),
        scratch_shapes=[
            pltpu.SemaphoreType.DMA((many,)),
            pltpu.SemaphoreType.DMA((n_copies,)),
            pltpu.SemaphoreType.DMA((n_copies,)),
        ],
        compiler_params=pltpu.CompilerParams(collective_id=collective, has_side_effects=True),
        cost_estimate=pl.CostEstimate(
            flops=0, bytes_accessed=int(3.5e6 * microseconds), transcendentals=0
        ),
    )(*arrays)


def scatter_kernel(sizes, orders, layouts, window, *refs):
    many = len(orders)
    depth = max(len(order) for order in orders)
    ins, outs = refs[:many], refs[many : 2 * many]
    own = refs[2 * many : 3 * many]
    landed = [refs[(3 + i) * many : (4 + i) * many] for i in range(depth)]
    own_sem, send_sem, recv_sem = refs[-3:]
    here = {a: lax.axis_index(a) for a in sizes}

    def forth(axis, s):
        return lax.rem(here[axis] + s, sizes[axis])

    barrier = pltpu.get_barrier_semaphore()
    peers = 0
    for axis in sizes:
        for s in range(1, sizes[axis]):
            pl.semaphore_signal(
                barrier, inc=1, device_id={axis: forth(axis, s)}, device_id_type=MESH
            )
            peers += 1
    pl.semaphore_wait(barrier, peers)

    started = []

    def send(source, target, axis, s):
        which = len(started)
        copy = pltpu.make_async_remote_copy(
            src_ref=source,
            dst_ref=target,
            send_sem=send_sem.at[which],
            recv_sem=recv_sem.at[which],
            device_id={axis: forth(axis, s)},
            device_id_type=MESH,
        )
        copy.start()
        started.append(copy)
        return copy

    places = []
    for order in orders:
        steps = [list(range(1, sizes[a])) + [0] for a in order[1:]]
        places.append(list(itertools.product(*steps)))

    def block(p, steps):
        index = 0
        at = dict(zip(orders[p], steps))
        for axis in layouts[p]:
            index = index * sizes[axis] + forth(axis, at[axis])
        return index

    def slot(p, stage, steps):
        index = 0
        for axis, s in zip(orders[p][stage + 1 :], steps):
            index = index * sizes[axis] + s
        return index

    loads, copies = {}, {}
    for p in range(many):
        for k, place in enumerate(places[p]):
            copy = pltpu.make_async_copy(
                ins[p].at[block(p, (0,) + place)], own[p].at[k], own_sem.at[len(loads)]
            )
            copy.start()
            loads[p, k] = copy

    def send_first(k):
        for p in range(many):
            if k < len(places[p]):
                place = places[p][k]
                for s in range(1, sizes[orders[p][0]]):
                    copies[p, 0, s, place] = send(
                        ins[p].at[block(p, (s,) + place)],
                        landed[0][p].at[s - 1, slot(p, 0, place)],
                        orders[p][0],
                        s,
                    )

    waited = set()
    longest = max(len(each) for each in places)
    for k in range(min(window, longest)):
        send_first(k)
    for k in range(longest):
        for p in range(many):
            own_k = k - (longest - len(places[p]))
            if own_k < 0:
                continue
            order, place = orders[p], places[p][own_k]
            loads[p, own_k].wait()
            terms, onward = [], None
            for stage, axis in enumerate(order):
                later = place[stage:]
                if stage > 0 and place[stage - 1] > 0:
                    onward = (stage, axis, place[stage - 1], later)
                    break
                for s in range(1, sizes[axis]):
                    copies[p, stage, s, later].wait_recv()
                    terms.append((landed[stage][p], (s - 1, slot(p, stage, later))))

            def add(t, carry, p=p, k=own_k, terms=terms, final=onward is None):
                value = own[p][k, t].astype(F32)
                for ref, index in terms:
                    value = value + ref[(*index, t)].astype(F32)
                if final:
                    outs[p][t] = value
                else:
                    own[p][k, t] = value.astype(BF)
                return carry

            lax.fori_loop(0, own[p].shape[1], add, 0)
            if onward:
                stage, axis, s, later = onward
                copies[p, stage, s, later] = send(
                    own[p].at[own_k], landed[stage][p].at[s - 1, slot(p, stage, later)], axis, s
                )
        if k + window < longest:
            for p in range(many):
                if k < len(places[p]):
                    for s in range(1, sizes[orders[p][0]]):
                        copy = copies[p, 0, s, places[p][k]]
                        copy.wait_send()
                        waited.add(id(copy))
            send_first(k + window)
    for copy in started:
        if id(copy) not in waited:
            copy.wait_send()


def scatter_blocks(arrays, orders, layouts, window, collective):
    sizes = {a: lax.axis_size(a) for a in ALL}
    depth = max(len(order) for order in orders)
    own, landed = [], [[] for _ in range(depth)]
    loads = copies = 0
    for array, order in zip(arrays, orders):
        shape = array.shape[1:]
        own.append(pltpu.VMEM((total(sizes[a] for a in order[1:]),) + shape, BF))
        loads += total(sizes[a] for a in order[1:])
        for stage in range(depth):
            if stage < len(order):
                peers, later = sizes[order[stage]] - 1, total(sizes[a] for a in order[stage + 1 :])
                landed[stage].append(pltpu.VMEM((peers, later) + shape, BF))
                copies += peers * later
            else:
                landed[stage].append(pltpu.VMEM((1, 1, 16, 128), BF))
    return pl.pallas_call(
        functools.partial(scatter_kernel, sizes, orders, layouts, window),
        out_shape=[jax.ShapeDtypeStruct(a.shape[1:], F32) for a in arrays],
        in_specs=[pl.BlockSpec(memory_space=pl.ANY)] * len(arrays),
        out_specs=[pl.BlockSpec(memory_space=pltpu.VMEM)] * len(arrays),
        scratch_shapes=own
        + sum(landed, [])
        + [
            pltpu.SemaphoreType.DMA((loads,)),
            pltpu.SemaphoreType.DMA((copies,)),
            pltpu.SemaphoreType.DMA((copies,)),
        ],
        compiler_params=pltpu.CompilerParams(
            collective_id=collective, has_side_effects=True, vmem_limit_bytes=VMEM_BYTES
        ),
        cost_estimate=pl.CostEstimate(flops=0, bytes_accessed=250_000_000, transcendentals=0),
    )(*arrays)


def combine_cols(before, same, after, col, spread):
    n = same.shape[0]
    before = jnp.where(col < spread, 0.0, pltpu.roll(before, spread, 0))
    after = jnp.where(col >= n - spread, 0.0, pltpu.roll(after, n - spread, 0))
    return before + same + after


def conv_fwd(xpad, weights, chosen, spread, kc, nc, n_blocks, n_first, moments, out_dtype):
    batch, height_pad, width, depth = xpad.shape
    height, wide = height_pad - 2 * spread, n_blocks * nc
    px = batch * height * width
    steps = depth // kc

    def body(first_ref, x_ref, *rest):
        taps = [ref.at[t] for ref, w in zip(rest, weights) for t in range(w.shape[0])]
        rest = rest[len(weights) :]
        o_ref, acc = rest[0], rest[-1]
        k = pl.program_id(1)

        def dots(first):
            for b in range(3):
                for a in range(3):
                    xa = x_ref[:, a * spread : a * spread + height].reshape(px, kc)
                    d = jnp.dot(xa, taps[3 * a + b][...], preferred_element_type=F32)
                    if first and a == 0:
                        acc[b] = d
                    else:
                        acc[b] += d

        @pl.when(k == 0)
        def _():
            dots(True)

        @pl.when(k > 0)
        def _():
            dots(False)

        @pl.when(k == steps - 1)
        def _():
            col = lax.broadcasted_iota(jnp.int32, (width, nc), 0)

            def store(i, running):
                r = pl.ds(pl.multiple_of(i * width, width), width)
                v = combine_cols(acc[0, r], acc[1, r], acc[2, r], col, spread)
                o_ref[r] = v.astype(out_dtype)
                return running + jnp.sum(v.reshape(width // 8, 8, nc), axis=0) if moments else 0

            start = jnp.zeros((8, nc), F32)
            running = lax.fori_loop(0, batch * height, store, start if moments else 0)
            if moments:
                mean = jnp.sum(running, axis=0, keepdims=True) / px

                def deviation(i, so_far):
                    r = pl.ds(pl.multiple_of(i * width, width), width)
                    v = jnp.square(o_ref[r] - mean)
                    return so_far + jnp.sum(v.reshape(width // 8, 8, nc), axis=0)

                m2 = lax.fori_loop(0, batch * height, deviation, start)
                row = lax.broadcasted_iota(jnp.int32, (8, nc), 0)
                rest[1][...] = jnp.where(row == 0, mean, jnp.sum(m2, axis=0, keepdims=True))

    out_specs = [pl.BlockSpec((px, nc), lambda n, k, f: (0, n))]
    out_shape = [jax.ShapeDtypeStruct((px, wide), out_dtype)]
    if moments:
        out_specs.append(pl.BlockSpec((8, nc), lambda n, k, f: (0, n)))
        out_shape.append(jax.ShapeDtypeStruct((8, wide), F32))
    return pl.pallas_call(
        body,
        grid_spec=pltpu.PrefetchScalarGridSpec(
            num_scalar_prefetch=1,
            grid=(n_blocks, steps),
            in_specs=[
                pl.BlockSpec((batch, height_pad, width, kc), lambda n, k, f: (0, 0, 0, k)),
                *(
                    pl.BlockSpec(
                        (w.shape[0], kc, nc), lambda n, k, f, c=c: (0, k, n + f[0] if c else n)
                    )
                    for w, c in zip(weights, chosen)
                ),
            ],
            out_specs=out_specs,
            scratch_shapes=[pltpu.VMEM((3, px, nc), F32)],
        ),
        out_shape=out_shape,
        compiler_params=pltpu.CompilerParams(vmem_limit_bytes=VMEM_BYTES),
        cost_estimate=pl.CostEstimate(
            flops=18 * px * depth * wide,
            bytes_accessed=18 * depth * wide + 2 * px * depth + 4 * px * wide,
            transcendentals=0,
        ),
    )(n_first, xpad, *weights)


def conv_dgrad(gpads, weights, chosen, spread, cc, c_range, n_first, out_dtype, by_core=False):
    batch, height_pad, width, wide = gpads[0].shape
    many, arrays = len(gpads), [w for group in weights for w in group]
    height, depth = height_pad - 2 * spread, len(c_range) * cc
    c_first = c_range[0]
    px = batch * height * width
    dims = (((1,), (1,)), ((), ()))
    results = 2 if by_core else 1
    lines = height // results

    def body(first_ref, *refs):
        gs, outs, acc = refs[:many], refs[many + len(arrays) : -1], refs[-1]
        taps = [
            ref.at[t]
            for ref, w in zip(refs[many : many + len(arrays)], arrays)
            for t in range(w.shape[0])
        ]
        for q in range(many):
            for b in range(3):
                for a in range(3):
                    top = (2 - a) * spread
                    ga = gs[q][:, top : top + height].reshape(px, wide)
                    d = lax.dot_general(
                        ga, taps[9 * q + 3 * a + b][...], dims, preferred_element_type=F32
                    )
                    if q == 0 and a == 0:
                        acc[2 - b] = d
                    else:
                        acc[2 - b] += d
        col = lax.broadcasted_iota(jnp.int32, (width, cc), 0)

        for which, o_ref in enumerate(outs):

            def store(i, carry, which=which, o_ref=o_ref):
                line = i
                if by_core:
                    part = first_ref[0] if which == 0 else 1 - first_ref[0]
                    line = i // lines * height + part * lines + lax.rem(i, lines)
                r = pl.ds(pl.multiple_of(line * width, width), width)
                value = combine_cols(acc[0, r], acc[1, r], acc[2, r], col, spread)
                o_ref[pl.ds(pl.multiple_of(i * width, width), width)] = value.astype(out_dtype)
                return carry

            lax.fori_loop(0, batch * lines, store, 0)

    return pl.pallas_call(
        body,
        grid_spec=pltpu.PrefetchScalarGridSpec(
            num_scalar_prefetch=1,
            grid=(depth // cc,),
            in_specs=[pl.BlockSpec((batch, height_pad, width, wide), lambda c, f: (0, 0, 0, 0))]
            * many
            + [
                pl.BlockSpec(
                    (w.shape[0], cc, wide),
                    lambda c, f, pick=pick: (0, c + c_first, f[0] if pick else 0),
                )
                for w, pick in zip(arrays, chosen)
            ],
            out_specs=[pl.BlockSpec((px // results, cc), lambda c, f: (0, c))] * results,
            scratch_shapes=[pltpu.VMEM((3, px, cc), F32)],
        ),
        out_shape=[jax.ShapeDtypeStruct((px // results, depth), out_dtype)] * results,
        compiler_params=pltpu.CompilerParams(vmem_limit_bytes=VMEM_BYTES),
        cost_estimate=pl.CostEstimate(
            flops=18 * many * px * depth * wide,
            bytes_accessed=18 * many * depth * wide + 4 * px * depth,
            transcendentals=0,
        ),
    )(n_first, *gpads, *arrays)


def conv_wgrad(xpad, grad, spread, cc, nc, piece, plane, shares):
    batch, height_pad, width, depth = xpad.shape
    height, wide = height_pad - 2 * spread, grad.shape[1]
    px = batch * height * width
    each, blocks = cc // piece, wide // nc
    lines = 128 // width

    def body(x_ref, g_ref, *rest):
        outs, shifted = rest[:-1], rest[-1]

        @pl.when(pl.program_id(1) == 0)
        def _():
            col = lax.broadcasted_iota(jnp.int32, (width, nc), 0)

            def turn(i, carry):
                r = pl.ds(pl.multiple_of(i * 128, 128), 128)
                block = g_ref[r].astype(F32)
                for b in range(3):
                    moved = []
                    for j in range(lines):
                        v = block[j * width : (j + 1) * width]
                        if b == 0:
                            v = jnp.where(
                                col >= width - spread, 0.0, pltpu.roll(v, width - spread, 0)
                            )
                        elif b == 2:
                            v = jnp.where(col < spread, 0.0, pltpu.roll(v, spread, 0))
                        moved.append(v)
                    shifted[b, :, r] = jnp.concatenate(moved, axis=0).T.astype(BF)
                return carry

            lax.fori_loop(0, px // 128, turn, 0)

        for a in range(3):
            xa = x_ref[:, a * spread : a * spread + height].reshape(px, cc)
            for b in range(3):
                d = jnp.dot(shifted[b], xa, preferred_element_type=F32).T.astype(BF)
                for out, (taps, low, high) in zip(outs, shares):
                    if 3 * a + b in taps:
                        for j in range(each):
                            out[j % plane, j // plane, taps.index(3 * a + b)] = d[
                                j * piece : (j + 1) * piece, low:high
                            ]

    return pl.pallas_call(
        body,
        grid=(blocks, depth // cc),
        in_specs=[
            pl.BlockSpec((batch, height_pad, width, cc), lambda n, c: (0, 0, 0, c)),
            pl.BlockSpec((px, nc), lambda n, c: (0, n)),
        ],
        out_specs=[
            pl.BlockSpec(
                (plane, each // plane, len(taps), piece, high - low), lambda n, c: (0, c, 0, 0, n)
            )
            for taps, low, high in shares
        ],
        out_shape=[
            jax.ShapeDtypeStruct(
                (plane, depth // (plane * piece), len(taps), piece, blocks * (high - low)), BF
            )
            for taps, low, high in shares
        ],
        scratch_shapes=[pltpu.VMEM((3, nc, px), BF)],
        compiler_params=pltpu.CompilerParams(vmem_limit_bytes=VMEM_BYTES),
        cost_estimate=pl.CostEstimate(
            flops=18 * px * depth * wide,
            bytes_accessed=18 * depth * wide + 2 * px * depth,
            transcendentals=0,
        ),
    )(xpad, grad)


def outer_sum(left, right, cc, turned):
    px, wide = left.shape
    deep = right.shape[1]

    def body(l_ref, r_ref, o_ref, flipped):
        @pl.when(pl.program_id(0) == 0)
        def _():
            def turn(i, carry):
                r = pl.ds(pl.multiple_of(i * 128, 128), 128)
                flipped[:, r] = l_ref[r].astype(F32).T.astype(BF)
                return carry

            lax.fori_loop(0, px // 128, turn, 0)

        d = jnp.dot(flipped[...], r_ref[...], preferred_element_type=F32)
        o_ref[...] = (d.T if turned else d).astype(BF)

    return pl.pallas_call(
        body,
        grid=(deep // cc,),
        in_specs=[
            pl.BlockSpec((px, wide), lambda c: (0, 0)),
            pl.BlockSpec((px, cc), lambda c: (0, c)),
        ],
        out_specs=pl.BlockSpec((cc, wide), lambda c: (c, 0))
        if turned
        else pl.BlockSpec((wide, cc), lambda c: (0, c)),
        out_shape=jax.ShapeDtypeStruct((deep, wide) if turned else (wide, deep), BF),
        scratch_shapes=[pltpu.VMEM((wide, px), BF)],
        compiler_params=pltpu.CompilerParams(vmem_limit_bytes=VMEM_BYTES),
        cost_estimate=pl.CostEstimate(
            flops=2 * px * deep * wide,
            bytes_accessed=2 * (deep * wide + px * (deep + wide)),
            transcendentals=0,
        ),
    )(left, right)


def swap(value):
    return lax.ppermute(value, "c", [(0, 1), (1, 0)])


def in_order(mine, other, dim):
    first = lax.axis_index("c") == 0
    return jnp.concatenate(
        [jnp.where(first, mine, other), jnp.where(first, other, mine)], axis=dim
    )


def rims(block, axes, width):
    count = 1
    for a in axes:
        count *= lax.axis_size(a)
    forward = [(i, i + 1) for i in range(count - 1)]
    backward = [(t, s) for s, t in forward]
    low = lax.ppermute(block[:, block.shape[1] - width :], axes, forward)
    high = lax.ppermute(block[:, :width], axes, backward)
    return low, high


def with_rims(block, axes, width):
    low, high = rims(block, axes, width)
    return jnp.concatenate([low, block, high], axis=1)


def local_moments(value):
    mean = jnp.mean(value, axis=(0, 1, 2))
    return mean, jnp.sum(jnp.square(value - mean), axis=(0, 1, 2))


def gelu_back(inner, upstream):
    return jax.vjp(jax.nn.gelu, inner)[1](upstream)[0]


def gather(value, axes, dim):
    return lax.all_gather(value, axes, axis=dim, tiled=True)


def scatter_sum(value, axes, dim):
    return lax.psum_scatter(value, axes, scatter_dimension=dim, tiled=True)


def per_device(
    features,
    w_reduce,
    w_dilated,
    w_expand,
    gain_reduce,
    bias_reduce,
    gain_dilated,
    bias_dilated,
    gain_expand,
    bias_expand,
    w_heads,
    gain_heads,
    bias_heads,
    w_message,
    w_gate,
    w_seg,
    w_depth,
    labels,
    depth_target,
    depth_mask,
):
    core = lax.axis_index("c")
    chips = lax.axis_size("z") * lax.axis_size("x") * lax.axis_size("y")
    devices = chips * 2
    crops, height, width, deep = features.shape
    mid = w_reduce.shape[1]
    classes = w_seg.shape[1]
    local_px = crops * height * width
    pixels = local_px * devices
    chip_px = local_px * 2

    tied = lax.optimization_barrier
    r_rows, d_rows = w_reduce.shape[0], w_dilated.shape[1]
    last_chip = in_order(
        lax.dynamic_slice_in_dim(w_heads[7:], core * mid, mid, axis=2),
        swap(lax.dynamic_slice_in_dim(w_heads[7:], (1 - core) * mid, mid, axis=2)),
        1,
    )
    heads_most = gather(w_heads[:7], ALL, 1)
    sides_own = jnp.stack([w_message[1 - core], w_gate[core]])
    sides_other = jnp.stack([w_message[core], w_gate[1 - core]])
    sides_full = gather(in_order(sides_own, swap(sides_other), 2), CHIPS, 2)
    quarters = deep // mid
    small = jnp.concatenate([w_seg, w_depth[:, None]], axis=1)
    small = jnp.pad(small, ((0, 0), (0, mid - classes - 1)))
    side_blocks = jnp.stack(
        [w_expand[:, q * mid : (q + 1) * mid] for q in range(quarters)] + [small]
    )
    reduce_full, dilated_full, blocks_full = gather_pieces(
        (w_reduce, w_dilated, side_blocks),
        ((0, None, 0, r_rows, 2), (1, None, 1, d_rows, 1), (2, None, 1, d_rows, 2)),
        True,
        8,
        40,
    )
    expand_full = blocks_full[:quarters]
    class_full = blocks_full[quarters, :, :128]
    none = jnp.zeros((1,), jnp.int32)
    own_half = core.astype(jnp.int32).reshape(1)

    first_raw = jnp.einsum("bhwc,co->bhwo", features, reduce_full, preferred_element_type=F32)

    def norm(raw_moments, axes, count, collective):
        mean, m2 = small_sum(raw_moments, axes, "moments", count, collective)
        return mean, lax.rsqrt(m2 / pixels + EPS)

    stats_one = norm(local_moments(first_raw), ALL, local_px, 0)
    scaled_one = (first_raw - stats_one[0]) * stats_one[1]
    inner_one = scaled_one * gain_reduce + bias_reduce
    hidden_one = jax.nn.gelu(inner_one).astype(BF)
    padded_one = with_rims(hidden_one, ROWS, 2)

    second_raw, second_moments = conv_fwd(
        padded_one, (dilated_full,), (False,), 2, 256, mid, 1, none, True, F32
    )
    second_raw = second_raw.reshape(crops, height, width, mid)
    stats_two = norm((second_moments[0], second_moments[1]), ALL, local_px, 1)
    scaled_two = (second_raw - stats_two[0]) * stats_two[1]
    inner_two = scaled_two * gain_dilated + bias_dilated
    hidden_two = jax.nn.gelu(inner_two).astype(BF)
    third_raw = jnp.einsum(
        "bhwc,qco->bhwqo", hidden_two, expand_full, preferred_element_type=F32
    ).reshape(crops, height, width, deep)
    stats_three = norm(local_moments(third_raw), ALL, local_px, 2)
    scaled_three = (third_raw - stats_three[0]) * stats_three[1]
    inner_three = scaled_three * gain_expand + bias_expand + features.astype(F32)
    output = jax.nn.gelu(inner_three).astype(BF)

    low, high = rims(output, ROWS, 1)
    outer = jnp.where(core == 0, low, high)
    outer_other = swap(outer)
    output_other = swap(output)
    output_pad = jnp.concatenate(
        [
            jnp.where(core == 0, low, outer_other),
            in_order(output, output_other, 1),
            jnp.where(core == 0, outer_other, high),
        ],
        axis=1,
    )
    tall = 2 * height
    last_chip, output_pad = tied((last_chip, output_pad))
    last_rows = last_chip.shape[1]
    (heads_last,) = gather_pieces(
        (last_chip,), ((0, (0, 1), 1, last_rows, 1), (0, (1, 1), 1, last_rows, 2)), False, 9, 45
    )
    heads_last, output_pad = tied((heads_last, output_pad))
    heads_full = (heads_most, heads_last)
    heads_raw, heads_moments = conv_fwd(
        output_pad, heads_full, (True, False), 1, 512, mid, 1, own_half, True, F32
    )
    stats_heads = norm((heads_moments[0], heads_moments[1]), CHIPS, chip_px, 3)
    gain_own = lax.dynamic_slice_in_dim(gain_heads, core * mid, mid)
    bias_own = lax.dynamic_slice_in_dim(bias_heads, core * mid, mid)
    scaled_heads = (heads_raw - stats_heads[0]) * stats_heads[1]
    inner_heads = scaled_heads * gain_own + bias_own
    feature = jax.nn.gelu(inner_heads).astype(BF)
    feature_pad = with_rims(feature.reshape(crops, tall, width, mid), ("y",), 1)

    message_full, gate_full = sides_full[0], sides_full[1]
    (give,) = conv_fwd(
        feature_pad, (message_full,), (False,), 1, 256, mid, 1, none, False, BF
    )
    (gate,) = conv_fwd(feature_pad, (gate_full,), (False,), 1, 256, mid, 1, none, False, F32)
    message = swap(give).astype(F32)
    sigma = jax.nn.sigmoid(gate)
    stream = (feature.astype(F32) + sigma * message).astype(BF)
    scores = jnp.dot(stream, class_full, preferred_element_type=F32)
    own_side = jnp.stack(
        [labels.astype(F32), depth_target, depth_mask.astype(F32)]
    )
    labels_chip, target_chip, mask_chip = in_order(own_side, swap(own_side), 2).reshape(3, chip_px)
    seg_scores = scores[:, :classes]
    log_total = jax.nn.logsumexp(seg_scores, axis=-1, keepdims=True)
    class_ids = jnp.arange(classes, dtype=jnp.int32)
    seg_back = jnp.exp(seg_scores - log_total) - (
        labels_chip.astype(jnp.int32)[:, None] == class_ids
    ).astype(F32)
    depth_scores = scores[:, classes]
    differ = depth_scores - target_chip
    depth_back = mask_chip * differ * lax.rsqrt(differ * differ + 1.0)
    score_back = jnp.concatenate(
        [
            jnp.where(core == 1, seg_back, 0.0),
            jnp.where(core == 0, depth_back, 0.0)[:, None],
            jnp.zeros((chip_px, 128 - classes - 1), F32),
        ],
        axis=1,
    ).astype(BF)
    class_grad = lax.dot_general(
        stream, score_back, (((0,), (0,)), ((), ())), preferred_element_type=F32
    )
    stream_grad = lax.dot_general(
        score_back, class_full, (((1,), (1,)), ((), ())), preferred_element_type=F32
    )

    scores_map = scores[:, : classes + 1].reshape(crops, tall, width, classes + 1)
    for_own = lax.dynamic_slice_in_dim(scores_map, core * height, height, axis=1)
    for_other = lax.dynamic_slice_in_dim(scores_map, (1 - core) * height, height, axis=1)
    from_other = swap(for_other)
    depth_pred = jnp.where(core == 0, for_own[..., classes], from_other[..., classes])
    seg_logits = jnp.where(core == 0, from_other[..., :classes], for_own[..., :classes])

    give_grad_other = (stream_grad * sigma).astype(BF)
    gate_grad_low = (stream_grad * message * sigma * (1.0 - sigma)).astype(BF)
    give_grad_low = swap(give_grad_other)
    piece_side = mid // chips
    plane = lax.axis_size("x") * lax.axis_size("y")
    tall_shape = (crops, tall, width, mid)
    give_pad, gate_pad = (
        with_rims(g.reshape(tall_shape), ("y",), 1) for g in (give_grad_low, gate_grad_low)
    )
    every_tap = tuple(range(9))
    (sides_grad,) = conv_wgrad(
        feature_pad,
        jnp.concatenate([give_grad_low, gate_grad_low], axis=1),
        1,
        mid,
        mid,
        piece_side,
        plane,
        ((every_tap, 0, mid),),
    )
    sides_grad, give_pad, gate_pad = tied((sides_grad, give_pad, gate_pad))
    sides_grad = scatter_sum(sides_grad.reshape(-1, 2 * mid), PLANE, 0)
    (feature_back,) = conv_dgrad(
        [give_pad, gate_pad],
        [(message_full,), (gate_full,)],
        (False, False),
        1,
        256,
        range(mid // 256),
        none,
        F32,
    )
    feature_grad = stream_grad + feature_back

    def norm_back(upstream, scaled, inverse, gain, axes, collective):
        dims = tuple(range(upstream.ndim - 1))
        bias_grad, gain_grad = small_sum(
            (jnp.sum(upstream, axis=dims), jnp.sum(upstream * scaled, axis=dims)),
            axes,
            "sums",
            1,
            collective,
        )
        grad = gain * inverse * (upstream - bias_grad / pixels - scaled * (gain_grad / pixels))
        return grad, gain_grad, bias_grad

    heads_raw_grad, gain_heads_own, bias_heads_own = norm_back(
        gelu_back(inner_heads, feature_grad), scaled_heads, stats_heads[1], gain_own, CHIPS, 4
    )
    heads_pair = jnp.stack([gain_heads_own, bias_heads_own])
    gain_heads_grad, bias_heads_grad = in_order(heads_pair, swap(heads_pair), 1)
    heads_low = heads_raw_grad.astype(BF)
    heads_pad = with_rims(heads_low.reshape(tall_shape), ("y",), 1)
    most_taps, last_tap = every_tap[:8], every_tap[8:]
    heads_first, heads_yx, heads_xy = conv_wgrad(
        output_pad,
        heads_low,
        1,
        512,
        mid,
        deep // chips,
        plane,
        ((most_taps, 0, mid), (last_tap, 0, mid // 2), (last_tap, mid // 2, mid)),
    )
    heads_first, heads_yx, heads_xy, heads_pad = tied((heads_first, heads_yx, heads_xy, heads_pad))
    heads_first = scatter_sum(heads_first.reshape(-1, mid), PLANE, 0)
    heads_yx, heads_xy = (v.reshape(chips, *v.shape[2:]) for v in (heads_yx, heads_xy))
    grad_own, grad_other = conv_dgrad(
        [heads_pad], [heads_full], (True, False), 1, 512, range(deep // 512), own_half, BF, True
    )
    output_grad = (grad_own.astype(F32) + swap(grad_other).astype(F32)).reshape(
        crops, height, width, deep
    )

    inner_three_grad = gelu_back(inner_three, output_grad)
    third_grad, gain_expand_grad, bias_expand_grad = norm_back(
        inner_three_grad, scaled_three, stats_three[1], gain_expand, ALL, 5
    )
    third_low = third_grad.astype(BF)
    expand_grad = outer_sum(hidden_two.reshape(-1, mid), third_low.reshape(-1, deep), 512, False)
    expand_grad = expand_grad.reshape(devices, 1, d_rows, deep)
    class_grad = class_grad.astype(BF).reshape(devices, 1, d_rows, 128)
    hidden_two_grad = jnp.einsum(
        "bhwqo,qco->bhwc",
        third_low.reshape(crops, height, width, quarters, mid),
        expand_full,
        preferred_element_type=F32,
    )
    second_grad, gain_dilated_grad, bias_dilated_grad = norm_back(
        gelu_back(inner_two, hidden_two_grad), scaled_two, stats_two[1], gain_dilated, ALL, 6
    )
    second_low = second_grad.astype(BF)
    second_pad = with_rims(second_low, ROWS, 2)
    second_pad, second_low, sides_grad, heads_first = tied(
        (second_pad, second_low, sides_grad, heads_first)
    )
    sides_grad = scatter_sum(sides_grad, "z", 0)
    heads_first = scatter_sum(heads_first, "z", 0)
    (dilated_grad,) = conv_wgrad(
        padded_one, second_low.reshape(-1, mid), 2, mid, mid, d_rows, 1, ((every_tap, 0, mid),)
    )
    (hidden_one_grad,) = conv_dgrad(
        [second_pad], [(dilated_full,)], (False,), 2, 256, range(mid // 256), none, F32
    )
    hidden_one_grad = hidden_one_grad.reshape(crops, height, width, mid)
    first_grad, gain_reduce_grad, bias_reduce_grad = norm_back(
        gelu_back(inner_one, hidden_one_grad), scaled_one, stats_one[1], gain_reduce, ALL, 7
    )
    first_low = first_grad.astype(BF)
    reduce_grad = outer_sum(first_low.reshape(-1, mid), features.reshape(-1, deep), 512, True)
    reduce_grad = reduce_grad.reshape(devices, 1, r_rows, mid)
    features_grad = inner_three_grad + jnp.einsum(
        "bhwo,co->bhwc", first_low, reduce_full, preferred_element_type=F32
    )

    dilated_grad = dilated_grad.reshape(devices, 9, d_rows, mid)
    features_grad, reduce_grad, sides_grad = tied((features_grad, reduce_grad, sides_grad))
    by_y, by_x = ("y", "x", "z"), ("x", "y", "z")
    heads_yx, heads_xy, dilated_grad, expand_grad, reduce_grad, class_grad = scatter_blocks(
        (heads_yx, heads_xy, dilated_grad, expand_grad, reduce_grad, class_grad),
        (by_y, by_x, ("c", *by_y), ("c", *by_x), ("c", *by_x), ("c", *by_x)),
        (by_x, by_x, ALL, ALL, ALL, ALL),
        4,
        10,
    )
    reduce_grad = reduce_grad[0]
    expand_grad, class_grad = expand_grad[0], class_grad[0]

    heads_first = heads_first.astype(F32).reshape(8, deep // chips, mid)
    heads_grad = jnp.concatenate([heads_first, jnp.concatenate([heads_yx, heads_xy], axis=2)])
    own_rows = w_heads.shape[1]
    heads_grad = in_order(
        lax.dynamic_slice_in_dim(heads_grad, core * own_rows, own_rows, axis=1),
        swap(lax.dynamic_slice_in_dim(heads_grad, (1 - core) * own_rows, own_rows, axis=1)),
        2,
    ).astype(F32)
    sides_grad = sides_grad.astype(F32).reshape(9, piece_side, 2, mid)
    own_rows = piece_side // 2
    sides_mine = lax.dynamic_slice_in_dim(sides_grad, core * own_rows, own_rows, axis=1)
    sides_from = swap(
        lax.dynamic_slice_in_dim(sides_grad, (1 - core) * own_rows, own_rows, axis=1)
    )
    message_grad = jnp.stack(
        [
            jnp.where(core == 0, sides_from[:, :, 0], sides_mine[:, :, 0]),
            jnp.where(core == 0, sides_mine[:, :, 0], sides_from[:, :, 0]),
        ]
    )
    gate_grad = jnp.stack(
        [
            jnp.where(core == 0, sides_mine[:, :, 1], sides_from[:, :, 1]),
            jnp.where(core == 0, sides_from[:, :, 1], sides_mine[:, :, 1]),
        ]
    )
    return (
        depth_pred,
        seg_logits,
        features_grad,
        reduce_grad,
        dilated_grad,
        expand_grad,
        gain_reduce_grad,
        bias_reduce_grad,
        gain_dilated_grad,
        bias_dilated_grad,
        gain_expand_grad,
        bias_expand_grad,
        heads_grad,
        gain_heads_grad,
        bias_heads_grad,
        message_grad.astype(F32),
        gate_grad.astype(F32),
        class_grad[:, :classes],
        class_grad[:, classes],
    )


def solution(mesh):
    img, row = mesh.shape["img"], mesh.shape["row"]
    side = row // 2
    fine = Mesh(mesh.devices.reshape(img // side, side, side, 2), ALL)
    crops, rows = ("z", "x"), ("y", "c")
    every = ALL
    placed = (
        P(crops, rows, None, None),
        P(every, None),
        P(None, every, None),
        P(every, None),
        P(),
        P(),
        P(),
        P(),
        P(),
        P(),
        P(None, every, None),
        P(),
        P(),
        P(None, None, every, None),
        P(None, None, every, None),
        P(every, None),
        P(every),
        P(crops, rows, None),
        P(crops, rows, None),
        P(crops, rows, None),
    )
    return jax.shard_map(
        per_device,
        mesh=fine,
        in_specs=placed,
        out_specs=(
            P(crops, rows, None),
            P(crops, rows, None, None),
            P(crops, rows, None, None),
            P(every, None),
            P(None, every, None),
            P(every, None),
            P(),
            P(),
            P(),
            P(),
            P(),
            P(),
            P(None, every, None),
            P(),
            P(),
            P(None, None, every, None),
            P(None, None, every, None),
            P(every, None),
            P(every),
        ),
        check_vma=False,
    )
```

```python
import functools
import itertools

import jax
import jax.numpy as jnp
from jax import lax
from jax.experimental import pallas as pl
from jax.experimental.pallas import tpu as pltpu
from jax.sharding import Mesh
from jax.sharding import PartitionSpec as P

EPS = 1e-05
ALL = ("z", "x", "y", "c")
CHIPS = ("z", "x", "y")
PLANE = ("x", "y")
ROWS = ("y", "c")
BF, F32 = jnp.bfloat16, jnp.float32
MESH = pl.DeviceIdType.MESH
VMEM_BYTES = 60 * 1024 * 1024


def flat_index(axes, sizes):
    index = 0
    for a, n in zip(axes, sizes):
        index = index * n + lax.axis_index(a)
    return index


def coordinates(axes, sizes, index):
    place = {}
    for a, n in reversed(list(zip(axes, sizes))):
        place[a] = lax.rem(index, n)
        index = index // n
    return place


def small_sum_kernel(stages, kind, count, v_ref, o_ref, *scratch):
    slots, send_sem, recv_sem = scratch[: len(stages)], scratch[-2], scratch[-1]
    barrier = pltpu.get_barrier_semaphore()
    peers = 0
    for axes, sizes in stages:
        me, n = flat_index(axes, sizes), total(sizes)
        for s in range(1, n):
            pl.semaphore_signal(
                barrier,
                inc=1,
                device_id=coordinates(axes, sizes, lax.rem(me + s, n)),
                device_id_type=MESH,
            )
            peers += 1
    pl.semaphore_wait(barrier, peers)
    current = v_ref[...]
    which = 0
    for slot, (axes, sizes) in zip(slots, stages):
        me, n = flat_index(axes, sizes), total(sizes)
        slot[me] = current
        copies = []
        for s in range(1, n):
            copy = pltpu.make_async_remote_copy(
                src_ref=slot.at[me],
                dst_ref=slot.at[me],
                send_sem=send_sem.at[which],
                recv_sem=recv_sem.at[which],
                device_id=coordinates(axes, sizes, lax.rem(me + s, n)),
                device_id_type=MESH,
            )
            copy.start()
            copies.append(copy)
            which += 1
        for copy in copies:
            copy.wait()
        first, second = slot[0, 0], slot[0, 1]
        for s in range(1, n):
            first = first + slot[s, 0]
            second = second + slot[s, 1]
        if kind == "moments":
            mean = first / n
            for s in range(n):
                second = second + count * jnp.square(slot[s, 0] - mean)
            first = mean
            count = count * n
        current = jnp.stack([first, second])
    o_ref[...] = current


def total(sizes):
    n = 1
    for size in sizes:
        n *= size
    return n


def small_sum(pair, axes, kind, count, collective):
    channels = pair[0].shape[0]
    stages = tuple(
        (group, tuple(lax.axis_size(a) for a in group)) for group in (axes[1:], axes[:1])
    )
    shape = (2, channels // 128, 128)
    n_copies = sum(total(sizes) - 1 for _, sizes in stages)
    out = pl.pallas_call(
        functools.partial(small_sum_kernel, stages, kind, float(count)),
        out_shape=jax.ShapeDtypeStruct(shape, F32),
        in_specs=[pl.BlockSpec(memory_space=pltpu.VMEM)],
        out_specs=pl.BlockSpec(memory_space=pltpu.VMEM),
        scratch_shapes=[pltpu.VMEM((total(sizes),) + shape, F32) for _, sizes in stages]
        + [pltpu.SemaphoreType.DMA((n_copies,)), pltpu.SemaphoreType.DMA((n_copies,))],
        compiler_params=pltpu.CompilerParams(collective_id=collective, has_side_effects=True),
        cost_estimate=pl.CostEstimate(flops=0, bytes_accessed=30_000_000, transcendentals=0),
    )(jnp.stack(pair).reshape(shape))
    return out[0].reshape(channels), out[1].reshape(channels)


def gather_kernel(geometry, both_cores, parts, *refs):
    n_z, n_x, n_y = geometry
    many = len(parts)
    arrays = (len(refs) - 3) // 2
    ins, outs = refs[:arrays], refs[arrays : 2 * arrays]
    own_sem, send_sem, recv_sem = refs[2 * arrays :]
    z, x, y, core = (lax.axis_index(a) for a in ALL)
    sizes = {"z": n_z, "x": n_x, "y": n_y, "c": 2}
    here = {"z": z, "x": x, "y": y, "c": core}
    used = ("z", "x", "y", "c") if both_cores else ("z", "x", "y")

    def peer(axis, s):
        return {axis: lax.rem(here[axis] + s, sizes[axis])}

    barrier = pltpu.get_barrier_semaphore()
    peers = 0
    for axis in used:
        for s in range(1, sizes[axis]):
            pl.semaphore_signal(barrier, inc=1, device_id=peer(axis, s), device_id_type=MESH)
            peers += 1
    pl.semaphore_wait(barrier, peers)

    def back(axis, s):
        return lax.rem(here[axis] + sizes[axis] - s, sizes[axis])

    def view(p, place):
        array, lead, dim, rows, _ = parts[p]
        index = (back("z", place[0]) * n_x + back("x", place[1])) * n_y + back("y", place[2])
        if both_cores:
            index = index * 2 + core
        span = pl.ds(pl.multiple_of(index * rows, rows), rows)
        if dim == 0:
            return outs[array].at[span]
        return outs[array].at[pl.ds(*lead), span] if lead else outs[array].at[:, span]

    def given(p):
        array, lead = parts[p][:2]
        return ins[array].at[pl.ds(*lead)] if lead else ins[array]

    started = []

    def send(p, place, axis, s):
        source = given(p) if place == (0, 0, 0) else view(p, place)
        which = len(started)
        copy = pltpu.make_async_remote_copy(
            src_ref=source,
            dst_ref=view(p, place),
            send_sem=send_sem.at[which],
            recv_sem=recv_sem.at[which],
            device_id=peer(axis, s),
            device_id_type=MESH,
        )
        copy.start()
        started.append(copy)
        return copy

    last = []

    def to_core(p, place):
        if both_cores:
            last.append(send(p, place, "c", 1))

    own = []
    along_z = {}
    for s in range(1, n_z):
        for p in range(many):
            along_z[s, p] = send(p, (0, 0, 0), "z", s)
    second, third = {}, {}

    def spread(p, zs):
        first_axis, second_axis = ("x", "y") if parts[p][4] == 1 else ("y", "x")
        for s in range(1, sizes[first_axis]):
            second[p, zs, s] = send(p, (zs, 0, 0), first_axis, s)
        for s in range(1, sizes[second_axis]):
            third[p, zs, 0, s] = send(p, (zs, 0, 0), second_axis, s)
        to_core(p, (zs, 0, 0))

    def place_of(p, zs, a, b):
        return (zs, a, b) if parts[p][4] == 1 else (zs, b, a)

    for p in range(many):
        spread(p, 0)
    for p in range(many):
        copy = pltpu.make_async_copy(given(p), view(p, (0, 0, 0)), own_sem.at[p])
        copy.start()
        own.append(copy)
    for zs in range(1, n_z):
        for p in range(many):
            along_z[zs, p].wait_recv()
            spread(p, zs)
    for zs in range(n_z):
        for p in range(many):
            first_axis, second_axis = ("x", "y") if parts[p][4] == 1 else ("y", "x")
            for a in range(1, sizes[first_axis]):
                second[p, zs, a].wait_recv()
                for s in range(1, sizes[second_axis]):
                    third[p, zs, a, s] = send(p, place_of(p, zs, a, 0), second_axis, s)
                to_core(p, place_of(p, zs, a, 0))
    for zs in range(n_z):
        for p in range(many):
            first_axis, second_axis = ("x", "y") if parts[p][4] == 1 else ("y", "x")
            for b in range(1, sizes[second_axis]):
                for a in range(sizes[first_axis]):
                    third[p, zs, a, b].wait_recv()
                    to_core(p, place_of(p, zs, a, b))
    for copy in last:
        copy.wait_recv()
    for copy in own:
        copy.wait()
    for copy in started:
        copy.wait_send()


def gather_pieces(arrays, parts, both_cores, collective, microseconds):
    geometry = tuple(lax.axis_size(a) for a in CHIPS)
    chips = total(geometry)
    many = len(parts)
    cut_at = {part[0]: part[2] for part in parts}
    shapes = []
    for i, array in enumerate(arrays):
        shape = list(array.shape)
        shape[cut_at[i]] *= chips * (2 if both_cores else 1)
        shapes.append(jax.ShapeDtypeStruct(tuple(shape), array.dtype))
    n_copies = many * (chips - 1 + (chips if both_cores else 0))
    return pl.pallas_call(
        functools.partial(gather_kernel, geometry, both_cores, parts),
        out_shape=shapes,
        in_specs=[pl.BlockSpec(memory_space=pl.ANY)] * len(arrays),
        out_specs=[pl.BlockSpec(memory_space=pl.ANY)] * len(arrays),
        scratch_shapes=[
            pltpu.SemaphoreType.DMA((many,)),
            pltpu.SemaphoreType.DMA((n_copies,)),
            pltpu.SemaphoreType.DMA((n_copies,)),
        ],
        compiler_params=pltpu.CompilerParams(collective_id=collective, has_side_effects=True),
        cost_estimate=pl.CostEstimate(
            flops=0, bytes_accessed=int(3.5e6 * microseconds), transcendentals=0
        ),
    )(*arrays)


def scatter_kernel(sizes, orders, layouts, window, *refs):
    many = len(orders)
    depth = max(len(order) for order in orders)
    ins, outs = refs[:many], refs[many : 2 * many]
    own = refs[2 * many : 3 * many]
    landed = [refs[(3 + i) * many : (4 + i) * many] for i in range(depth)]
    own_sem, send_sem, recv_sem = refs[-3:]
    here = {a: lax.axis_index(a) for a in sizes}

    def forth(axis, s):
        return lax.rem(here[axis] + s, sizes[axis])

    barrier = pltpu.get_barrier_semaphore()
    peers = 0
    for axis in sizes:
        for s in range(1, sizes[axis]):
            pl.semaphore_signal(
                barrier, inc=1, device_id={axis: forth(axis, s)}, device_id_type=MESH
            )
            peers += 1
    pl.semaphore_wait(barrier, peers)

    started = []

    def send(source, target, axis, s):
        which = len(started)
        copy = pltpu.make_async_remote_copy(
            src_ref=source,
            dst_ref=target,
            send_sem=send_sem.at[which],
            recv_sem=recv_sem.at[which],
            device_id={axis: forth(axis, s)},
            device_id_type=MESH,
        )
        copy.start()
        started.append(copy)
        return copy

    places = []
    for order in orders:
        steps = [list(range(1, sizes[a])) + [0] for a in order[1:]]
        places.append(list(itertools.product(*steps)))

    def block(p, steps):
        index = 0
        at = dict(zip(orders[p], steps))
        for axis in layouts[p]:
            index = index * sizes[axis] + forth(axis, at[axis])
        return index

    def slot(p, stage, steps):
        index = 0
        for axis, s in zip(orders[p][stage + 1 :], steps):
            index = index * sizes[axis] + s
        return index

    loads, copies = {}, {}
    for p in range(many):
        for k, place in enumerate(places[p]):
            copy = pltpu.make_async_copy(
                ins[p].at[block(p, (0,) + place)], own[p].at[k], own_sem.at[len(loads)]
            )
            copy.start()
            loads[p, k] = copy

    def send_first(k):
        for p in range(many):
            if k < len(places[p]):
                place = places[p][k]
                for s in range(1, sizes[orders[p][0]]):
                    copies[p, 0, s, place] = send(
                        ins[p].at[block(p, (s,) + place)],
                        landed[0][p].at[s - 1, slot(p, 0, place)],
                        orders[p][0],
                        s,
                    )

    waited = set()
    longest = max(len(each) for each in places)
    for k in range(min(window, longest)):
        send_first(k)
    for k in range(longest):
        for p in range(many):
            own_k = k - (longest - len(places[p]))
            if own_k < 0:
                continue
            order, place = orders[p], places[p][own_k]
            loads[p, own_k].wait()
            terms, onward = [], None
            for stage, axis in enumerate(order):
                later = place[stage:]
                if stage > 0 and place[stage - 1] > 0:
                    onward = (stage, axis, place[stage - 1], later)
                    break
                for s in range(1, sizes[axis]):
                    copies[p, stage, s, later].wait_recv()
                    terms.append((landed[stage][p], (s - 1, slot(p, stage, later))))

            def add(t, carry, p=p, k=own_k, terms=terms, final=onward is None):
                value = own[p][k, t].astype(F32)
                for ref, index in terms:
                    value = value + ref[(*index, t)].astype(F32)
                if final:
                    outs[p][t] = value
                else:
                    own[p][k, t] = value.astype(BF)
                return carry

            lax.fori_loop(0, own[p].shape[1], add, 0)
            if onward:
                stage, axis, s, later = onward
                copies[p, stage, s, later] = send(
                    own[p].at[own_k], landed[stage][p].at[s - 1, slot(p, stage, later)], axis, s
                )
        if k + window < longest:
            for p in range(many):
                if k < len(places[p]):
                    for s in range(1, sizes[orders[p][0]]):
                        copy = copies[p, 0, s, places[p][k]]
                        copy.wait_send()
                        waited.add(id(copy))
            send_first(k + window)
    for copy in started:
        if id(copy) not in waited:
            copy.wait_send()


def scatter_blocks(arrays, orders, layouts, window, collective):
    sizes = {a: lax.axis_size(a) for a in ALL}
    depth = max(len(order) for order in orders)
    own, landed = [], [[] for _ in range(depth)]
    loads = copies = 0
    for array, order in zip(arrays, orders):
        shape = array.shape[1:]
        own.append(pltpu.VMEM((total(sizes[a] for a in order[1:]),) + shape, BF))
        loads += total(sizes[a] for a in order[1:])
        for stage in range(depth):
            if stage < len(order):
                peers, later = sizes[order[stage]] - 1, total(sizes[a] for a in order[stage + 1 :])
                landed[stage].append(pltpu.VMEM((peers, later) + shape, BF))
                copies += peers * later
            else:
                landed[stage].append(pltpu.VMEM((1, 1, 16, 128), BF))
    return pl.pallas_call(
        functools.partial(scatter_kernel, sizes, orders, layouts, window),
        out_shape=[jax.ShapeDtypeStruct(a.shape[1:], F32) for a in arrays],
        in_specs=[pl.BlockSpec(memory_space=pl.ANY)] * len(arrays),
        out_specs=[pl.BlockSpec(memory_space=pltpu.VMEM)] * len(arrays),
        scratch_shapes=own
        + sum(landed, [])
        + [
            pltpu.SemaphoreType.DMA((loads,)),
            pltpu.SemaphoreType.DMA((copies,)),
            pltpu.SemaphoreType.DMA((copies,)),
        ],
        compiler_params=pltpu.CompilerParams(
            collective_id=collective, has_side_effects=True, vmem_limit_bytes=VMEM_BYTES
        ),
        cost_estimate=pl.CostEstimate(flops=0, bytes_accessed=250_000_000, transcendentals=0),
    )(*arrays)


def combine_cols(before, same, after, col, spread):
    n = same.shape[0]
    before = jnp.where(col < spread, 0.0, pltpu.roll(before, spread, 0))
    after = jnp.where(col >= n - spread, 0.0, pltpu.roll(after, n - spread, 0))
    return before + same + after


def conv_fwd(xpad, weights, spread, kc, nc, n_blocks, n_first, moments, out_dtype):
    batch, height_pad, width, depth = xpad.shape
    height, wide = height_pad - 2 * spread, n_blocks * nc
    px = batch * height * width
    steps = depth // kc

    def body(first_ref, x_ref, *rest):
        taps = [ref.at[t] for ref, w in zip(rest, weights) for t in range(w[1])]
        rest = rest[len(weights) :]
        o_ref, acc = rest[0], rest[-1]
        k = pl.program_id(1)

        def dots(first):
            for b in range(3):
                for a in range(3):
                    xa = x_ref[:, a * spread : a * spread + height].reshape(px, kc)
                    d = jnp.dot(xa, taps[3 * a + b][...], preferred_element_type=F32)
                    if first and a == 0:
                        acc[b] = d
                    else:
                        acc[b] += d

        @pl.when(k == 0)
        def _():
            dots(True)

        @pl.when(k > 0)
        def _():
            dots(False)

        @pl.when(k == steps - 1)
        def _():
            col = lax.broadcasted_iota(jnp.int32, (width, nc), 0)

            def store(i, running):
                r = pl.ds(pl.multiple_of(i * width, width), width)
                v = combine_cols(acc[0, r], acc[1, r], acc[2, r], col, spread)
                o_ref[r] = v.astype(out_dtype)
                return running + jnp.sum(v.reshape(width // 8, 8, nc), axis=0) if moments else 0

            start = jnp.zeros((8, nc), F32)
            running = lax.fori_loop(0, batch * height, store, start if moments else 0)
            if moments:
                mean = jnp.sum(running, axis=0, keepdims=True) / px

                def deviation(i, so_far):
                    r = pl.ds(pl.multiple_of(i * width, width), width)
                    v = jnp.square(o_ref[r] - mean)
                    return so_far + jnp.sum(v.reshape(width // 8, 8, nc), axis=0)

                m2 = lax.fori_loop(0, batch * height, deviation, start)
                row = lax.broadcasted_iota(jnp.int32, (8, nc), 0)
                rest[1][...] = jnp.where(row == 0, mean, jnp.sum(m2, axis=0, keepdims=True))

    out_specs = [pl.BlockSpec((px, nc), lambda n, k, f: (0, n))]
    out_shape = [jax.ShapeDtypeStruct((px, wide), out_dtype)]
    if moments:
        out_specs.append(pl.BlockSpec((8, nc), lambda n, k, f: (0, n)))
        out_shape.append(jax.ShapeDtypeStruct((8, wide), F32))
    return pl.pallas_call(
        body,
        grid_spec=pltpu.PrefetchScalarGridSpec(
            num_scalar_prefetch=1,
            grid=(n_blocks, steps),
            in_specs=[
                pl.BlockSpec((batch, height_pad, width, kc), lambda n, k, f: (0, 0, 0, k)),
                *(
                    pl.BlockSpec(
                        (many, kc, nc),
                        lambda n, k, f, lead=lead, pick=pick: (lead, k, n + f[0] if pick else n),
                    )
                    for _, many, lead, pick in weights
                ),
            ],
            out_specs=out_specs,
            scratch_shapes=[pltpu.VMEM((3, px, nc), F32)],
        ),
        out_shape=out_shape,
        compiler_params=pltpu.CompilerParams(vmem_limit_bytes=VMEM_BYTES),
        cost_estimate=pl.CostEstimate(
            flops=18 * px * depth * wide,
            bytes_accessed=18 * depth * wide + 2 * px * depth + 4 * px * wide,
            transcendentals=0,
        ),
    )(n_first, xpad, *(w[0] for w in weights))


def conv_dgrad(gpads, weights, spread, cc, c_range, n_first, out_dtype, by_core=False):
    batch, height_pad, width, wide = gpads[0].shape
    many = len(gpads)
    height, depth = height_pad - 2 * spread, len(c_range) * cc
    c_first = c_range[0]
    px = batch * height * width
    dims = (((1,), (1,)), ((), ()))
    results = 2 if by_core else 1
    lines = height // results

    def body(first_ref, *refs):
        gs, outs, acc = refs[:many], refs[many + len(weights) : -1], refs[-1]
        taps = [
            ref.at[t]
            for ref, w in zip(refs[many : many + len(weights)], weights)
            for t in range(w[1])
        ]
        for q in range(many):
            for b in range(3):
                for a in range(3):
                    top = (2 - a) * spread
                    ga = gs[q][:, top : top + height].reshape(px, wide)
                    d = lax.dot_general(
                        ga, taps[9 * q + 3 * a + b][...], dims, preferred_element_type=F32
                    )
                    if q == 0 and a == 0:
                        acc[2 - b] = d
                    else:
                        acc[2 - b] += d
        col = lax.broadcasted_iota(jnp.int32, (width, cc), 0)

        for which, o_ref in enumerate(outs):

            def store(i, carry, which=which, o_ref=o_ref):
                line = i
                if by_core:
                    part = first_ref[0] if which == 0 else 1 - first_ref[0]
                    line = i // lines * height + part * lines + lax.rem(i, lines)
                r = pl.ds(pl.multiple_of(line * width, width), width)
                value = combine_cols(acc[0, r], acc[1, r], acc[2, r], col, spread)
                o_ref[pl.ds(pl.multiple_of(i * width, width), width)] = value.astype(out_dtype)
                return carry

            lax.fori_loop(0, batch * lines, store, 0)

    return pl.pallas_call(
        body,
        grid_spec=pltpu.PrefetchScalarGridSpec(
            num_scalar_prefetch=1,
            grid=(depth // cc,),
            in_specs=[pl.BlockSpec((batch, height_pad, width, wide), lambda c, f: (0, 0, 0, 0))]
            * many
            + [
                pl.BlockSpec(
                    (taps, cc, wide),
                    lambda c, f, lead=lead, pick=pick: (lead, c + c_first, f[0] if pick else 0),
                )
                for _, taps, lead, pick in weights
            ],
            out_specs=[pl.BlockSpec((px // results, cc), lambda c, f: (0, c))] * results,
            scratch_shapes=[pltpu.VMEM((3, px, cc), F32)],
        ),
        out_shape=[jax.ShapeDtypeStruct((px // results, depth), out_dtype)] * results,
        compiler_params=pltpu.CompilerParams(vmem_limit_bytes=VMEM_BYTES),
        cost_estimate=pl.CostEstimate(
            flops=18 * many * px * depth * wide,
            bytes_accessed=18 * many * depth * wide + 4 * px * depth,
            transcendentals=0,
        ),
    )(n_first, *gpads, *(w[0] for w in weights))


def conv_wgrad(xpad, grad, spread, cc, nc, piece, plane, shares):
    batch, height_pad, width, depth = xpad.shape
    height, wide = height_pad - 2 * spread, grad.shape[1]
    px = batch * height * width
    each, blocks = cc // piece, wide // nc
    lines = 128 // width

    def body(x_ref, g_ref, *rest):
        outs, shifted = rest[:-1], rest[-1]

        @pl.when(pl.program_id(1) == 0)
        def _():
            col = lax.broadcasted_iota(jnp.int32, (width, nc), 0)

            def turn(i, carry):
                r = pl.ds(pl.multiple_of(i * 128, 128), 128)
                block = g_ref[r].astype(F32)
                for b in range(3):
                    moved = []
                    for j in range(lines):
                        v = block[j * width : (j + 1) * width]
                        if b == 0:
                            v = jnp.where(
                                col >= width - spread, 0.0, pltpu.roll(v, width - spread, 0)
                            )
                        elif b == 2:
                            v = jnp.where(col < spread, 0.0, pltpu.roll(v, spread, 0))
                        moved.append(v)
                    shifted[b, :, r] = jnp.concatenate(moved, axis=0).T.astype(BF)
                return carry

            lax.fori_loop(0, px // 128, turn, 0)

        for a in range(3):
            xa = x_ref[:, a * spread : a * spread + height].reshape(px, cc)
            for b in range(3):
                d = jnp.dot(shifted[b], xa, preferred_element_type=F32).T.astype(BF)
                for out, (taps, low, high) in zip(outs, shares):
                    if 3 * a + b in taps:
                        for j in range(each):
                            out[j % plane, j // plane, taps.index(3 * a + b)] = d[
                                j * piece : (j + 1) * piece, low:high
                            ]

    return pl.pallas_call(
        body,
        grid=(blocks, depth // cc),
        in_specs=[
            pl.BlockSpec((batch, height_pad, width, cc), lambda n, c: (0, 0, 0, c)),
            pl.BlockSpec((px, nc), lambda n, c: (0, n)),
        ],
        out_specs=[
            pl.BlockSpec(
                (plane, each // plane, len(taps), piece, high - low), lambda n, c: (0, c, 0, 0, n)
            )
            for taps, low, high in shares
        ],
        out_shape=[
            jax.ShapeDtypeStruct(
                (plane, depth // (plane * piece), len(taps), piece, blocks * (high - low)), BF
            )
            for taps, low, high in shares
        ],
        scratch_shapes=[pltpu.VMEM((3, nc, px), BF)],
        compiler_params=pltpu.CompilerParams(vmem_limit_bytes=VMEM_BYTES),
        cost_estimate=pl.CostEstimate(
            flops=18 * px * depth * wide,
            bytes_accessed=18 * depth * wide + 2 * px * depth,
            transcendentals=0,
        ),
    )(xpad, grad)


def outer_sum(left, right, cc, turned):
    px, wide = left.shape
    deep = right.shape[1]

    def body(l_ref, r_ref, o_ref, flipped):
        @pl.when(pl.program_id(0) == 0)
        def _():
            def turn(i, carry):
                r = pl.ds(pl.multiple_of(i * 128, 128), 128)
                flipped[:, r] = l_ref[r].astype(F32).T.astype(BF)
                return carry

            lax.fori_loop(0, px // 128, turn, 0)

        d = jnp.dot(flipped[...], r_ref[...], preferred_element_type=F32)
        o_ref[...] = (d.T if turned else d).astype(BF)

    return pl.pallas_call(
        body,
        grid=(deep // cc,),
        in_specs=[
            pl.BlockSpec((px, wide), lambda c: (0, 0)),
            pl.BlockSpec((px, cc), lambda c: (0, c)),
        ],
        out_specs=pl.BlockSpec((cc, wide), lambda c: (c, 0))
        if turned
        else pl.BlockSpec((wide, cc), lambda c: (0, c)),
        out_shape=jax.ShapeDtypeStruct((deep, wide) if turned else (wide, deep), BF),
        scratch_shapes=[pltpu.VMEM((wide, px), BF)],
        compiler_params=pltpu.CompilerParams(vmem_limit_bytes=VMEM_BYTES),
        cost_estimate=pl.CostEstimate(
            flops=2 * px * deep * wide,
            bytes_accessed=2 * (deep * wide + px * (deep + wide)),
            transcendentals=0,
        ),
    )(left, right)


def swap(value):
    return lax.ppermute(value, "c", [(0, 1), (1, 0)])


def in_order(mine, other, dim):
    first = lax.axis_index("c") == 0
    return jnp.concatenate(
        [jnp.where(first, mine, other), jnp.where(first, other, mine)], axis=dim
    )


def rims(block, axes, width):
    count = 1
    for a in axes:
        count *= lax.axis_size(a)
    forward = [(i, i + 1) for i in range(count - 1)]
    backward = [(t, s) for s, t in forward]
    low = lax.ppermute(block[:, block.shape[1] - width :], axes, forward)
    high = lax.ppermute(block[:, :width], axes, backward)
    return low, high


def with_rims(block, axes, width):
    low, high = rims(block, axes, width)
    return jnp.concatenate([low, block, high], axis=1)


def local_moments(value):
    mean = jnp.mean(value, axis=(0, 1, 2))
    return mean, jnp.sum(jnp.square(value - mean), axis=(0, 1, 2))


def gelu_back(inner, upstream):
    return jax.vjp(jax.nn.gelu, inner)[1](upstream)[0]


def gather(value, axes, dim):
    return lax.all_gather(value, axes, axis=dim, tiled=True)


def scatter_sum(value, axes, dim):
    return lax.psum_scatter(value, axes, scatter_dimension=dim, tiled=True)


def per_device(
    features,
    w_reduce,
    w_dilated,
    w_expand,
    gain_reduce,
    bias_reduce,
    gain_dilated,
    bias_dilated,
    gain_expand,
    bias_expand,
    w_heads,
    gain_heads,
    bias_heads,
    w_message,
    w_gate,
    w_seg,
    w_depth,
    labels,
    depth_target,
    depth_mask,
):
    core = lax.axis_index("c")
    chips = lax.axis_size("z") * lax.axis_size("x") * lax.axis_size("y")
    devices = chips * 2
    crops, height, width, deep = features.shape
    mid = w_reduce.shape[1]
    classes = w_seg.shape[1]
    local_px = crops * height * width
    pixels = local_px * devices
    chip_px = local_px * 2

    tied = lax.optimization_barrier
    r_rows, d_rows = w_reduce.shape[0], w_dilated.shape[1]
    last_chip = in_order(
        lax.dynamic_slice_in_dim(w_heads[7:], core * mid, mid, axis=2),
        swap(lax.dynamic_slice_in_dim(w_heads[7:], (1 - core) * mid, mid, axis=2)),
        1,
    )
    heads_most = gather(w_heads[:7], ALL, 1)
    sides_own = jnp.stack([w_message[1 - core], w_gate[core]])
    sides_other = jnp.stack([w_message[core], w_gate[1 - core]])
    sides_full = gather(in_order(sides_own, swap(sides_other), 2), CHIPS, 2)
    quarters = deep // mid
    small = jnp.concatenate([w_seg, w_depth[:, None]], axis=1)
    small = jnp.pad(small, ((0, 0), (0, mid - classes - 1)))
    side_blocks = jnp.stack(
        [w_expand[:, q * mid : (q + 1) * mid] for q in range(quarters)] + [small]
    )
    reduce_full, dilated_full, blocks_full = gather_pieces(
        (w_reduce, w_dilated, side_blocks),
        ((0, None, 0, r_rows, 2), (1, None, 1, d_rows, 1), (2, None, 1, d_rows, 2)),
        True,
        8,
        40,
    )
    expand_full = blocks_full[:quarters]
    class_full = blocks_full[quarters, :, :128]
    none = jnp.zeros((1,), jnp.int32)
    own_half = core.astype(jnp.int32).reshape(1)

    first_raw = jnp.einsum("bhwc,co->bhwo", features, reduce_full, preferred_element_type=F32)

    def norm(raw_moments, axes, count, collective):
        mean, m2 = small_sum(raw_moments, axes, "moments", count, collective)
        return mean, lax.rsqrt(m2 / pixels + EPS)

    stats_one = norm(local_moments(first_raw), ALL, local_px, 0)
    scaled_one = (first_raw - stats_one[0]) * stats_one[1]
    inner_one = scaled_one * gain_reduce + bias_reduce
    hidden_one = jax.nn.gelu(inner_one).astype(BF)
    padded_one = with_rims(hidden_one, ROWS, 2)

    dilated_taps = ((dilated_full, 9, 0, False),)
    second_raw, second_moments = conv_fwd(
        padded_one, dilated_taps, 2, 256, mid, 1, none, True, F32
    )
    second_raw = second_raw.reshape(crops, height, width, mid)
    stats_two = norm((second_moments[0], second_moments[1]), ALL, local_px, 1)
    scaled_two = (second_raw - stats_two[0]) * stats_two[1]
    inner_two = scaled_two * gain_dilated + bias_dilated
    hidden_two = jax.nn.gelu(inner_two).astype(BF)
    third_raw = jnp.einsum(
        "bhwc,qco->bhwqo", hidden_two, expand_full, preferred_element_type=F32
    ).reshape(crops, height, width, deep)
    stats_three = norm(local_moments(third_raw), ALL, local_px, 2)
    scaled_three = (third_raw - stats_three[0]) * stats_three[1]
    inner_three = scaled_three * gain_expand + bias_expand + features.astype(F32)
    output = jax.nn.gelu(inner_three).astype(BF)

    low, high = rims(output, ROWS, 1)
    outer = jnp.where(core == 0, low, high)
    outer_other = swap(outer)
    output_other = swap(output)
    output_pad = jnp.concatenate(
        [
            jnp.where(core == 0, low, outer_other),
            in_order(output, output_other, 1),
            jnp.where(core == 0, outer_other, high),
        ],
        axis=1,
    )
    tall = 2 * height
    last_chip, output_pad = tied((last_chip, output_pad))
    last_rows = last_chip.shape[1]
    (heads_last,) = gather_pieces(
        (last_chip,), ((0, (0, 1), 1, last_rows, 1), (0, (1, 1), 1, last_rows, 2)), False, 9, 45
    )
    heads_last, output_pad = tied((heads_last, output_pad))
    heads_taps = ((heads_most, 7, 0, True), (heads_last, 2, 0, False))
    heads_raw, heads_moments = conv_fwd(
        output_pad, heads_taps, 1, 512, mid, 1, own_half, True, F32
    )
    stats_heads = norm((heads_moments[0], heads_moments[1]), CHIPS, chip_px, 3)
    gain_own = lax.dynamic_slice_in_dim(gain_heads, core * mid, mid)
    bias_own = lax.dynamic_slice_in_dim(bias_heads, core * mid, mid)
    scaled_heads = (heads_raw - stats_heads[0]) * stats_heads[1]
    inner_heads = scaled_heads * gain_own + bias_own
    feature = jax.nn.gelu(inner_heads).astype(BF)
    feature_pad = with_rims(feature.reshape(crops, tall, width, mid), ("y",), 1)

    sides_full = sides_full.reshape(18, mid, mid)
    side_taps = ((sides_full, 9, 0, False), (sides_full, 9, 1, False))
    (give,) = conv_fwd(
        feature_pad, side_taps[:1], 1, 256, mid, 1, none, False, BF
    )
    (gate,) = conv_fwd(feature_pad, side_taps[1:], 1, 256, mid, 1, none, False, F32)
    message = swap(give).astype(F32)
    sigma = jax.nn.sigmoid(gate)
    stream = (feature.astype(F32) + sigma * message).astype(BF)
    scores = jnp.dot(stream, class_full, preferred_element_type=F32)
    own_side = jnp.stack(
        [labels.astype(F32), depth_target, depth_mask.astype(F32)]
    )
    labels_chip, target_chip, mask_chip = in_order(own_side, swap(own_side), 2).reshape(3, chip_px)
    seg_scores = scores[:, :classes]
    log_total = jax.nn.logsumexp(seg_scores, axis=-1, keepdims=True)
    class_ids = jnp.arange(classes, dtype=jnp.int32)
    seg_back = jnp.exp(seg_scores - log_total) - (
        labels_chip.astype(jnp.int32)[:, None] == class_ids
    ).astype(F32)
    depth_scores = scores[:, classes]
    differ = depth_scores - target_chip
    depth_back = mask_chip * differ * lax.rsqrt(differ * differ + 1.0)
    score_back = jnp.concatenate(
        [
            jnp.where(core == 1, seg_back, 0.0),
            jnp.where(core == 0, depth_back, 0.0)[:, None],
            jnp.zeros((chip_px, 128 - classes - 1), F32),
        ],
        axis=1,
    ).astype(BF)
    class_grad = lax.dot_general(
        stream, score_back, (((0,), (0,)), ((), ())), preferred_element_type=F32
    )
    stream_grad = lax.dot_general(
        score_back, class_full, (((1,), (1,)), ((), ())), preferred_element_type=F32
    )

    scores_map = scores[:, : classes + 1].reshape(crops, tall, width, classes + 1)
    for_own = lax.dynamic_slice_in_dim(scores_map, core * height, height, axis=1)
    for_other = lax.dynamic_slice_in_dim(scores_map, (1 - core) * height, height, axis=1)
    from_other = swap(for_other)
    depth_pred = jnp.where(core == 0, for_own[..., classes], from_other[..., classes])
    seg_logits = jnp.where(core == 0, from_other[..., :classes], for_own[..., :classes])

    give_grad_other = (stream_grad * sigma).astype(BF)
    gate_grad_low = (stream_grad * message * sigma * (1.0 - sigma)).astype(BF)
    give_grad_low = swap(give_grad_other)
    piece_side = mid // chips
    plane = lax.axis_size("x") * lax.axis_size("y")
    tall_shape = (crops, tall, width, mid)
    side_rims = [rims(g.reshape(tall_shape), ("y",), 1) for g in (give_grad_low, gate_grad_low)]
    every_tap = tuple(range(9))
    (sides_grad,) = conv_wgrad(
        feature_pad,
        jnp.concatenate([give_grad_low, gate_grad_low], axis=1),
        1,
        mid,
        mid,
        piece_side,
        plane,
        ((every_tap, 0, mid),),
    )
    sides_grad, side_rims = tied((sides_grad, side_rims))
    give_pad, gate_pad = (
        jnp.concatenate([low, g.reshape(tall_shape), high], axis=1)
        for g, (low, high) in zip((give_grad_low, gate_grad_low), side_rims)
    )
    sides_grad = scatter_sum(sides_grad.reshape(-1, 2 * mid), PLANE, 0)
    (feature_back,) = conv_dgrad(
        [give_pad, gate_pad],
        side_taps,
        1,
        256,
        range(mid // 256),
        none,
        F32,
    )
    feature_grad = stream_grad + feature_back

    def norm_back(upstream, scaled, inverse, gain, axes, collective, kept=None):
        dims = tuple(range(upstream.ndim - 1))
        bias_grad, gain_grad = small_sum(
            (jnp.sum(upstream, axis=dims), jnp.sum(upstream * scaled, axis=dims)),
            axes,
            "sums",
            1,
            collective,
        )
        upstream = upstream if kept is None else kept
        grad = gain * inverse * (upstream - bias_grad / pixels - scaled * (gain_grad / pixels))
        return grad, gain_grad, bias_grad

    heads_raw_grad, gain_heads_own, bias_heads_own = norm_back(
        gelu_back(inner_heads, feature_grad), scaled_heads, stats_heads[1], gain_own, CHIPS, 4
    )
    heads_pair = jnp.stack([gain_heads_own, bias_heads_own])
    gain_heads_grad, bias_heads_grad = in_order(heads_pair, swap(heads_pair), 1)
    heads_low = heads_raw_grad.astype(BF)
    heads_rims = rims(heads_low.reshape(tall_shape), ("y",), 1)
    most_taps, last_tap = every_tap[:8], every_tap[8:]
    heads_first, heads_yx, heads_xy = conv_wgrad(
        output_pad,
        heads_low,
        1,
        512,
        mid,
        deep // chips,
        plane,
        ((most_taps, 0, mid), (last_tap, 0, mid // 2), (last_tap, mid // 2, mid)),
    )
    heads_first, heads_yx, heads_xy, heads_rims = tied(
        (heads_first, heads_yx, heads_xy, heads_rims)
    )
    heads_pad = jnp.concatenate(
        [heads_rims[0], heads_low.reshape(tall_shape), heads_rims[1]], axis=1
    )
    heads_first = scatter_sum(heads_first.reshape(-1, mid), PLANE, 0)
    heads_yx, heads_xy = (v.reshape(chips, *v.shape[2:]) for v in (heads_yx, heads_xy))
    grad_own, grad_other = conv_dgrad(
        [heads_pad], heads_taps, 1, 512, range(deep // 512), own_half, BF, True
    )
    output_grad = (grad_own.astype(F32) + swap(grad_other).astype(F32)).reshape(
        crops, height, width, deep
    )

    inner_three_grad = gelu_back(inner_three, output_grad)
    kept_grad = tied(inner_three_grad.astype(BF)).astype(F32)
    third_grad, gain_expand_grad, bias_expand_grad = norm_back(
        inner_three_grad, scaled_three, stats_three[1], gain_expand, ALL, 5, kept_grad
    )
    third_low = third_grad.astype(BF)
    expand_grad = outer_sum(hidden_two.reshape(-1, mid), third_low.reshape(-1, deep), 512, False)
    expand_grad = expand_grad.reshape(devices, 1, d_rows, deep)
    class_grad = class_grad.astype(BF).reshape(devices, 1, d_rows, 128)
    hidden_two_grad = jnp.einsum(
        "bhwqo,qco->bhwc",
        third_low.reshape(crops, height, width, quarters, mid),
        expand_full,
        preferred_element_type=F32,
    )
    second_grad, gain_dilated_grad, bias_dilated_grad = norm_back(
        gelu_back(inner_two, hidden_two_grad), scaled_two, stats_two[1], gain_dilated, ALL, 6
    )
    second_low = second_grad.astype(BF)
    second_rims = rims(second_low, ROWS, 2)
    (dilated_grad,) = conv_wgrad(
        padded_one, second_low.reshape(-1, mid), 2, mid, mid, d_rows, 1, ((every_tap, 0, mid),)
    )
    dilated_grad, expand_grad, second_rims = tied((dilated_grad, expand_grad, second_rims))
    second_pad = jnp.concatenate([second_rims[0], second_low, second_rims[1]], axis=1)
    (hidden_one_grad,) = conv_dgrad(
        [second_pad], dilated_taps, 2, 256, range(mid // 256), none, F32
    )
    hidden_one_grad, sides_grad, heads_first = tied((hidden_one_grad, sides_grad, heads_first))
    sides_grad = scatter_sum(sides_grad, "z", 0)
    heads_first = scatter_sum(heads_first, "z", 0)
    hidden_one_grad = hidden_one_grad.reshape(crops, height, width, mid)
    first_grad, gain_reduce_grad, bias_reduce_grad = norm_back(
        gelu_back(inner_one, hidden_one_grad), scaled_one, stats_one[1], gain_reduce, ALL, 7
    )
    first_low = first_grad.astype(BF)
    reduce_grad = outer_sum(first_low.reshape(-1, mid), features.reshape(-1, deep), 512, True)
    reduce_grad = reduce_grad.reshape(devices, 1, r_rows, mid)
    features_grad = kept_grad + jnp.einsum(
        "bhwo,co->bhwc", first_low, reduce_full, preferred_element_type=F32
    )

    dilated_grad = dilated_grad.reshape(devices, 9, d_rows, mid)
    features_grad, reduce_grad, sides_grad = tied((features_grad, reduce_grad, sides_grad))
    by_y, by_x = ("y", "x", "z"), ("x", "y", "z")
    heads_yx, heads_xy, dilated_grad, expand_grad, reduce_grad, class_grad = scatter_blocks(
        (heads_yx, heads_xy, dilated_grad, expand_grad, reduce_grad, class_grad),
        (by_y, by_x, ("c", *by_y), ("c", *by_x), ("c", *by_x), ("c", *by_x)),
        (by_x, by_x, ALL, ALL, ALL, ALL),
        4,
        10,
    )
    reduce_grad = reduce_grad[0]
    expand_grad, class_grad = expand_grad[0], class_grad[0]

    heads_first = heads_first.astype(F32).reshape(8, deep // chips, mid)
    heads_grad = jnp.concatenate([heads_first, jnp.concatenate([heads_yx, heads_xy], axis=2)])
    own_rows = w_heads.shape[1]
    heads_grad = in_order(
        lax.dynamic_slice_in_dim(heads_grad, core * own_rows, own_rows, axis=1),
        swap(lax.dynamic_slice_in_dim(heads_grad, (1 - core) * own_rows, own_rows, axis=1)),
        2,
    ).astype(F32)
    sides_grad = sides_grad.astype(F32).reshape(9, piece_side, 2, mid)
    own_rows = piece_side // 2
    sides_mine = lax.dynamic_slice_in_dim(sides_grad, core * own_rows, own_rows, axis=1)
    sides_from = swap(
        lax.dynamic_slice_in_dim(sides_grad, (1 - core) * own_rows, own_rows, axis=1)
    )
    message_grad = jnp.stack(
        [
            jnp.where(core == 0, sides_from[:, :, 0], sides_mine[:, :, 0]),
            jnp.where(core == 0, sides_mine[:, :, 0], sides_from[:, :, 0]),
        ]
    )
    gate_grad = jnp.stack(
        [
            jnp.where(core == 0, sides_mine[:, :, 1], sides_from[:, :, 1]),
            jnp.where(core == 0, sides_from[:, :, 1], sides_mine[:, :, 1]),
        ]
    )
    return (
        depth_pred,
        seg_logits,
        features_grad,
        reduce_grad,
        dilated_grad,
        expand_grad,
        gain_reduce_grad,
        bias_reduce_grad,
        gain_dilated_grad,
        bias_dilated_grad,
        gain_expand_grad,
        bias_expand_grad,
        heads_grad,
        gain_heads_grad,
        bias_heads_grad,
        message_grad.astype(F32),
        gate_grad.astype(F32),
        class_grad[:, :classes],
        class_grad[:, classes],
    )


def solution(mesh):
    img, row = mesh.shape["img"], mesh.shape["row"]
    side = row // 2
    fine = Mesh(mesh.devices.reshape(img // side, side, side, 2), ALL)
    crops, rows = ("z", "x"), ("y", "c")
    every = ALL
    placed = (
        P(crops, rows, None, None),
        P(every, None),
        P(None, every, None),
        P(every, None),
        P(),
        P(),
        P(),
        P(),
        P(),
        P(),
        P(None, every, None),
        P(),
        P(),
        P(None, None, every, None),
        P(None, None, every, None),
        P(every, None),
        P(every),
        P(crops, rows, None),
        P(crops, rows, None),
        P(crops, rows, None),
    )
    return jax.shard_map(
        per_device,
        mesh=fine,
        in_specs=placed,
        out_specs=(
            P(crops, rows, None),
            P(crops, rows, None, None),
            P(crops, rows, None, None),
            P(every, None),
            P(None, every, None),
            P(every, None),
            P(),
            P(),
            P(),
            P(),
            P(),
            P(),
            P(None, every, None),
            P(),
            P(),
            P(None, None, every, None),
            P(None, None, every, None),
            P(every, None),
            P(every),
        ),
        check_vma=False,
    )
```

```python
import functools
import itertools

import jax
import jax.numpy as jnp
from jax import lax
from jax.experimental import pallas as pl
from jax.experimental.pallas import tpu as pltpu
from jax.sharding import Mesh
from jax.sharding import PartitionSpec as P

EPS = 1e-05
ALL = ("z", "x", "y", "c")
CHIPS = ("z", "x", "y")
PLANE = ("x", "y")
ROWS = ("y", "c")
BF, F32 = jnp.bfloat16, jnp.float32
MESH = pl.DeviceIdType.MESH
VMEM_BYTES = 60 * 1024 * 1024


def flat_index(axes, sizes):
    index = 0
    for a, n in zip(axes, sizes):
        index = index * n + lax.axis_index(a)
    return index


def coordinates(axes, sizes, index):
    place = {}
    for a, n in reversed(list(zip(axes, sizes))):
        place[a] = lax.rem(index, n)
        index = index // n
    return place


def small_sum_kernel(stages, kind, count, v_ref, o_ref, *scratch):
    slots, send_sem, recv_sem = scratch[: len(stages)], scratch[-2], scratch[-1]
    barrier = pltpu.get_barrier_semaphore()
    peers = 0
    for axes, sizes in stages:
        me, n = flat_index(axes, sizes), total(sizes)
        for s in range(1, n):
            pl.semaphore_signal(
                barrier,
                inc=1,
                device_id=coordinates(axes, sizes, lax.rem(me + s, n)),
                device_id_type=MESH,
            )
            peers += 1
    pl.semaphore_wait(barrier, peers)
    current = v_ref[...]
    which = 0
    for slot, (axes, sizes) in zip(slots, stages):
        me, n = flat_index(axes, sizes), total(sizes)
        slot[me] = current
        copies = []
        for s in range(1, n):
            copy = pltpu.make_async_remote_copy(
                src_ref=slot.at[me],
                dst_ref=slot.at[me],
                send_sem=send_sem.at[which],
                recv_sem=recv_sem.at[which],
                device_id=coordinates(axes, sizes, lax.rem(me + s, n)),
                device_id_type=MESH,
            )
            copy.start()
            copies.append(copy)
            which += 1
        for copy in copies:
            copy.wait()
        first, second = slot[0, 0], slot[0, 1]
        for s in range(1, n):
            first = first + slot[s, 0]
            second = second + slot[s, 1]
        if kind == "moments":
            mean = first / n
            for s in range(n):
                second = second + count * jnp.square(slot[s, 0] - mean)
            first = mean
            count = count * n
        current = jnp.stack([first, second])
    o_ref[...] = current


def total(sizes):
    n = 1
    for size in sizes:
        n *= size
    return n


def small_sum(pair, axes, kind, count, collective):
    channels = pair[0].shape[0]
    stages = tuple(
        (group, tuple(lax.axis_size(a) for a in group)) for group in (axes[1:], axes[:1])
    )
    shape = (2, channels // 128, 128)
    n_copies = sum(total(sizes) - 1 for _, sizes in stages)
    out = pl.pallas_call(
        functools.partial(small_sum_kernel, stages, kind, float(count)),
        out_shape=jax.ShapeDtypeStruct(shape, F32),
        in_specs=[pl.BlockSpec(memory_space=pltpu.VMEM)],
        out_specs=pl.BlockSpec(memory_space=pltpu.VMEM),
        scratch_shapes=[pltpu.VMEM((total(sizes),) + shape, F32) for _, sizes in stages]
        + [pltpu.SemaphoreType.DMA((n_copies,)), pltpu.SemaphoreType.DMA((n_copies,))],
        compiler_params=pltpu.CompilerParams(collective_id=collective, has_side_effects=True),
        cost_estimate=pl.CostEstimate(flops=0, bytes_accessed=30_000_000, transcendentals=0),
    )(jnp.stack(pair).reshape(shape))
    return out[0].reshape(channels), out[1].reshape(channels)


def gather_kernel(geometry, both_cores, parts, *refs):
    n_z, n_x, n_y = geometry
    many = len(parts)
    arrays = (len(refs) - 3) // 2
    ins, outs = refs[:arrays], refs[arrays : 2 * arrays]
    own_sem, send_sem, recv_sem = refs[2 * arrays :]
    z, x, y, core = (lax.axis_index(a) for a in ALL)
    sizes = {"z": n_z, "x": n_x, "y": n_y, "c": 2}
    here = {"z": z, "x": x, "y": y, "c": core}
    used = ("z", "x", "y", "c") if both_cores else ("z", "x", "y")

    def peer(axis, s):
        return {axis: lax.rem(here[axis] + s, sizes[axis])}

    barrier = pltpu.get_barrier_semaphore()
    peers = 0
    for axis in used:
        for s in range(1, sizes[axis]):
            pl.semaphore_signal(barrier, inc=1, device_id=peer(axis, s), device_id_type=MESH)
            peers += 1
    pl.semaphore_wait(barrier, peers)

    def back(axis, s):
        return lax.rem(here[axis] + sizes[axis] - s, sizes[axis])

    def view(p, place):
        array, lead, dim, rows, _ = parts[p]
        index = (back("z", place[0]) * n_x + back("x", place[1])) * n_y + back("y", place[2])
        if both_cores:
            index = index * 2 + core
        span = pl.ds(pl.multiple_of(index * rows, rows), rows)
        if dim == 0:
            return outs[array].at[span]
        return outs[array].at[pl.ds(*lead), span] if lead else outs[array].at[:, span]

    def given(p):
        array, lead = parts[p][:2]
        return ins[array].at[pl.ds(*lead)] if lead else ins[array]

    started = []

    def send(p, place, axis, s):
        source = given(p) if place == (0, 0, 0) else view(p, place)
        which = len(started)
        copy = pltpu.make_async_remote_copy(
            src_ref=source,
            dst_ref=view(p, place),
            send_sem=send_sem.at[which],
            recv_sem=recv_sem.at[which],
            device_id=peer(axis, s),
            device_id_type=MESH,
        )
        copy.start()
        started.append(copy)
        return copy

    last = []

    def to_core(p, place):
        if both_cores:
            last.append(send(p, place, "c", 1))

    own = []
    along_z = {}
    for s in range(1, n_z):
        for p in range(many):
            along_z[s, p] = send(p, (0, 0, 0), "z", s)
    second, third = {}, {}

    def spread(p, zs):
        first_axis, second_axis = ("x", "y") if parts[p][4] == 1 else ("y", "x")
        for s in range(1, sizes[first_axis]):
            second[p, zs, s] = send(p, (zs, 0, 0), first_axis, s)
        for s in range(1, sizes[second_axis]):
            third[p, zs, 0, s] = send(p, (zs, 0, 0), second_axis, s)
        to_core(p, (zs, 0, 0))

    def place_of(p, zs, a, b):
        return (zs, a, b) if parts[p][4] == 1 else (zs, b, a)

    for p in range(many):
        spread(p, 0)
    for p in range(many):
        copy = pltpu.make_async_copy(given(p), view(p, (0, 0, 0)), own_sem.at[p])
        copy.start()
        own.append(copy)
    for zs in range(1, n_z):
        for p in range(many):
            along_z[zs, p].wait_recv()
            spread(p, zs)
    for zs in range(n_z):
        for p in range(many):
            first_axis, second_axis = ("x", "y") if parts[p][4] == 1 else ("y", "x")
            for a in range(1, sizes[first_axis]):
                second[p, zs, a].wait_recv()
                for s in range(1, sizes[second_axis]):
                    third[p, zs, a, s] = send(p, place_of(p, zs, a, 0), second_axis, s)
                to_core(p, place_of(p, zs, a, 0))
    for zs in range(n_z):
        for p in range(many):
            first_axis, second_axis = ("x", "y") if parts[p][4] == 1 else ("y", "x")
            for b in range(1, sizes[second_axis]):
                for a in range(sizes[first_axis]):
                    third[p, zs, a, b].wait_recv()
                    to_core(p, place_of(p, zs, a, b))
    for copy in last:
        copy.wait_recv()
    for copy in own:
        copy.wait()
    for copy in started:
        copy.wait_send()


def gather_pieces(arrays, parts, both_cores, collective, microseconds):
    geometry = tuple(lax.axis_size(a) for a in CHIPS)
    chips = total(geometry)
    many = len(parts)
    cut_at = {part[0]: part[2] for part in parts}
    shapes = []
    for i, array in enumerate(arrays):
        shape = list(array.shape)
        shape[cut_at[i]] *= chips * (2 if both_cores else 1)
        shapes.append(jax.ShapeDtypeStruct(tuple(shape), array.dtype))
    n_copies = many * (chips - 1 + (chips if both_cores else 0))
    return pl.pallas_call(
        functools.partial(gather_kernel, geometry, both_cores, parts),
        out_shape=shapes,
        in_specs=[pl.BlockSpec(memory_space=pl.ANY)] * len(arrays),
        out_specs=[pl.BlockSpec(memory_space=pl.ANY)] * len(arrays),
        scratch_shapes=[
            pltpu.SemaphoreType.DMA((many,)),
            pltpu.SemaphoreType.DMA((n_copies,)),
            pltpu.SemaphoreType.DMA((n_copies,)),
        ],
        compiler_params=pltpu.CompilerParams(collective_id=collective, has_side_effects=True),
        cost_estimate=pl.CostEstimate(
            flops=0, bytes_accessed=int(3.5e6 * microseconds), transcendentals=0
        ),
    )(*arrays)


def scatter_kernel(sizes, orders, layouts, window, *refs):
    many = len(orders)
    depth = max(len(order) for order in orders)
    ins, outs = refs[:many], refs[many : 2 * many]
    own = refs[2 * many : 3 * many]
    landed = [refs[(3 + i) * many : (4 + i) * many] for i in range(depth)]
    own_sem, send_sem, recv_sem = refs[-3:]
    here = {a: lax.axis_index(a) for a in sizes}

    def forth(axis, s):
        return lax.rem(here[axis] + s, sizes[axis])

    barrier = pltpu.get_barrier_semaphore()
    peers = 0
    for axis in sizes:
        for s in range(1, sizes[axis]):
            pl.semaphore_signal(
                barrier, inc=1, device_id={axis: forth(axis, s)}, device_id_type=MESH
            )
            peers += 1
    pl.semaphore_wait(barrier, peers)

    started = []

    def send(source, target, axis, s):
        which = len(started)
        copy = pltpu.make_async_remote_copy(
            src_ref=source,
            dst_ref=target,
            send_sem=send_sem.at[which],
            recv_sem=recv_sem.at[which],
            device_id={axis: forth(axis, s)},
            device_id_type=MESH,
        )
        copy.start()
        started.append(copy)
        return copy

    places = []
    for order in orders:
        steps = [list(range(1, sizes[a])) + [0] for a in order[1:]]
        places.append(list(itertools.product(*steps)))

    def block(p, steps):
        index = 0
        at = dict(zip(orders[p], steps))
        for axis in layouts[p]:
            index = index * sizes[axis] + forth(axis, at[axis])
        return index

    def slot(p, stage, steps):
        index = 0
        for axis, s in zip(orders[p][stage + 1 :], steps):
            index = index * sizes[axis] + s
        return index

    loads, copies = {}, {}
    for p in range(many):
        for k, place in enumerate(places[p]):
            copy = pltpu.make_async_copy(
                ins[p].at[block(p, (0,) + place)], own[p].at[k], own_sem.at[len(loads)]
            )
            copy.start()
            loads[p, k] = copy

    def send_first(k):
        for p in range(many):
            if k < len(places[p]):
                place = places[p][k]
                for s in range(1, sizes[orders[p][0]]):
                    copies[p, 0, s, place] = send(
                        ins[p].at[block(p, (s,) + place)],
                        landed[0][p].at[s - 1, slot(p, 0, place)],
                        orders[p][0],
                        s,
                    )

    waited = set()
    longest = max(len(each) for each in places)
    for k in range(min(window, longest)):
        send_first(k)
    for k in range(longest):
        for p in range(many):
            own_k = k - (longest - len(places[p]))
            if own_k < 0:
                continue
            order, place = orders[p], places[p][own_k]
            loads[p, own_k].wait()
            terms, onward = [], None
            for stage, axis in enumerate(order):
                later = place[stage:]
                if stage > 0 and place[stage - 1] > 0:
                    onward = (stage, axis, place[stage - 1], later)
                    break
                for s in range(1, sizes[axis]):
                    copies[p, stage, s, later].wait_recv()
                    terms.append((landed[stage][p], (s - 1, slot(p, stage, later))))

            def add(t, carry, p=p, k=own_k, terms=terms, final=onward is None):
                value = own[p][k, t].astype(F32)
                for ref, index in terms:
                    value = value + ref[(*index, t)].astype(F32)
                if final:
                    outs[p][t] = value
                else:
                    own[p][k, t] = value.astype(BF)
                return carry

            lax.fori_loop(0, own[p].shape[1], add, 0)
            if onward:
                stage, axis, s, later = onward
                copies[p, stage, s, later] = send(
                    own[p].at[own_k], landed[stage][p].at[s - 1, slot(p, stage, later)], axis, s
                )
        if k + window < longest:
            for p in range(many):
                if k < len(places[p]):
                    for s in range(1, sizes[orders[p][0]]):
                        copy = copies[p, 0, s, places[p][k]]
                        copy.wait_send()
                        waited.add(id(copy))
            send_first(k + window)
    for copy in started:
        if id(copy) not in waited:
            copy.wait_send()


def scatter_blocks(arrays, orders, layouts, window, collective):
    sizes = {a: lax.axis_size(a) for a in ALL}
    depth = max(len(order) for order in orders)
    own, landed = [], [[] for _ in range(depth)]
    loads = copies = 0
    for array, order in zip(arrays, orders):
        shape = array.shape[1:]
        own.append(pltpu.VMEM((total(sizes[a] for a in order[1:]),) + shape, BF))
        loads += total(sizes[a] for a in order[1:])
        for stage in range(depth):
            if stage < len(order):
                peers, later = sizes[order[stage]] - 1, total(sizes[a] for a in order[stage + 1 :])
                landed[stage].append(pltpu.VMEM((peers, later) + shape, BF))
                copies += peers * later
            else:
                landed[stage].append(pltpu.VMEM((1, 1, 16, 128), BF))
    return pl.pallas_call(
        functools.partial(scatter_kernel, sizes, orders, layouts, window),
        out_shape=[jax.ShapeDtypeStruct(a.shape[1:], F32) for a in arrays],
        in_specs=[pl.BlockSpec(memory_space=pl.ANY)] * len(arrays),
        out_specs=[pl.BlockSpec(memory_space=pltpu.VMEM)] * len(arrays),
        scratch_shapes=own
        + sum(landed, [])
        + [
            pltpu.SemaphoreType.DMA((loads,)),
            pltpu.SemaphoreType.DMA((copies,)),
            pltpu.SemaphoreType.DMA((copies,)),
        ],
        compiler_params=pltpu.CompilerParams(
            collective_id=collective, has_side_effects=True, vmem_limit_bytes=VMEM_BYTES
        ),
        cost_estimate=pl.CostEstimate(flops=0, bytes_accessed=250_000_000, transcendentals=0),
    )(*arrays)


def combine_cols(before, same, after, col, spread):
    n = same.shape[0]
    before = jnp.where(col < spread, 0.0, pltpu.roll(before, spread, 0))
    after = jnp.where(col >= n - spread, 0.0, pltpu.roll(after, n - spread, 0))
    return before + same + after


def conv_fwd(xpad, weights, spread, kc, nc, n_blocks, n_first, moments, out_dtype):
    batch, height_pad, width, depth = xpad.shape
    height, wide = height_pad - 2 * spread, n_blocks * nc
    px = batch * height * width
    steps = depth // kc

    def body(first_ref, x_ref, *rest):
        taps = [ref.at[t] for ref, w in zip(rest, weights) for t in range(w[1])]
        rest = rest[len(weights) :]
        o_ref, acc = rest[0], rest[-1]
        k = pl.program_id(1)

        def dots(first):
            for b in range(3):
                for a in range(3):
                    xa = x_ref[:, a * spread : a * spread + height].reshape(px, kc)
                    d = jnp.dot(xa, taps[3 * a + b][...], preferred_element_type=F32)
                    if first and a == 0:
                        acc[b] = d
                    else:
                        acc[b] += d

        @pl.when(k == 0)
        def _():
            dots(True)

        @pl.when(k > 0)
        def _():
            dots(False)

        @pl.when(k == steps - 1)
        def _():
            col = lax.broadcasted_iota(jnp.int32, (width, nc), 0)

            def store(i, running):
                r = pl.ds(pl.multiple_of(i * width, width), width)
                v = combine_cols(acc[0, r], acc[1, r], acc[2, r], col, spread)
                o_ref[r] = v.astype(out_dtype)
                return running + jnp.sum(v.reshape(width // 8, 8, nc), axis=0) if moments else 0

            start = jnp.zeros((8, nc), F32)
            running = lax.fori_loop(0, batch * height, store, start if moments else 0)
            if moments:
                mean = jnp.sum(running, axis=0, keepdims=True) / px

                def deviation(i, so_far):
                    r = pl.ds(pl.multiple_of(i * width, width), width)
                    v = jnp.square(o_ref[r] - mean)
                    return so_far + jnp.sum(v.reshape(width // 8, 8, nc), axis=0)

                m2 = lax.fori_loop(0, batch * height, deviation, start)
                row = lax.broadcasted_iota(jnp.int32, (8, nc), 0)
                rest[1][...] = jnp.where(row == 0, mean, jnp.sum(m2, axis=0, keepdims=True))

    out_specs = [pl.BlockSpec((px, nc), lambda n, k, f: (0, n))]
    out_shape = [jax.ShapeDtypeStruct((px, wide), out_dtype)]
    if moments:
        out_specs.append(pl.BlockSpec((8, nc), lambda n, k, f: (0, n)))
        out_shape.append(jax.ShapeDtypeStruct((8, wide), F32))
    return pl.pallas_call(
        body,
        grid_spec=pltpu.PrefetchScalarGridSpec(
            num_scalar_prefetch=1,
            grid=(n_blocks, steps),
            in_specs=[
                pl.BlockSpec((batch, height_pad, width, kc), lambda n, k, f: (0, 0, 0, k)),
                *(
                    pl.BlockSpec(
                        (many, kc, nc),
                        lambda n, k, f, lead=lead, pick=pick: (lead, k, n + f[0] if pick else n),
                    )
                    for _, many, lead, pick in weights
                ),
            ],
            out_specs=out_specs,
            scratch_shapes=[pltpu.VMEM((3, px, nc), F32)],
        ),
        out_shape=out_shape,
        compiler_params=pltpu.CompilerParams(vmem_limit_bytes=VMEM_BYTES),
        cost_estimate=pl.CostEstimate(
            flops=18 * px * depth * wide,
            bytes_accessed=18 * depth * wide + 2 * px * depth + 4 * px * wide,
            transcendentals=0,
        ),
    )(n_first, xpad, *(w[0] for w in weights))


def conv_dgrad(gpads, weights, spread, cc, c_range, n_first, out_dtype, by_core=False):
    batch, height_pad, width, wide = gpads[0].shape
    many = len(gpads)
    height, depth = height_pad - 2 * spread, len(c_range) * cc
    c_first = c_range[0]
    px = batch * height * width
    dims = (((1,), (1,)), ((), ()))
    results = 2 if by_core else 1
    lines = height // results

    def body(first_ref, *refs):
        gs, outs, acc = refs[:many], refs[many + len(weights) : -1], refs[-1]
        taps = [
            ref.at[t]
            for ref, w in zip(refs[many : many + len(weights)], weights)
            for t in range(w[1])
        ]
        for q in range(many):
            for b in range(3):
                for a in range(3):
                    top = (2 - a) * spread
                    ga = gs[q][:, top : top + height].reshape(px, wide)
                    d = lax.dot_general(
                        ga, taps[9 * q + 3 * a + b][...], dims, preferred_element_type=F32
                    )
                    if q == 0 and a == 0:
                        acc[2 - b] = d
                    else:
                        acc[2 - b] += d
        col = lax.broadcasted_iota(jnp.int32, (width, cc), 0)

        for which, o_ref in enumerate(outs):

            def store(i, carry, which=which, o_ref=o_ref):
                line = i
                if by_core:
                    part = first_ref[0] if which == 0 else 1 - first_ref[0]
                    line = i // lines * height + part * lines + lax.rem(i, lines)
                r = pl.ds(pl.multiple_of(line * width, width), width)
                value = combine_cols(acc[0, r], acc[1, r], acc[2, r], col, spread)
                o_ref[pl.ds(pl.multiple_of(i * width, width), width)] = value.astype(out_dtype)
                return carry

            lax.fori_loop(0, batch * lines, store, 0)

    return pl.pallas_call(
        body,
        grid_spec=pltpu.PrefetchScalarGridSpec(
            num_scalar_prefetch=1,
            grid=(depth // cc,),
            in_specs=[pl.BlockSpec((batch, height_pad, width, wide), lambda c, f: (0, 0, 0, 0))]
            * many
            + [
                pl.BlockSpec(
                    (taps, cc, wide),
                    lambda c, f, lead=lead, pick=pick: (lead, c + c_first, f[0] if pick else 0),
                )
                for _, taps, lead, pick in weights
            ],
            out_specs=[pl.BlockSpec((px // results, cc), lambda c, f: (0, c))] * results,
            scratch_shapes=[pltpu.VMEM((3, px, cc), F32)],
        ),
        out_shape=[jax.ShapeDtypeStruct((px // results, depth), out_dtype)] * results,
        compiler_params=pltpu.CompilerParams(vmem_limit_bytes=VMEM_BYTES),
        cost_estimate=pl.CostEstimate(
            flops=18 * many * px * depth * wide,
            bytes_accessed=18 * many * depth * wide + 4 * px * depth,
            transcendentals=0,
        ),
    )(n_first, *gpads, *(w[0] for w in weights))


def conv_wgrad(xpad, grad, spread, cc, nc, piece, plane, shares):
    batch, height_pad, width, depth = xpad.shape
    height, wide = height_pad - 2 * spread, grad.shape[1]
    px = batch * height * width
    each, blocks = cc // piece, wide // nc
    lines = 128 // width

    def body(x_ref, g_ref, *rest):
        outs, shifted = rest[:-1], rest[-1]

        @pl.when(pl.program_id(1) == 0)
        def _():
            col = lax.broadcasted_iota(jnp.int32, (width, nc), 0)

            def turn(i, carry):
                r = pl.ds(pl.multiple_of(i * 128, 128), 128)
                block = g_ref[r].astype(F32)
                for b in range(3):
                    moved = []
                    for j in range(lines):
                        v = block[j * width : (j + 1) * width]
                        if b == 0:
                            v = jnp.where(
                                col >= width - spread, 0.0, pltpu.roll(v, width - spread, 0)
                            )
                        elif b == 2:
                            v = jnp.where(col < spread, 0.0, pltpu.roll(v, spread, 0))
                        moved.append(v)
                    shifted[b, :, r] = jnp.concatenate(moved, axis=0).T.astype(BF)
                return carry

            lax.fori_loop(0, px // 128, turn, 0)

        for a in range(3):
            xa = x_ref[:, a * spread : a * spread + height].reshape(px, cc)
            for b in range(3):
                d = jnp.dot(shifted[b], xa, preferred_element_type=F32).T.astype(BF)
                for out, (taps, low, high) in zip(outs, shares):
                    if 3 * a + b in taps:
                        for j in range(each):
                            out[j % plane, j // plane, taps.index(3 * a + b)] = d[
                                j * piece : (j + 1) * piece, low:high
                            ]

    return pl.pallas_call(
        body,
        grid=(blocks, depth // cc),
        in_specs=[
            pl.BlockSpec((batch, height_pad, width, cc), lambda n, c: (0, 0, 0, c)),
            pl.BlockSpec((px, nc), lambda n, c: (0, n)),
        ],
        out_specs=[
            pl.BlockSpec(
                (plane, each // plane, len(taps), piece, high - low), lambda n, c: (0, c, 0, 0, n)
            )
            for taps, low, high in shares
        ],
        out_shape=[
            jax.ShapeDtypeStruct(
                (plane, depth // (plane * piece), len(taps), piece, blocks * (high - low)), BF
            )
            for taps, low, high in shares
        ],
        scratch_shapes=[pltpu.VMEM((3, nc, px), BF)],
        compiler_params=pltpu.CompilerParams(vmem_limit_bytes=VMEM_BYTES),
        cost_estimate=pl.CostEstimate(
            flops=18 * px * depth * wide,
            bytes_accessed=18 * depth * wide + 2 * px * depth,
            transcendentals=0,
        ),
    )(xpad, grad)


def outer_sum(left, right, cc, turned):
    px, wide = left.shape
    deep = right.shape[1]

    def body(l_ref, r_ref, o_ref, flipped):
        @pl.when(pl.program_id(0) == 0)
        def _():
            def turn(i, carry):
                r = pl.ds(pl.multiple_of(i * 128, 128), 128)
                flipped[:, r] = l_ref[r].astype(F32).T.astype(BF)
                return carry

            lax.fori_loop(0, px // 128, turn, 0)

        d = jnp.dot(flipped[...], r_ref[...], preferred_element_type=F32)
        o_ref[...] = (d.T if turned else d).astype(BF)

    return pl.pallas_call(
        body,
        grid=(deep // cc,),
        in_specs=[
            pl.BlockSpec((px, wide), lambda c: (0, 0)),
            pl.BlockSpec((px, cc), lambda c: (0, c)),
        ],
        out_specs=pl.BlockSpec((cc, wide), lambda c: (c, 0))
        if turned
        else pl.BlockSpec((wide, cc), lambda c: (0, c)),
        out_shape=jax.ShapeDtypeStruct((deep, wide) if turned else (wide, deep), BF),
        scratch_shapes=[pltpu.VMEM((wide, px), BF)],
        compiler_params=pltpu.CompilerParams(vmem_limit_bytes=VMEM_BYTES),
        cost_estimate=pl.CostEstimate(
            flops=2 * px * deep * wide,
            bytes_accessed=2 * (deep * wide + px * (deep + wide)),
            transcendentals=0,
        ),
    )(left, right)


def swap(value):
    return lax.ppermute(value, "c", [(0, 1), (1, 0)])


def in_order(mine, other, dim):
    first = lax.axis_index("c") == 0
    return jnp.concatenate(
        [jnp.where(first, mine, other), jnp.where(first, other, mine)], axis=dim
    )


def rims(block, axes, width):
    count = 1
    for a in axes:
        count *= lax.axis_size(a)
    forward = [(i, i + 1) for i in range(count - 1)]
    backward = [(t, s) for s, t in forward]
    low = lax.ppermute(block[:, block.shape[1] - width :], axes, forward)
    high = lax.ppermute(block[:, :width], axes, backward)
    return low, high


def with_rims(block, axes, width):
    low, high = rims(block, axes, width)
    return jnp.concatenate([low, block, high], axis=1)


def local_moments(value):
    mean = jnp.mean(value, axis=(0, 1, 2))
    return mean, jnp.sum(jnp.square(value - mean), axis=(0, 1, 2))


def gelu_back(inner, upstream):
    return jax.vjp(jax.nn.gelu, inner)[1](upstream)[0]


def gather(value, axes, dim):
    return lax.all_gather(value, axes, axis=dim, tiled=True)


def scatter_sum(value, axes, dim):
    return lax.psum_scatter(value, axes, scatter_dimension=dim, tiled=True)


def per_device(
    features,
    w_reduce,
    w_dilated,
    w_expand,
    gain_reduce,
    bias_reduce,
    gain_dilated,
    bias_dilated,
    gain_expand,
    bias_expand,
    w_heads,
    gain_heads,
    bias_heads,
    w_message,
    w_gate,
    w_seg,
    w_depth,
    labels,
    depth_target,
    depth_mask,
):
    core = lax.axis_index("c")
    chips = lax.axis_size("z") * lax.axis_size("x") * lax.axis_size("y")
    devices = chips * 2
    crops, height, width, deep = features.shape
    mid = w_reduce.shape[1]
    classes = w_seg.shape[1]
    local_px = crops * height * width
    pixels = local_px * devices
    chip_px = local_px * 2

    tied = lax.optimization_barrier
    r_rows, d_rows = w_reduce.shape[0], w_dilated.shape[1]
    last_chip = in_order(
        lax.dynamic_slice_in_dim(w_heads[7:], core * mid, mid, axis=2),
        swap(lax.dynamic_slice_in_dim(w_heads[7:], (1 - core) * mid, mid, axis=2)),
        1,
    )
    heads_most = gather(w_heads[:7], ALL, 1)
    sides_own = jnp.stack([w_message[1 - core], w_gate[core]])
    sides_other = jnp.stack([w_message[core], w_gate[1 - core]])
    sides_full = gather(in_order(sides_own, swap(sides_other), 2), CHIPS, 2)
    quarters = deep // mid
    small = jnp.concatenate([w_seg, w_depth[:, None]], axis=1)
    small = jnp.pad(small, ((0, 0), (0, mid - classes - 1)))
    side_blocks = jnp.stack(
        [w_expand[:, q * mid : (q + 1) * mid] for q in range(quarters)] + [small]
    )
    reduce_full, dilated_full, blocks_full = gather_pieces(
        (w_reduce, w_dilated, side_blocks),
        ((0, None, 0, r_rows, 2), (1, None, 1, d_rows, 1), (2, None, 1, d_rows, 2)),
        True,
        8,
        40,
    )
    expand_full = blocks_full[:quarters]
    class_full = blocks_full[quarters, :, :128]
    none = jnp.zeros((1,), jnp.int32)
    own_half = core.astype(jnp.int32).reshape(1)

    first_raw = jnp.einsum("bhwc,co->bhwo", features, reduce_full, preferred_element_type=F32)

    def norm(raw_moments, axes, count, collective):
        mean, m2 = small_sum(raw_moments, axes, "moments", count, collective)
        return mean, lax.rsqrt(m2 / pixels + EPS)

    stats_one = norm(local_moments(first_raw), ALL, local_px, 0)
    scaled_one = (first_raw - stats_one[0]) * stats_one[1]
    inner_one = scaled_one * gain_reduce + bias_reduce
    hidden_one = jax.nn.gelu(inner_one).astype(BF)
    padded_one = with_rims(hidden_one, ROWS, 2)

    dilated_taps = ((dilated_full, 9, 0, False),)
    second_raw, second_moments = conv_fwd(
        padded_one, dilated_taps, 2, 256, mid, 1, none, True, F32
    )
    second_raw = second_raw.reshape(crops, height, width, mid)
    stats_two = norm((second_moments[0], second_moments[1]), ALL, local_px, 1)
    scaled_two = (second_raw - stats_two[0]) * stats_two[1]
    inner_two = scaled_two * gain_dilated + bias_dilated
    hidden_two = jax.nn.gelu(inner_two).astype(BF)
    third_raw = jnp.einsum(
        "bhwc,qco->bhwqo", hidden_two, expand_full, preferred_element_type=F32
    ).reshape(crops, height, width, deep)
    stats_three = norm(local_moments(third_raw), ALL, local_px, 2)
    scaled_three = (third_raw - stats_three[0]) * stats_three[1]
    inner_three = scaled_three * gain_expand + bias_expand + features.astype(F32)
    output = jax.nn.gelu(inner_three).astype(BF)

    low, high = rims(output, ROWS, 1)
    outer = jnp.where(core == 0, low, high)
    outer_other = swap(outer)
    output_other = swap(output)
    output_pad = jnp.concatenate(
        [
            jnp.where(core == 0, low, outer_other),
            in_order(output, output_other, 1),
            jnp.where(core == 0, outer_other, high),
        ],
        axis=1,
    )
    tall = 2 * height
    last_chip, output_pad = tied((last_chip, output_pad))
    last_rows = last_chip.shape[1]
    (heads_last,) = gather_pieces(
        (last_chip,), ((0, (0, 1), 1, last_rows, 1), (0, (1, 1), 1, last_rows, 2)), False, 9, 45
    )
    heads_last, output_pad = tied((heads_last, output_pad))
    heads_taps = ((heads_most, 7, 0, True), (heads_last, 2, 0, False))
    heads_raw, heads_moments = conv_fwd(
        output_pad, heads_taps, 1, 512, mid, 1, own_half, True, F32
    )
    stats_heads = norm((heads_moments[0], heads_moments[1]), CHIPS, chip_px, 3)
    gain_own = lax.dynamic_slice_in_dim(gain_heads, core * mid, mid)
    bias_own = lax.dynamic_slice_in_dim(bias_heads, core * mid, mid)
    scaled_heads = (heads_raw - stats_heads[0]) * stats_heads[1]
    inner_heads = scaled_heads * gain_own + bias_own
    feature = jax.nn.gelu(inner_heads).astype(BF)
    feature_pad = with_rims(feature.reshape(crops, tall, width, mid), ("y",), 1)

    sides_full = sides_full.reshape(18, mid, mid)
    side_taps = ((sides_full, 9, 0, False), (sides_full, 9, 1, False))
    (give,) = conv_fwd(
        feature_pad, side_taps[:1], 1, 256, mid, 1, none, False, BF
    )
    (gate,) = conv_fwd(feature_pad, side_taps[1:], 1, 256, mid, 1, none, False, F32)
    message = swap(give).astype(F32)
    sigma = jax.nn.sigmoid(gate)
    stream = (feature.astype(F32) + sigma * message).astype(BF)
    scores = jnp.dot(stream, class_full, preferred_element_type=F32)
    own_side = jnp.stack(
        [labels.astype(F32), depth_target, depth_mask.astype(F32)]
    )
    labels_chip, target_chip, mask_chip = in_order(own_side, swap(own_side), 2).reshape(3, chip_px)
    seg_scores = scores[:, :classes]
    log_total = jax.nn.logsumexp(seg_scores, axis=-1, keepdims=True)
    class_ids = jnp.arange(classes, dtype=jnp.int32)
    seg_back = jnp.exp(seg_scores - log_total) - (
        labels_chip.astype(jnp.int32)[:, None] == class_ids
    ).astype(F32)
    depth_scores = scores[:, classes]
    differ = depth_scores - target_chip
    depth_back = mask_chip * differ * lax.rsqrt(differ * differ + 1.0)
    score_back = jnp.concatenate(
        [
            jnp.where(core == 1, seg_back, 0.0),
            jnp.where(core == 0, depth_back, 0.0)[:, None],
            jnp.zeros((chip_px, 128 - classes - 1), F32),
        ],
        axis=1,
    ).astype(BF)
    class_grad = lax.dot_general(
        stream, score_back, (((0,), (0,)), ((), ())), preferred_element_type=F32
    )
    stream_grad = lax.dot_general(
        score_back, class_full, (((1,), (1,)), ((), ())), preferred_element_type=F32
    )

    scores_map = scores[:, : classes + 1].reshape(crops, tall, width, classes + 1)
    for_own = lax.dynamic_slice_in_dim(scores_map, core * height, height, axis=1)
    for_other = lax.dynamic_slice_in_dim(scores_map, (1 - core) * height, height, axis=1)
    from_other = swap(for_other)
    depth_pred = jnp.where(core == 0, for_own[..., classes], from_other[..., classes])
    seg_logits = jnp.where(core == 0, from_other[..., :classes], for_own[..., :classes])

    give_grad_other = (stream_grad * sigma).astype(BF)
    gate_grad_low = (stream_grad * message * sigma * (1.0 - sigma)).astype(BF)
    give_grad_low = swap(give_grad_other)
    piece_side = mid // chips
    plane = lax.axis_size("x") * lax.axis_size("y")
    tall_shape = (crops, tall, width, mid)
    side_rims = [rims(g.reshape(tall_shape), ("y",), 1) for g in (give_grad_low, gate_grad_low)]
    every_tap = tuple(range(9))
    (sides_grad,) = conv_wgrad(
        feature_pad,
        jnp.concatenate([give_grad_low, gate_grad_low], axis=1),
        1,
        mid,
        mid,
        piece_side,
        plane,
        ((every_tap, 0, mid),),
    )
    sides_grad, side_rims = tied((sides_grad, side_rims))
    give_pad, gate_pad = (
        jnp.concatenate([low, g.reshape(tall_shape), high], axis=1)
        for g, (low, high) in zip((give_grad_low, gate_grad_low), side_rims)
    )
    sides_grad = scatter_sum(sides_grad.reshape(-1, 2 * mid), PLANE, 0)
    (feature_back,) = conv_dgrad(
        [give_pad, gate_pad],
        side_taps,
        1,
        256,
        range(mid // 256),
        none,
        F32,
    )
    feature_grad = stream_grad + feature_back

    def norm_back(upstream, scaled, inverse, gain, axes, collective, kept=None):
        dims = tuple(range(upstream.ndim - 1))
        bias_grad, gain_grad = small_sum(
            (jnp.sum(upstream, axis=dims), jnp.sum(upstream * scaled, axis=dims)),
            axes,
            "sums",
            1,
            collective,
        )
        upstream = upstream if kept is None else kept
        grad = gain * inverse * (upstream - bias_grad / pixels - scaled * (gain_grad / pixels))
        return grad, gain_grad, bias_grad

    heads_raw_grad, gain_heads_own, bias_heads_own = norm_back(
        gelu_back(inner_heads, feature_grad), scaled_heads, stats_heads[1], gain_own, CHIPS, 4
    )
    heads_pair = jnp.stack([gain_heads_own, bias_heads_own])
    gain_heads_grad, bias_heads_grad = in_order(heads_pair, swap(heads_pair), 1)
    heads_low = heads_raw_grad.astype(BF)
    heads_rims = rims(heads_low.reshape(tall_shape), ("y",), 1)
    most_taps, last_tap = every_tap[:8], every_tap[8:]
    heads_first, heads_yx, heads_xy = conv_wgrad(
        output_pad,
        heads_low,
        1,
        512,
        mid,
        deep // chips,
        plane,
        ((most_taps, 0, mid), (last_tap, 0, mid // 2), (last_tap, mid // 2, mid)),
    )
    heads_first, heads_yx, heads_xy, heads_rims, sides_grad = tied(
        (heads_first, heads_yx, heads_xy, heads_rims, sides_grad)
    )
    n_z, me_z = lax.axis_size("z"), lax.axis_index("z")
    sides_grad = sides_grad.reshape(n_z, 9, piece_side, 2 * mid)
    sides_sent = [
        lax.ppermute(
            lax.dynamic_index_in_dim(sides_grad, lax.rem(me_z + s, n_z), 0, keepdims=False),
            "z",
            [(i, (i + s) % n_z) for i in range(n_z)],
        )
        for s in range(1, n_z)
    ]
    sides_grad = lax.dynamic_index_in_dim(sides_grad, me_z, 0, keepdims=False)
    heads_pad = jnp.concatenate(
        [heads_rims[0], heads_low.reshape(tall_shape), heads_rims[1]], axis=1
    )
    heads_first = scatter_sum(heads_first.reshape(-1, mid), PLANE, 0)
    heads_yx, heads_xy = (v.reshape(chips, *v.shape[2:]) for v in (heads_yx, heads_xy))
    grad_own, grad_other = conv_dgrad(
        [heads_pad], heads_taps, 1, 512, range(deep // 512), own_half, BF, True
    )
    grad_own, grad_other, sides_grad, sides_sent = tied(
        (grad_own, grad_other, sides_grad, sides_sent)
    )
    output_grad = (grad_own.astype(F32) + swap(grad_other).astype(F32)).reshape(
        crops, height, width, deep
    )

    inner_three_grad = gelu_back(inner_three, output_grad)
    kept_grad = tied(inner_three_grad.astype(BF)).astype(F32)
    third_grad, gain_expand_grad, bias_expand_grad = norm_back(
        inner_three_grad, scaled_three, stats_three[1], gain_expand, ALL, 5, kept_grad
    )
    third_low = third_grad.astype(BF)
    expand_grad = outer_sum(hidden_two.reshape(-1, mid), third_low.reshape(-1, deep), 512, False)
    expand_grad = expand_grad.reshape(devices, 1, d_rows, deep)
    class_grad = class_grad.astype(BF).reshape(devices, 1, d_rows, 128)
    hidden_two_grad = jnp.einsum(
        "bhwqo,qco->bhwc",
        third_low.reshape(crops, height, width, quarters, mid),
        expand_full,
        preferred_element_type=F32,
    )
    second_grad, gain_dilated_grad, bias_dilated_grad = norm_back(
        gelu_back(inner_two, hidden_two_grad), scaled_two, stats_two[1], gain_dilated, ALL, 6
    )
    second_low = second_grad.astype(BF)
    second_rims = rims(second_low, ROWS, 2)
    (dilated_grad,) = conv_wgrad(
        padded_one, second_low.reshape(-1, mid), 2, mid, mid, d_rows, 1, ((every_tap, 0, mid),)
    )
    dilated_grad, expand_grad, second_rims = tied((dilated_grad, expand_grad, second_rims))
    second_pad = jnp.concatenate([second_rims[0], second_low, second_rims[1]], axis=1)
    (hidden_one_grad,) = conv_dgrad(
        [second_pad], dilated_taps, 2, 256, range(mid // 256), none, F32
    )
    hidden_one_grad, heads_first = tied((hidden_one_grad, heads_first))
    heads_first = scatter_sum(heads_first, "z", 0)
    hidden_one_grad = hidden_one_grad.reshape(crops, height, width, mid)
    first_grad, gain_reduce_grad, bias_reduce_grad = norm_back(
        gelu_back(inner_one, hidden_one_grad), scaled_one, stats_one[1], gain_reduce, ALL, 7
    )
    first_low = first_grad.astype(BF)
    reduce_grad = outer_sum(first_low.reshape(-1, mid), features.reshape(-1, deep), 512, True)
    reduce_grad = reduce_grad.reshape(devices, 1, r_rows, mid)
    features_grad = kept_grad + jnp.einsum(
        "bhwo,co->bhwc", first_low, reduce_full, preferred_element_type=F32
    )

    dilated_grad = dilated_grad.reshape(devices, 9, d_rows, mid)
    sides_grad = sides_grad.astype(F32)
    for block in sides_sent:
        sides_grad = sides_grad + block.astype(F32)
    sides_grad = sides_grad.reshape(9, piece_side, 2, mid)
    own_rows = piece_side // 2
    sides_mine = lax.dynamic_slice_in_dim(sides_grad, core * own_rows, own_rows, axis=1)
    sides_from = swap(
        lax.dynamic_slice_in_dim(sides_grad, (1 - core) * own_rows, own_rows, axis=1)
    )
    message_grad = jnp.stack(
        [
            jnp.where(core == 0, sides_from[:, :, 0], sides_mine[:, :, 0]),
            jnp.where(core == 0, sides_mine[:, :, 0], sides_from[:, :, 0]),
        ]
    )
    gate_grad = jnp.stack(
        [
            jnp.where(core == 0, sides_mine[:, :, 1], sides_from[:, :, 1]),
            jnp.where(core == 0, sides_from[:, :, 1], sides_mine[:, :, 1]),
        ]
    )
    features_grad, reduce_grad, message_grad, gate_grad = tied(
        (features_grad, reduce_grad, message_grad, gate_grad)
    )
    by_y, by_x = ("y", "x", "z"), ("x", "y", "z")
    heads_yx, heads_xy, dilated_grad, expand_grad, reduce_grad, class_grad = scatter_blocks(
        (heads_yx, heads_xy, dilated_grad, expand_grad, reduce_grad, class_grad),
        (by_y, by_x, ("c", *by_y), ("c", *by_x), ("c", *by_x), ("c", *by_x)),
        (by_x, by_x, ALL, ALL, ALL, ALL),
        4,
        10,
    )
    reduce_grad = reduce_grad[0]
    expand_grad, class_grad = expand_grad[0], class_grad[0]

    heads_first = heads_first.astype(F32).reshape(8, deep // chips, mid)
    heads_grad = jnp.concatenate([heads_first, jnp.concatenate([heads_yx, heads_xy], axis=2)])
    own_rows = w_heads.shape[1]
    heads_grad = in_order(
        lax.dynamic_slice_in_dim(heads_grad, core * own_rows, own_rows, axis=1),
        swap(lax.dynamic_slice_in_dim(heads_grad, (1 - core) * own_rows, own_rows, axis=1)),
        2,
    ).astype(F32)
    return (
        depth_pred,
        seg_logits,
        features_grad,
        reduce_grad,
        dilated_grad,
        expand_grad,
        gain_reduce_grad,
        bias_reduce_grad,
        gain_dilated_grad,
        bias_dilated_grad,
        gain_expand_grad,
        bias_expand_grad,
        heads_grad,
        gain_heads_grad,
        bias_heads_grad,
        message_grad.astype(F32),
        gate_grad.astype(F32),
        class_grad[:, :classes],
        class_grad[:, classes],
    )


def solution(mesh):
    img, row = mesh.shape["img"], mesh.shape["row"]
    side = row // 2
    fine = Mesh(mesh.devices.reshape(img // side, side, side, 2), ALL)
    crops, rows = ("z", "x"), ("y", "c")
    every = ALL
    placed = (
        P(crops, rows, None, None),
        P(every, None),
        P(None, every, None),
        P(every, None),
        P(),
        P(),
        P(),
        P(),
        P(),
        P(),
        P(None, every, None),
        P(),
        P(),
        P(None, None, every, None),
        P(None, None, every, None),
        P(every, None),
        P(every),
        P(crops, rows, None),
        P(crops, rows, None),
        P(crops, rows, None),
    )
    return jax.shard_map(
        per_device,
        mesh=fine,
        in_specs=placed,
        out_specs=(
            P(crops, rows, None),
            P(crops, rows, None, None),
            P(crops, rows, None, None),
            P(every, None),
            P(None, every, None),
            P(every, None),
            P(),
            P(),
            P(),
            P(),
            P(),
            P(),
            P(None, every, None),
            P(),
            P(),
            P(None, None, every, None),
            P(None, None, every, None),
            P(every, None),
            P(every),
        ),
        check_vma=False,
    )
```
